128 devices in a mesh: dp: 16 (over x, z), tensor: 8 (over y, core).
Axes of the slice: x: 4, y: 4, z: 4, core: 2. Of those that a mesh axis runs over, the one named last changes fastest.
Arguments:
- images: bfloat16 [32, 577, 1024], P('dp', None, 'tensor'), may hold values from -6 to 6
- cotangent: bfloat16 [32, 577, 1024], P('dp', None, 'tensor'), may hold values from -6 to 6
- counts: int32 [16], P('dp'), may hold values from 1 to 2, as said below
- attention_gain: bfloat16 [2, 1024], P(None, 'dp'), may hold values from 0.099609375 to 1.8984375
- attention_shift: bfloat16 [2, 1024], P(None, 'dp'), may hold values from -1.5 to 1.5
- query_weight: bfloat16 [2, 1024, 1024], P(None, 'dp', 'tensor'), may hold values from -0.1875 to 0.1875
- query_bias: bfloat16 [2, 16, 64], P(None, 'tensor', 'dp'), may hold values from -1.5 to 1.5
- key_weight: bfloat16 [2, 1024, 1024], P(None, 'dp', 'tensor'), may hold values from -0.1875 to 0.1875
- value_weight: bfloat16 [2, 1024, 1024], P(None, 'dp', 'tensor'), may hold values from -0.1875 to 0.1875
- value_bias: bfloat16 [2, 16, 64], P(None, 'tensor', 'dp'), may hold values from -1.5 to 1.5
- output_weight: bfloat16 [2, 1024, 1024], P(None, 'tensor', 'dp'), may hold values from -0.75 to 0.75
- output_bias: bfloat16 [2, 1024], P(None, 'dp'), may hold values from -1.5 to 1.5
- feedforward_gain: bfloat16 [2, 1024], P(None, 'dp'), may hold values from 0.099609375 to 1.8984375
- feedforward_shift: bfloat16 [2, 1024], P(None, 'dp'), may hold values from -1.5 to 1.5
- upward_weight: bfloat16 [2, 1024, 4096], P(None, 'dp', 'tensor'), may hold values from -0.1875 to 0.1875
- upward_bias: bfloat16 [2, 64, 64], P(None, 'tensor', 'dp'), may hold values from -1.5 to 1.5
- downward_weight: bfloat16 [2, 4096, 1024], P(None, 'tensor', 'dp'), may hold values from -0.09375 to 0.09375
- downward_bias: bfloat16 [2, 1024], P(None, 'dp'), may hold values from -1.5 to 1.5
Outputs:
- activations: bfloat16 [32, 577, 1024], P('dp', None, 'tensor')
- input_gradient: float32 [32, 577, 1024], P('dp', None, 'tensor')
- attention_gain_gradient: float32 [2, 1024], P(None, 'dp')
- attention_shift_gradient: float32 [2, 1024], P(None, 'dp')
- query_weight_gradient: float32 [2, 1024, 1024], P(None, 'dp', 'tensor')
- query_bias_gradient: float32 [2, 16, 64], P(None, 'tensor', 'dp')
- key_weight_gradient: float32 [2, 1024, 1024], P(None, 'dp', 'tensor')
- value_weight_gradient: float32 [2, 1024, 1024], P(None, 'dp', 'tensor')
- value_bias_gradient: float32 [2, 16, 64], P(None, 'tensor', 'dp')
- output_weight_gradient: float32 [2, 1024, 1024], P(None, 'tensor', 'dp')
- output_bias_gradient: float32 [2, 1024], P(None, 'dp')
- feedforward_gain_gradient: float32 [2, 1024], P(None, 'dp')
- feedforward_shift_gradient: float32 [2, 1024], P(None, 'dp')
- upward_weight_gradient: float32 [2, 1024, 4096], P(None, 'dp', 'tensor')
- upward_bias_gradient: float32 [2, 64, 64], P(None, 'tensor', 'dp')
- downward_weight_gradient: float32 [2, 4096, 1024], P(None, 'tensor', 'dp')
- downward_bias_gradient: float32 [2, 1024], P(None, 'dp')
The draws below stay inside these ranges and needn't reach their ends.
Inputs may be any that keep to these rules, and one draw needn't show every extreme that they name: counts[g] slots of data group g hold an image, slots 0 to counts[g] - 1; in every draw one group holds 2 and one holds 1.
All inputs are finite; a program needn't handle non-finite values.
Results may differ from the reference program's by a relative error of at most 0.029.
Values may be sent and summed in bfloat16 or wider, within the bound.
A program may use at most 192 MiB of HBM per device.

```python
import math
import jax
import jax.numpy as jnp
from jax import lax

D = 1024
HEADS = 16
HD = 64
FF = 4096
SEQ = 577
LAYERS = 2
SLOTS = 2
IMAGES = 32
N_DP = 16


def draw_counts(key, part):
    key = jax.random.fold_in(key, 11)
    first_key, second_key = jax.random.split(key)
    drawn_counts = jax.random.randint(first_key, (N_DP,), 1, SLOTS + 1, dtype=jnp.int32)
    shuffled = jax.random.permutation(second_key, N_DP)
    drawn_counts = drawn_counts.at[shuffled[0]].set(SLOTS)
    return drawn_counts.at[shuffled[1]].set(1)


def shard_levels(stream_key, shape, shards, low, high):
    loudness, own = 1.0, jax.random.fold_in(stream_key, 6)
    for dim, blocks in shards:
        heights = jnp.exp(jax.random.uniform(jax.random.fold_in(own, dim), (blocks,), jnp.float32, low / len(shards), high / len(shards)))
        loudness = loudness * jnp.repeat(heights, shape[dim] // blocks).reshape([-1 if axis == dim else 1 for axis in range(len(shape))])
    return loudness


def normal_values(stream_key, dims, scale, limit, shards=(), kind=jnp.bfloat16):
    values = jax.random.normal(stream_key, dims, jnp.float32) * scale
    if len(shards) > 0:
        values = shard_levels(stream_key, dims, shards, -0.22, 0.18) * values
    return jnp.clip(values, min=-limit, max=limit).astype(kind)


def setup_inputs(seed: int = 0) -> dict:
    arg_keys = jax.random.split(jax.random.key(seed), 19)
    return {
        "images": normal_values(arg_keys[0], (IMAGES, SEQ, D), 1.0, 6.0, ((0, 16), (2, 8))),
        "cotangent": normal_values(arg_keys[1], (IMAGES, SEQ, D), 1.0, 6.0, ((0, 16), (2, 8))),
        "counts": draw_counts(jax.random.fold_in(arg_keys[18], 71), 0),
        "attention_gain": jnp.clip(1.0 + 0.18 * jax.random.normal(arg_keys[3], (LAYERS, D), jnp.float32), 0.099609375, 1.8984375).astype(jnp.bfloat16),
        "attention_shift": normal_values(arg_keys[4], (LAYERS, D), 0.3, 1.5, ((1, 16),)),
        "query_weight": normal_values(arg_keys[5], (LAYERS, D, D), D ** -0.5, 0.1875, ((1, 16), (2, 8))),
        "query_bias": normal_values(arg_keys[6], (LAYERS, HEADS, HD), 0.3, 1.5, ((1, 8), (2, 16))),
        "key_weight": normal_values(arg_keys[7], (LAYERS, D, D), D ** -0.5, 0.1875, ((1, 16), (2, 8))),
        "value_weight": normal_values(arg_keys[8], (LAYERS, D, D), D ** -0.5, 0.1875, ((1, 16), (2, 8))),
        "value_bias": normal_values(arg_keys[9], (LAYERS, HEADS, HD), 0.3, 1.5, ((1, 8), (2, 16))),
        "output_weight": normal_values(arg_keys[10], (LAYERS, D, D), (D // 16) ** -0.5, 0.75, ((1, 8), (2, 16))),
        "output_bias": normal_values(arg_keys[11], (LAYERS, D), 0.3, 1.5, ((1, 16),)),
        "feedforward_gain": jnp.clip(1.0 + 0.18 * jax.random.normal(arg_keys[12], (LAYERS, D), jnp.float32), 0.099609375, 1.8984375).astype(jnp.bfloat16),
        "feedforward_shift": normal_values(arg_keys[13], (LAYERS, D), 0.3, 1.5, ((1, 16),)),
        "upward_weight": normal_values(arg_keys[14], (LAYERS, D, FF), D ** -0.5, 0.1875, ((1, 16), (2, 8))),
        "upward_bias": normal_values(arg_keys[15], (LAYERS, FF // HD, HD), 0.3, 1.5, ((1, 8), (2, 16))),
        "downward_weight": normal_values(arg_keys[16], (LAYERS, FF, D), FF ** -0.5, 0.09375, ((1, 8), (2, 16))),
        "downward_bias": normal_values(arg_keys[17], (LAYERS, D), 0.3, 1.5, ((1, 16),)),
    }


@jax.custom_vjp
def low(v):
    return lax.optimization_barrier(v.astype(jnp.bfloat16)).astype(jnp.float32)

@jax.custom_vjp
def low_back(v):
    return v

def low_keep(v):
    return (low(v), None)

def low_pass(kept, grad):
    return (grad,)

def back_keep(v):
    return (v, None)

def back_low(kept, grad):
    return (low(grad),)
low.defvjp(low_keep, low_pass)
low_back.defvjp(back_keep, back_low)
EPSILON = 1e-06

def product(left, right):
    return jnp.dot(left, right, precision=lax.Precision.HIGHEST)

def normalize(stream, gain_row, shift_row):
    average = lax.optimization_barrier(jnp.mean(stream, axis=-1, keepdims=True))
    centered = stream - average
    variance = lax.optimization_barrier(jnp.mean(centered * centered, axis=-1, keepdims=True))
    return centered * lax.rsqrt(variance + EPSILON) * gain_row + shift_row

def one_layer(stream, params):
    attention_gain, attention_shift, query_weight, query_bias, key_weight, value_weight, value_bias, output_weight, output_bias, feedforward_gain, feedforward_shift, upward_weight, upward_bias, downward_weight, downward_bias = params
    scale_factor = 1.0 / math.sqrt(HD)
    normed = low(normalize(stream, attention_gain, attention_shift))
    query_rows = low_back(low(product(normed, query_weight) + query_bias.reshape(-1)))
    key_rows = low_back(low(product(normed, key_weight)))
    value_rows = low_back(low(product(normed, value_weight) + value_bias.reshape(-1)))
    split_query = query_rows.reshape(SEQ, HEADS, HD)
    split_key = key_rows.reshape(SEQ, HEADS, HD)
    split_value = value_rows.reshape(SEQ, HEADS, HD)
    scores = low_back(jnp.einsum('qhd,khd->hqk', split_query, split_key, precision=lax.Precision.HIGHEST) * scale_factor)
    highest = lax.optimization_barrier(jnp.max(scores, axis=-1, keepdims=True))
    expo_scores = jnp.exp(scores - highest)
    attention = expo_scores / lax.optimization_barrier(jnp.sum(expo_scores, axis=-1, keepdims=True))
    mixed = jnp.einsum('hqk,khd->qhd', low(attention), split_value, precision=lax.Precision.HIGHEST)
    mixed = low_back(low(mixed.reshape(SEQ, D)))
    stream = stream + low_back(product(mixed, output_weight) + output_bias)
    normed_second = low(normalize(stream, feedforward_gain, feedforward_shift))
    hidden = low_back(product(normed_second, upward_weight) + upward_bias.reshape(-1))
    activated = low(jax.nn.gelu(hidden, approximate=False))
    return stream + low_back(product(activated, downward_weight) + downward_bias)

def reference(images, cotangent, counts, attention_gain, attention_shift, query_weight, query_bias, key_weight, value_weight, value_bias, output_weight, output_bias, feedforward_gain, feedforward_shift, upward_weight, upward_bias, downward_weight, downward_bias):
    params = tuple((w.astype(jnp.float32) for w in (attention_gain, attention_shift, query_weight, query_bias, key_weight, value_weight, value_bias, output_weight, output_bias, feedforward_gain, feedforward_shift, upward_weight, upward_bias, downward_weight, downward_bias)))
    slot_ids = jnp.arange(N_DP * SLOTS, dtype=jnp.int32)
    alive = (slot_ids % SLOTS < counts[slot_ids // SLOTS]).astype(jnp.float32)

    def forward(stream, weights):
        for layer_index in range(LAYERS):
            stream = one_layer(stream, tuple((w[layer_index] for w in weights)))
        return stream

    def step(totals, inputs):
        image_rows, direction, alive_flag = inputs
        result, pullback = jax.vjp(forward, image_rows.astype(jnp.float32), params)
        input_grad, weight_grads = pullback(direction.astype(jnp.float32) * alive_flag)
        totals = tuple((left + right for left, right in zip(totals, weight_grads)))
        return (totals, ((result * alive_flag).astype(jnp.bfloat16), input_grad))
    starting = tuple((jnp.zeros(w.shape, jnp.float32) for w in params))
    totals, (activations, input_gradient) = lax.scan(step, starting, (images, cotangent, alive))
    return (activations, input_gradient, totals[0], totals[1], totals[2], totals[3], totals[4], totals[5], totals[6], totals[7], totals[8], totals[9], totals[10], totals[11], totals[12], totals[13], totals[14])
```

```python
import functools
import math

import jax
import jax.numpy as jnp
from jax import lax
from jax.experimental import pallas as pl
from jax.experimental.pallas import tpu as pltpu
from jax.sharding import PartitionSpec as P

HD = 64
EPSILON = 1e-06
SCALE = 1.0 / math.sqrt(HD)
BF = jnp.bfloat16
F32 = jnp.float32

SEQ = 577
D = 1024
ROWS = 592
KEYS = 640
WIDE = 1664
CHUNKS = ((0, 128), (128, 128), (256, 128), (384, 128), (512, 80))
NQ = len(CHUNKS)

TN = (((1,), (1,)), ((), ()))
NT = (((0,), (0,)), ((), ()))


def dot(a, b, dims=(((1,), (0,)), ((), ()))):
    return lax.dot_general(a, b, dims, preferred_element_type=F32)


def block(k, width=256):
    return pl.ds(pl.multiple_of(k * width, width), width)


def greet(devices):
    barrier = pltpu.get_barrier_semaphore()
    for device in devices:
        pl.semaphore_signal(barrier, inc=1, device_id=device, device_id_type=pl.DeviceIdType.MESH)
    return lambda: pl.semaphore_wait(barrier, len(devices))


class Ring:
    def __init__(self, send, near, far, full, send_sem, recv_sem):
        t = lax.axis_index("tensor")
        y = t // 2
        self.y = y
        self.yl, self.yr, self.yo = lax.rem(y + 3, 4), lax.rem(y + 1, 4), lax.rem(y + 2, 4)
        self.left = {"tensor": lax.rem(t + 6, 8)}
        self.right = {"tensor": lax.rem(t + 2, 8)}
        self.send, self.near, self.far, self.full = send, near, far, full
        self.send_sem, self.recv_sem = send_sem, recv_sem
        self.flying = {}

    def go(self, stage, q, to_left, to_right):
        copies = []
        for side, (src, dst) in enumerate((to_left, to_right)):
            copy = pltpu.make_async_remote_copy(
                src_ref=src,
                dst_ref=dst,
                send_sem=self.send_sem.at[stage, q, side],
                recv_sem=self.recv_sem.at[stage, q, side],
                device_id=self.left if side == 0 else self.right,
                device_id_type=pl.DeviceIdType.MESH,
            )
            copy.start()
            copies.append(copy)
        self.flying[stage, q] = copies

    def arrive(self, stage, q):
        for copy in self.flying[stage, q]:
            copy.wait_recv()

    def parts(self, q):
        r0, nr = CHUNKS[q]
        top = 64 if nr == 128 else 48
        return pl.ds(r0, nr), pl.ds(r0, top), pl.ds(r0 + top, nr - top)

    def stage0(self, q):
        rows, a, b = self.parts(q)
        c = block(self.yo)
        self.go(0, q, (self.send.at[a, c], self.near.at[0, a, :]), (self.send.at[b, c], self.near.at[1, b, :]))

    def stage1(self, q):
        rows, a, b = self.parts(q)
        self.arrive(0, q)
        cl, cr = block(self.yl), block(self.yr)
        self.send[a, cl] = (self.send[a, cl].astype(F32) + self.near[0, a, :].astype(F32)).astype(BF)
        self.send[b, cr] = (self.send[b, cr].astype(F32) + self.near[1, b, :].astype(F32)).astype(BF)
        self.go(
            1, q, (self.send.at[rows, cl], self.far.at[0, rows, :]), (self.send.at[rows, cr], self.far.at[1, rows, :])
        )

    def stage2(self, q):
        rows, a, b = self.parts(q)
        self.arrive(1, q)
        c = block(self.y)
        total = self.send[rows, c].astype(F32) + self.far[0, rows, :].astype(F32) + self.far[1, rows, :].astype(F32)
        self.full[rows, c] = total.astype(BF)
        self.go(2, q, (self.full.at[rows, c], self.full.at[rows, c]), (self.full.at[rows, c], self.full.at[rows, c]))

    def stage3(self, q):
        rows, a, b = self.parts(q)
        self.arrive(2, q)
        cl, cr = block(self.yl), block(self.yr)
        self.go(3, q, (self.full.at[a, cr], self.full.at[a, cr]), (self.full.at[b, cl], self.full.at[b, cl]))

    def stage4(self, q):
        self.arrive(3, q)

    def drain(self):
        for copies in self.flying.values():
            for copy in copies:
                copy.wait_send()


def ring_scratch():
    return [
        pltpu.VMEM((ROWS, D), BF),
        pltpu.VMEM((2, ROWS, 256), BF),
        pltpu.VMEM((2, ROWS, 256), BF),
        pltpu.VMEM((ROWS, D), BF),
        pltpu.SemaphoreType.DMA((4, NQ, 2)),
        pltpu.SemaphoreType.DMA((4, NQ, 2)),
    ]


def standardize(x):
    average = jnp.mean(x, axis=1, keepdims=True)
    centered = x - average
    variance = jnp.mean(centered * centered, axis=1, keepdims=True)
    rstd = lax.rsqrt(variance + EPSILON)
    return centered * rstd, rstd


def half_masks():
    lane = lax.broadcasted_iota(jnp.int32, (1, 128), 1)
    first = (lane < 64).astype(F32)
    return first.astype(BF), (1.0 - first).astype(BF)


def key_rows():
    return lax.broadcasted_iota(jnp.int32, (KEYS, 128), 0) < SEQ


def flip(rows):
    return jnp.transpose(rows.astype(F32), (1, 0))


def pair(first, second):
    top = lax.broadcasted_iota(jnp.int32, first.shape, 0) < 64
    return jnp.where(top, first, second)


def fetch(w_ref, targets, sem):
    copies = []
    for k, target in enumerate(targets):
        copy = pltpu.make_async_copy(w_ref.at[:, :, pl.ds(512 * k, 512)], target, sem.at[k])
        copy.start()
        copies.append(copy)
    return copies


def forward_kernel(
    x_ref, w_ref, vec_ref,
    n1_ref, qkv_ref, lse_ref, o_ref, mid_ref, n2_ref, slope_ref, a_ref, out_ref,
    vt_ref, wa_ref, wu_ref, wd_ref, local_sem, *scratch,
):
    attention_in, up_in, down_in = fetch(w_ref, (wa_ref, wu_ref, wd_ref), local_sem)
    one, two = Ring(*scratch[:6]), Ring(*scratch[6:12])
    entered = greet((one.left, one.right))
    masks = half_masks()
    gain, shift = vec_ref[0:1, :], vec_ref[1:2, :]
    qkv_ref[:, ROWS:KEYS, :] = jnp.zeros((2, KEYS - ROWS, 384), BF)
    for r0, nr in CHUNKS:
        rows = pl.ds(r0, nr)
        xhat, _ = standardize(x_ref[rows, :])
        n1_ref[rows, :] = (xhat * gain + shift).astype(BF)
    attention_in.wait()
    for c in range(2):
        out = dot(n1_ref[...], wa_ref[c, :, 0:384])
        qkv_ref[c, 0:ROWS, 0:128] = (out[:, 0:128] + vec_ref[6:7, c * 128 : c * 128 + 128]).astype(BF)
        qkv_ref[c, 0:ROWS, 128:256] = out[:, 128:256].astype(BF)
        qkv_ref[c, 0:ROWS, 256:384] = (out[:, 256:384] + vec_ref[6:7, 256 + c * 128 : 384 + c * 128]).astype(BF)
        vt_ref[c] = flip(qkv_ref[c, :, 256:384]).astype(BF)
    entered()
    up_in.wait()
    down_in.wait()
    valid = key_rows()

    def attend(q):
        r0, nr = CHUNKS[q]
        total = None
        for c in range(2):
            queries, keys = qkv_ref[c, r0 : r0 + 128, 0:128], qkv_ref[c, :, 128:256]
            halves = []
            for h in range(2):
                s = dot(keys, queries * masks[h], TN) * SCALE
                s = jnp.where(valid, s, -1e30)
                top = jnp.max(s, axis=0, keepdims=True)
                e = jnp.exp(s - top)
                norm = jnp.sum(e, axis=0, keepdims=True)
                lse_ref[2 * c + h : 2 * c + h + 1, r0 : r0 + 128] = top + jnp.log(norm)
                p = (e * (1.0 / norm)).astype(BF)
                halves.append(dot(vt_ref[c], p))
            mixed = flip(pair(*halves))[0:nr].astype(BF)
            o_ref[c, r0 : r0 + nr, :] = mixed
            part = dot(mixed, wa_ref[c, :, 384:512], TN)
            total = part if total is None else total + part
        one.send[r0 : r0 + nr, :] = total.astype(BF)
        one.stage0(q)

    def feed(q):
        r0, nr = CHUNKS[q]
        rows = pl.ds(r0, nr)
        one.stage4(q)
        mid = x_ref[rows, :] + one.full[rows, :].astype(F32) + vec_ref[2:3, :]
        mid_ref[rows, :] = mid
        xhat, _ = standardize(mid)
        n2 = (xhat * vec_ref[3:4, :] + vec_ref[4:5, :]).astype(BF)
        n2_ref[rows, :] = n2
        total = None
        for c in range(2):
            u = dot(n2, wu_ref[c]) + vec_ref[7:8, c * 512 : c * 512 + 512]
            phi = 0.5 * (1.0 + lax.erf(u * (1.0 / math.sqrt(2.0))))
            slope_ref[c, rows, :] = phi + u * (jnp.exp(-0.5 * u * u) * (1.0 / math.sqrt(2.0 * math.pi)))
            a = (u * phi).astype(BF)
            a_ref[c, rows, :] = a
            part = dot(a, wd_ref[c], TN)
            total = part if total is None else total + part
        two.send[rows, :] = total.astype(BF)
        two.stage0(q)

    def finish(q):
        r0, nr = CHUNKS[q]
        rows = pl.ds(r0, nr)
        two.stage4(q)
        out_ref[rows, :] = mid_ref[rows, :] + two.full[rows, :].astype(F32) + vec_ref[5:6, :]

    stages = (attend, one.stage1, one.stage2, one.stage3, feed, two.stage1, two.stage2, two.stage3, finish)
    pipeline(stages)
    one.drain()
    two.drain()


def pipeline(stages, fillers=()):
    fillers = dict(fillers)
    for step in range(NQ + len(stages) - 1):
        for k, stage in enumerate(stages):
            if 0 <= step - k < NQ:
                stage(step - k)
            if k == 0:
                for filler in fillers.get(step, ()):
                    filler()


def backward_kernel(
    g_ref, x_ref, mid_ref, n1_ref, n2_ref, qkv_ref, lse_ref, o_ref, slope_ref, a_ref, w_ref, vec_ref,
    gin_ref, da_ref, du_ref, dd_ref, vg_ref,
    gm_ref, go_ref, hid_ref, dout_ref, kt_ref, dqkv_ref, dk_ref, dv_ref, gmid_ref, wa_ref, wu_ref, wd_ref, local_sem, *scratch,
):
    copies = fetch(w_ref, (wa_ref, wu_ref, wd_ref), local_sem)
    one, two = Ring(*scratch[:6]), Ring(*scratch[6:12])
    entered = greet((one.left, one.right))
    masks = half_masks()
    valid = key_rows()
    vg_ref[...] = jnp.zeros((8, D), F32)
    dout_ref[:, ROWS:KEYS, :] = jnp.zeros((2, KEYS - ROWS, 128), BF)
    dk_ref[...] = jnp.zeros(dk_ref.shape, F32)
    dv_ref[...] = jnp.zeros(dv_ref.shape, F32)
    for c in range(2):
        kt_ref[c] = flip(qkv_ref[c, :, 128:256]).astype(BF)
    for r0, nr in CHUNKS:
        gm_ref[r0 : r0 + nr, :] = g_ref[r0 : r0 + nr, :].astype(BF)
    entered()
    for copy in copies:
        copy.wait()

    def add_vector(row, value, lane=0):
        width = value.shape[1]
        vg_ref[row : row + 1, lane : lane + width] = vg_ref[row : row + 1, lane : lane + width] + value

    def column_sum(value):
        return jnp.sum(value.astype(F32), axis=0, keepdims=True)

    def hidden(q):
        r0, nr = CHUNKS[q]
        rows = pl.ds(r0, nr)
        gm = gm_ref[rows, :]
        add_vector(5, column_sum(gm))
        total = None
        for c in range(2):
            da = dot(gm, wd_ref[c])
            du = (da * slope_ref[c, rows, :]).astype(BF)
            hid_ref[c, rows, :] = du
            add_vector(7, column_sum(du), c * 512)
            part = dot(du, wu_ref[c], TN)
            total = part if total is None else total + part
        one.send[rows, :] = total.astype(BF)
        one.stage0(q)

    def norm_back(ring, q, stream, grad, gain_row, shift_row):
        r0, nr = CHUNKS[q]
        rows = pl.ds(r0, nr)
        ring.stage4(q)
        dn = ring.full[rows, :].astype(F32)
        xhat, rstd = standardize(stream[rows, :])
        add_vector(gain_row, column_sum(dn * xhat))
        add_vector(shift_row, column_sum(dn))
        e = dn * vec_ref[gain_row : gain_row + 1, :]
        first = jnp.mean(e, axis=1, keepdims=True)
        second = jnp.mean(e * xhat, axis=1, keepdims=True)
        return grad[rows, :] + rstd * (e - first - xhat * second)

    def attend(q):
        r0, nr = CHUNKS[q]
        rows = pl.ds(r0, nr)
        mid_grad = norm_back(one, q, mid_ref, g_ref, 3, 4)
        gmid_ref[rows, :] = mid_grad
        go = mid_grad.astype(BF)
        go_ref[rows, :] = go
        add_vector(2, column_sum(go))
        for c in range(2):
            dout_ref[c, rows, :] = dot(go, wa_ref[c, :, 384:512]).astype(BF)
            queries = qkv_ref[c, r0 : r0 + 128, 0:128]
            keys, values = qkv_ref[c, :, 128:256], qkv_ref[c, :, 256:384]
            dout = dout_ref[c, r0 : r0 + 128, :]
            halves = []
            for h in range(2):
                qh, doh = queries * masks[h], dout * masks[h]
                s = dot(keys, qh, TN) * SCALE
                p = jnp.where(valid, jnp.exp(s - lse_ref[2 * c + h : 2 * c + h + 1, r0 : r0 + 128]), 0.0)
                dp = dot(values, doh, TN)
                delta = jnp.sum(dp * p, axis=0, keepdims=True)
                ds = (p * (dp - delta)).astype(BF)
                dv_ref[c] = dv_ref[c] + dot(p.astype(BF), doh)
                dk_ref[c] = dk_ref[c] + dot(ds, qh)
                halves.append(dot(kt_ref[c], ds))
            dq = (flip(pair(*halves)) * SCALE)[0:nr].astype(BF)
            dqkv_ref[c, rows, 0:128] = dq

    def down_grad(c):
        def run():
            dd_ref[c] = dot(gm_ref[...], a_ref[c], NT).astype(BF)

        return run

    def up_grad(c):
        def run():
            du_ref[c] = dot(n2_ref[...], hid_ref[c], NT).astype(BF)

        return run

    def out_grad():
        for c in range(2):
            da_ref[c, :, 384:512] = dot(go_ref[...], o_ref[c], NT).astype(BF)

    def qkv_grad(c):
        def run():
            da_ref[c, :, 0:384] = dot(n1_ref[...], dqkv_ref[c], NT).astype(BF)

        return run

    pipeline(
        (hidden, one.stage1, one.stage2, one.stage3, attend),
        {1: (down_grad(0),), 2: (down_grad(1),), 5: (up_grad(0),), 6: (up_grad(1),)}.items(),
    )
    for c in range(2):
        dqkv_ref[c, :, 128:256] = (dk_ref[c, 0:ROWS] * SCALE).astype(BF)
        dqkv_ref[c, :, 256:384] = dv_ref[c, 0:ROWS].astype(BF)

    def project(q):
        r0, nr = CHUNKS[q]
        rows = pl.ds(r0, nr)
        total = None
        for c in range(2):
            grads = dqkv_ref[c, rows, :]
            add_vector(6, column_sum(grads[:, 0:128]), c * 128)
            add_vector(6, column_sum(grads[:, 256:384]), 256 + c * 128)
            part = dot(grads, wa_ref[c, :, 0:384], TN)
            total = part if total is None else total + part
        two.send[rows, :] = total.astype(BF)
        two.stage0(q)

    def finish(q):
        r0, nr = CHUNKS[q]
        gin_ref[r0 : r0 + nr, :] = norm_back(two, q, x_ref, gmid_ref, 0, 1)

    pipeline(
        (project, two.stage1, two.stage2, two.stage3, finish),
        {1: (out_grad,), 2: (qkv_grad(0),), 3: (qkv_grad(1),)}.items(),
    )
    one.drain()
    two.drain()


def torus():
    d, t = lax.axis_index("dp"), lax.axis_index("tensor")
    x, z = d // 4, lax.rem(d, 4)
    return d, t, x, z, lax.rem(t, 2)


def dp_device(x, z):
    return {"dp": lax.rem(x + 4, 4) * 4 + lax.rem(z + 4, 4)}


class Exchange:
    def __init__(self, send_sem, recv_sem):
        self.send_sem, self.recv_sem, self.count, self.started = send_sem, recv_sem, 0, []

    def go(self, src, dst, device):
        copy = pltpu.make_async_remote_copy(
            src_ref=src,
            dst_ref=dst,
            send_sem=self.send_sem.at[self.count],
            recv_sem=self.recv_sem.at[self.count],
            device_id=device,
            device_id_type=pl.DeviceIdType.MESH,
        )
        copy.start()
        self.count += 1
        self.started.append(copy)
        return copy

    def drain(self):
        for copy in self.started:
            copy.wait_send()


def sides(half, x, z):
    if half == 0:
        a, b = x, z
        near = (dp_device(x + 3, z), dp_device(x + 1, z)), (dp_device(x, z + 3), dp_device(x, z + 1))
    else:
        a, b = z, x
        near = (dp_device(x, z + 3), dp_device(x, z + 1)), (dp_device(x + 3, z), dp_device(x + 1, z))
    return a, b, near[0], near[1]


def place(half, a, b):
    return (a, b) if half == 0 else (b, a)


def around(k):
    return lax.rem(k + 3, 4), lax.rem(k + 1, 4), lax.rem(k + 2, 4)


ALL = pl.ds(0, 4)


def gather_kernel(p_ref, img_ref, g_ref, xg_ref, local_sem, send_sem, recv_sem):
    d, t, x, z, c = torus()
    partner = {"tensor": t + 1 - 2 * c}
    others = [{"tensor": lax.rem(t + j, 8)} for j in range(1, 8)]
    entered = greet(
        [dp_device(x + 3, z), dp_device(x + 1, z), dp_device(x, z + 3), dp_device(x, z + 1)] + others
    )
    own = pltpu.make_async_copy(p_ref, g_ref.at[c, x, z], local_sem.at[0])
    own.start()
    image = pltpu.make_async_copy(img_ref.at[c], xg_ref.at[t], local_sem.at[1])
    image.start()
    entered()
    ex = Exchange(send_sem, recv_sem)
    state = []
    for h in range(2):
        a, b, near_a, near_b = sides(h, x, z)
        both = pl.ds(2 * h, 2)
        src, dst = p_ref.at[both], g_ref.at[(c, *place(h, a, b), both)]
        state.append([ex.go(src, dst, near_a[0]), ex.go(src, dst, near_a[1])])
    images = []
    for j in range(1, 8):
        target = lax.rem(t + j, 8)
        images.append(ex.go(img_ref.at[lax.rem(target, 2)], xg_ref.at[t], others[j - 1]))
    own.wait()
    for h in range(2):
        a, b, near_a, near_b = sides(h, x, z)
        lo, hi, far = around(a)
        from_hi, from_lo = state[h]
        from_lo.wait_recv()
        src = g_ref.at[(c, *place(h, lo, b), 2 * h)]
        up = ex.go(src, src, near_a[1])
        from_hi.wait_recv()
        src = g_ref.at[(c, *place(h, hi, b), 2 * h + 1)]
        down = ex.go(src, src, near_a[0])
        state[h] = [down, up]
    hand = []
    for h in range(2):
        a, b, near_a, near_b = sides(h, x, z)
        both = pl.ds(2 * h, 2)
        for copy in state[h]:
            copy.wait_recv()
        src = g_ref.at[(c, *place(h, ALL, b), both)]
        state[h] = [ex.go(src, src, near_b[0]), ex.go(src, src, near_b[1])]
        hand.append(ex.go(src, src, partner))
    for h in range(2):
        a, b, near_a, near_b = sides(h, x, z)
        both = pl.ds(2 * h, 2)
        lo, hi, far = around(b)
        from_hi, from_lo = state[h]
        from_lo.wait_recv()
        src = g_ref.at[(c, *place(h, ALL, lo), 2 * h)]
        up = ex.go(src, src, near_b[1])
        src = g_ref.at[(c, *place(h, ALL, lo), both)]
        hand.append(ex.go(src, src, partner))
        from_hi.wait_recv()
        src = g_ref.at[(c, *place(h, ALL, hi), 2 * h + 1)]
        down = ex.go(src, src, near_b[0])
        src = g_ref.at[(c, *place(h, ALL, hi), both)]
        hand.append(ex.go(src, src, partner))
        state[h] = [down, up]
    for h in range(2):
        a, b, near_a, near_b = sides(h, x, z)
        both = pl.ds(2 * h, 2)
        lo, hi, far = around(b)
        for copy in state[h]:
            copy.wait_recv()
        src = g_ref.at[(c, *place(h, ALL, far), both)]
        hand.append(ex.go(src, src, partner))
    for copy in hand + images:
        copy.wait_recv()
    image.wait()
    ex.drain()


def scatter_kernel(
    a0_ref, a1_ref, a2_ref, a3_ref, swap_ref,
    out_ref, swapped_ref,
    s_ref, p0_ref, p1_ref, p2_ref, p3_ref, r1_ref, r2_ref, r3_ref, r4_ref, send_sem, recv_sem,
):
    d, t, x, z, c = torus()
    partner = {"tensor": t + 1 - 2 * c}
    entered = greet(
        [dp_device(x + 3, z), dp_device(x + 1, z), dp_device(x, z + 3), dp_device(x, z + 1), partner]
    )
    entered()
    ex = Exchange(send_sem, recv_sem)
    parts = ((a0_ref, p0_ref, 0, 512), (a1_ref, p1_ref, 512, 512), (a2_ref, p2_ref, 1024, 512), (a3_ref, p3_ref, 1536, 128))
    hand = [
        [ex.go(src.at[1 - c, :, :, pl.ds(2 * h, 2)], dst.at[:, :, pl.ds(2 * h, 2)], partner) for src, dst, _, _ in parts]
        for h in range(2)
    ]
    swap = ex.go(swap_ref, swapped_ref, partner)

    def add(dst, *terms):
        total = dst[...].astype(F32)
        for term in terms:
            total = total + term[...].astype(F32)
        return total

    state = [None, None]
    for h in range(2):
        a, b, near_a, near_b = sides(h, x, z)
        lo, hi, far = around(b)
        both = pl.ds(2 * h, 2)
        for copy in hand[h]:
            copy.wait_recv()

        def merge(i, _):
            for src, got, lane, width in parts:
                total = src[c, i, :, both].astype(F32) + got[i, :, both].astype(F32)
                s_ref[i, :, both, :, lane : lane + width] = total.astype(BF)
            return 0

        lax.fori_loop(0, 4, merge, 0)
        state[h] = [
            ex.go(s_ref.at[(*place(h, ALL, far), 2 * h)], r1_ref.at[h, 0], near_b[0]),
            ex.go(s_ref.at[(*place(h, ALL, far), 2 * h + 1)], r1_ref.at[h, 1], near_b[1]),
        ]
    for h in range(2):
        a, b, near_a, near_b = sides(h, x, z)
        lo, hi, far = around(b)
        both = pl.ds(2 * h, 2)
        for copy in state[h]:
            copy.wait_recv()
        for i in range(4):
            for k, quarter, slot in ((lo, 2 * h, 0), (hi, 2 * h + 1, 1)):
                ref = s_ref.at[(*place(h, i, k), quarter)]
                ref[...] = add(ref, r1_ref.at[h, slot, i]).astype(BF)
        state[h] = [
            ex.go(s_ref.at[(*place(h, ALL, lo), both)], r2_ref.at[h, 0], near_b[0]),
            ex.go(s_ref.at[(*place(h, ALL, hi), both)], r2_ref.at[h, 1], near_b[1]),
        ]
    for h in range(2):
        a, b, near_a, near_b = sides(h, x, z)
        lo, hi, far = around(a)
        for copy in state[h]:
            copy.wait_recv()
        for i in range(4):
            ref = s_ref.at[(*place(h, i, b), pl.ds(2 * h, 2))]
            ref[...] = add(ref, r2_ref.at[h, 0, i], r2_ref.at[h, 1, i]).astype(BF)
        state[h] = [
            ex.go(s_ref.at[(*place(h, far, b), 2 * h)], r3_ref.at[h, 0], near_a[0]),
            ex.go(s_ref.at[(*place(h, far, b), 2 * h + 1)], r3_ref.at[h, 1], near_a[1]),
        ]
    for h in range(2):
        a, b, near_a, near_b = sides(h, x, z)
        lo, hi, far = around(a)
        both = pl.ds(2 * h, 2)
        for copy in state[h]:
            copy.wait_recv()
        for k, quarter, slot in ((lo, 2 * h, 0), (hi, 2 * h + 1, 1)):
            ref = s_ref.at[(*place(h, k, b), quarter)]
            ref[...] = add(ref, r3_ref.at[h, slot]).astype(BF)
        state[h] = [
            ex.go(s_ref.at[(*place(h, lo, b), both)], r4_ref.at[h, 0], near_a[0]),
            ex.go(s_ref.at[(*place(h, hi, b), both)], r4_ref.at[h, 1], near_a[1]),
        ]
    for h in range(2):
        a, b, near_a, near_b = sides(h, x, z)
        for copy in state[h]:
            copy.wait_recv()
        ref = s_ref.at[(*place(h, a, b), pl.ds(2 * h, 2))]
        out_ref[2 * h : 2 * h + 2] = add(ref, r4_ref.at[h, 0], r4_ref.at[h, 1])
    swap.wait_recv()
    ex.drain()


VM = pl.BlockSpec(memory_space=pltpu.VMEM)
HBM = pl.BlockSpec(memory_space=pl.ANY)


def params(collective_id, megabytes):
    return pltpu.CompilerParams(
        collective_id=collective_id, has_side_effects=True, vmem_limit_bytes=megabytes * 1024 * 1024
    )


def weight_scratch():
    return [pltpu.VMEM((2, D, 512), BF)] * 3 + [pltpu.SemaphoreType.DMA((3,))]


def shape(dims, dtype):
    return jax.ShapeDtypeStruct(dims, dtype)


def gather(packed, image):
    g, xg = pl.pallas_call(
        gather_kernel,
        out_shape=(shape((2, 4, 4, 4, 16, WIDE), BF), shape((8, ROWS, 128), BF)),
        in_specs=[HBM, HBM],
        out_specs=(HBM, HBM),
        scratch_shapes=[pltpu.SemaphoreType.DMA((2,)), pltpu.SemaphoreType.DMA((32,)), pltpu.SemaphoreType.DMA((32,))],
        compiler_params=params(0, 8),
        name="gather",
    )(packed, image)
    return g.reshape(2, D, WIDE), jnp.transpose(xg, (1, 0, 2)).reshape(ROWS, D).astype(F32)


def forward(x, weights, vec):
    return pl.pallas_call(
        forward_kernel,
        out_shape=(
            shape((ROWS, D), BF),
            shape((2, KEYS, 384), BF),
            shape((8, KEYS), F32),
            shape((2, ROWS, 128), BF),
            shape((ROWS, D), F32),
            shape((ROWS, D), BF),
            shape((2, ROWS, 512), F32),
            shape((2, ROWS, 512), BF),
            shape((ROWS, D), F32),
        ),
        in_specs=[VM, HBM, VM],
        out_specs=(VM,) * 9,
        scratch_shapes=[pltpu.VMEM((2, 128, KEYS), BF)] + weight_scratch() + ring_scratch() + ring_scratch(),
        compiler_params=params(1, 50),
        name="forward",
    )(x, weights, vec)


def backward(g, x, saved, weights, vec):
    n1, qkv, lse, o, mid, n2, slope, a = saved
    return pl.pallas_call(
        backward_kernel,
        out_shape=(
            shape((ROWS, D), F32),
            shape((2, D, 512), BF),
            shape((2, D, 512), BF),
            shape((2, D, 512), BF),
            shape((8, D), F32),
        ),
        in_specs=[VM] * 10 + [HBM, VM],
        out_specs=(VM,) * 5,
        scratch_shapes=[
            pltpu.VMEM((ROWS, D), BF),
            pltpu.VMEM((ROWS, D), BF),
            pltpu.VMEM((2, ROWS, 512), BF),
            pltpu.VMEM((2, KEYS, 128), BF),
            pltpu.VMEM((2, 128, KEYS), BF),
            pltpu.VMEM((2, ROWS, 384), BF),
            pltpu.VMEM((2, KEYS, 128), F32),
            pltpu.VMEM((2, KEYS, 128), F32),
            pltpu.VMEM((ROWS, D), F32),
        ]
        + weight_scratch()
        + ring_scratch()
        + ring_scratch(),
        compiler_params=params(2, 58),
        name="backward",
    )(g, x, mid, n1, n2, qkv, lse, o, slope, a, weights, vec)


def scatter(grads, vectors, swap):
    split = (2, 4, 4, 4, 16)
    operands = [grad.reshape(*split, 512) for grad in grads] + [vectors.reshape(*split, 128)]
    out, swapped = pl.pallas_call(
        scatter_kernel,
        out_shape=(shape((4, 16, WIDE), F32), shape((ROWS, 128), F32)),
        in_specs=[VM] * 5,
        out_specs=(VM, VM),
        scratch_shapes=[pltpu.VMEM((4, 4, 4, 16, WIDE), BF)]
        + [pltpu.VMEM((4, 4, 4, 16, width), BF) for width in (512, 512, 512, 128)]
        + [
            pltpu.VMEM((2, 2, 4, 16, WIDE), BF),
            pltpu.VMEM((2, 2, 4, 2, 16, WIDE), BF),
            pltpu.VMEM((2, 2, 16, WIDE), BF),
            pltpu.VMEM((2, 2, 2, 16, WIDE), BF),
            pltpu.SemaphoreType.DMA((32,)),
            pltpu.SemaphoreType.DMA((32,)),
        ],
        compiler_params=params(3, 40),
        name="scatter",
    )(*operands, swap)
    return out.reshape(64, WIDE), swapped


def pack_weights(w, layer):
    ag, ash, qw, qb, kw, vw, vb, ow, ob, fg, fs, uw, ub, dw, db = [v[layer] for v in w]
    heads = jnp.concatenate([qb.reshape(8), vb.reshape(8), ub.reshape(32), jnp.zeros((16,), BF)])
    columns = jnp.stack([ag, ash, ob, fg, fs, db, heads], axis=1)
    columns = jnp.pad(columns, ((0, 0), (0, 121)))
    return jnp.concatenate([qw, kw, vw, ow.T, uw, dw.T, columns], axis=1).reshape(4, 16, WIDE)


def unpack_vectors(g):
    rows = g[0, :, 1536:1542].T
    heads = g[:, :, 1542].reshape(2, 16, 64)
    qb = heads[:, :, 0:8].reshape(2, 16, 2, 4).transpose(0, 2, 1, 3).reshape(256)
    vb = heads[:, :, 8:16].reshape(2, 16, 2, 4).transpose(0, 2, 1, 3).reshape(256)
    ub = heads[:, :, 16:48].reshape(2, 16, 8, 4).transpose(0, 2, 1, 3).reshape(1, D)
    six = jnp.concatenate([qb, vb, jnp.zeros((512,), BF)]).reshape(1, D)
    return jnp.concatenate([rows, six, ub], axis=0).astype(F32)


def pack_vectors(vg):
    columns = vg[0:6].T
    both = []
    for c in range(2):
        heads = jnp.concatenate(
            [vg[6, c * 128 : c * 128 + 128], vg[6, 256 + c * 128 : 384 + c * 128], vg[7, c * 512 : c * 512 + 512]]
        )
        tiled = jnp.tile(heads.reshape(12, 64).T, (16, 1))
        both.append(jnp.concatenate([columns, tiled, jnp.zeros((D, 110), F32)], axis=1))
    return jnp.stack(both).astype(BF)


def unpack_grads(s, d):
    columns = [s[:, 1536 + k] for k in range(6)]
    heads = s[:, 1542:1554].T.reshape(12, 64)
    mine = lax.dynamic_slice_in_dim(heads, d * 4, 4, axis=1)
    return (
        columns[0], columns[1], s[:, 0:128], mine[0:2], s[:, 128:256], s[:, 256:384], mine[2:4], s[:, 384:512].T,
        columns[2], columns[3], columns[4], s[:, 512:1024], mine[4:12], s[:, 1024:1536].T, columns[5],
    )


def local(images, cotangent, counts, *weights):
    d, t = lax.axis_index("dp"), lax.axis_index("tensor")
    c = lax.rem(t, 2)
    alive = (counts[0] > c).astype(F32)
    pad = ((0, 0), (0, ROWS - SEQ), (0, 0))
    g0, x0 = gather(pack_weights(weights, 0), jnp.pad(images, pad))
    vec0 = unpack_vectors(g0)
    x1_and = forward(x0, g0, vec0)
    saved0, x1 = x1_and[:-1], x1_and[-1]
    g1, cot = gather(pack_weights(weights, 1), jnp.pad(cotangent, pad))
    vec1 = unpack_vectors(g1)
    x2_and = forward(x1, g1, vec1)
    saved1, x2 = x2_and[:-1], x2_and[-1]
    y = t // 2

    def keep_and_swap(full):
        kept = lax.dynamic_slice_in_dim(full, t * 128, 128, axis=1)
        given = lax.dynamic_slice_in_dim(full, (4 * y + 1 - t) * 128, 128, axis=1)
        return kept, given

    def both_images(kept, got):
        kept, got = kept[:SEQ], got[:SEQ]
        return jnp.where(c == 0, jnp.stack([kept, got]), jnp.stack([got, kept]))

    kept_act, given_act = keep_and_swap(x2 * alive)
    grad1, *grads1 = backward(cot * alive, x1, saved1, g1, vec1)
    s1, got_act = scatter(grads1[:3], pack_vectors(grads1[3]), given_act)
    grad0, *grads0 = backward(grad1, x0, saved0, g0, vec0)
    kept_in, given_in = keep_and_swap(grad0)
    s0, got_in = scatter(grads0[:3], pack_vectors(grads0[3]), given_in)
    u0, u1 = unpack_grads(s0, d), unpack_grads(s1, d)
    return (
        both_images(kept_act, got_act).astype(BF),
        both_images(kept_in, got_in),
        *(jnp.stack([a, b]) for a, b in zip(u0, u1)),
    )


def solution(mesh):
    row = P(None, "dp")
    columns = P(None, "dp", "tensor")
    heads = P(None, "tensor", "dp")
    weights = (
        row, row, columns, heads, columns, columns, heads, heads, row, row, row, columns, heads, heads, row,
    )
    stream = P("dp", None, "tensor")
    return jax.shard_map(
        local,
        mesh=mesh,
        in_specs=(stream, stream, P("dp"), *weights),
        out_specs=(stream, stream, *weights),
        check_vma=False,
    )
```

```python
import functools
import math

import jax
import jax.numpy as jnp
from jax import lax
from jax.experimental import pallas as pl
from jax.experimental.pallas import tpu as pltpu
from jax.sharding import PartitionSpec as P

HD = 64
EPSILON = 1e-06
SCALE = 1.0 / math.sqrt(HD)
BF = jnp.bfloat16
F32 = jnp.float32

SEQ = 577
D = 1024
ROWS = 592
KEYS = 640
ATT = 640
MLP = 1024
CHUNKS = ((0, 128), (128, 128), (256, 128), (384, 128), (512, 80))
NQ = len(CHUNKS)

TN = (((1,), (1,)), ((), ()))
NT = (((0,), (0,)), ((), ()))


def dot(a, b, dims=(((1,), (0,)), ((), ()))):
    return lax.dot_general(a, b, dims, preferred_element_type=F32)


def block(k, width=256):
    return pl.ds(pl.multiple_of(k * width, width), width)


def greet(devices):
    barrier = pltpu.get_barrier_semaphore()
    for device in devices:
        pl.semaphore_signal(barrier, inc=1, device_id=device, device_id_type=pl.DeviceIdType.MESH)
    return lambda: pl.semaphore_wait(barrier, len(devices))


class Ring:
    def __init__(self, send, near, far, full, send_sem, recv_sem):
        t = lax.axis_index("tensor")
        y = t // 2
        self.y = y
        self.yl, self.yr, self.yo = lax.rem(y + 3, 4), lax.rem(y + 1, 4), lax.rem(y + 2, 4)
        self.left = {"tensor": lax.rem(t + 6, 8)}
        self.right = {"tensor": lax.rem(t + 2, 8)}
        self.send, self.near, self.far, self.full = send, near, far, full
        self.send_sem, self.recv_sem = send_sem, recv_sem
        self.flying = {}

    def go(self, stage, q, to_left, to_right):
        copies = []
        for side, (src, dst) in enumerate((to_left, to_right)):
            copy = pltpu.make_async_remote_copy(
                src_ref=src,
                dst_ref=dst,
                send_sem=self.send_sem.at[stage, q, side],
                recv_sem=self.recv_sem.at[stage, q, side],
                device_id=self.left if side == 0 else self.right,
                device_id_type=pl.DeviceIdType.MESH,
            )
            copy.start()
            copies.append(copy)
        self.flying[stage, q] = copies

    def arrive(self, stage, q):
        for copy in self.flying[stage, q]:
            copy.wait_recv()

    def parts(self, q):
        r0, nr = CHUNKS[q]
        top = 64 if nr == 128 else 48
        return pl.ds(r0, nr), pl.ds(r0, top), pl.ds(r0 + top, nr - top)

    def stage0(self, q):
        rows, a, b = self.parts(q)
        c = block(self.yo)
        self.go(0, q, (self.send.at[a, c], self.near.at[0, a, :]), (self.send.at[b, c], self.near.at[1, b, :]))

    def stage1(self, q):
        rows, a, b = self.parts(q)
        self.arrive(0, q)
        cl, cr = block(self.yl), block(self.yr)
        self.send[a, cl] = (self.send[a, cl].astype(F32) + self.near[0, a, :].astype(F32)).astype(BF)
        self.send[b, cr] = (self.send[b, cr].astype(F32) + self.near[1, b, :].astype(F32)).astype(BF)
        self.go(
            1, q, (self.send.at[rows, cl], self.far.at[0, rows, :]), (self.send.at[rows, cr], self.far.at[1, rows, :])
        )

    def stage2(self, q):
        rows, a, b = self.parts(q)
        self.arrive(1, q)
        c = block(self.y)
        total = self.send[rows, c].astype(F32) + self.far[0, rows, :].astype(F32) + self.far[1, rows, :].astype(F32)
        self.full[rows, c] = total.astype(BF)
        self.go(2, q, (self.full.at[rows, c], self.full.at[rows, c]), (self.full.at[rows, c], self.full.at[rows, c]))

    def stage3(self, q):
        rows, a, b = self.parts(q)
        self.arrive(2, q)
        cl, cr = block(self.yl), block(self.yr)
        self.go(3, q, (self.full.at[a, cr], self.full.at[a, cr]), (self.full.at[b, cl], self.full.at[b, cl]))

    def stage4(self, q):
        self.arrive(3, q)

    def drain(self):
        for copies in self.flying.values():
            for copy in copies:
                copy.wait_send()
        self.flying = {}


def ring_scratch():
    return [
        pltpu.VMEM((ROWS, D), BF),
        pltpu.VMEM((2, ROWS, 256), BF),
        pltpu.VMEM((2, ROWS, 256), BF),
        pltpu.VMEM((ROWS, D), BF),
        pltpu.SemaphoreType.DMA((4, NQ, 2)),
        pltpu.SemaphoreType.DMA((4, NQ, 2)),
    ]


def standardize(x):
    average = jnp.mean(x, axis=1, keepdims=True)
    centered = x - average
    variance = jnp.mean(centered * centered, axis=1, keepdims=True)
    rstd = lax.rsqrt(variance + EPSILON)
    return centered * rstd, rstd


def half_masks():
    lane = lax.broadcasted_iota(jnp.int32, (1, 128), 1)
    first = (lane < 64).astype(F32)
    return first.astype(BF), (1.0 - first).astype(BF)


def key_rows():
    return lax.broadcasted_iota(jnp.int32, (KEYS, 128), 0) < SEQ


def flip(rows):
    return jnp.transpose(rows.astype(F32), (1, 0))


def pair(first, second):
    top = lax.broadcasted_iota(jnp.int32, first.shape, 0) < 64
    return jnp.where(top, first, second)


def torus():
    d, t = lax.axis_index("dp"), lax.axis_index("tensor")
    x, z = d // 4, lax.rem(d, 4)
    return d, t, x, z, lax.rem(t, 2)


def dp_device(x, z):
    return {"dp": lax.rem(x + 4, 4) * 4 + lax.rem(z + 4, 4)}


class Exchange:
    def __init__(self, send_sem, recv_sem):
        self.send_sem, self.recv_sem, self.count, self.started = send_sem, recv_sem, 0, []

    def go(self, src, dst, device):
        copy = pltpu.make_async_remote_copy(
            src_ref=src,
            dst_ref=dst,
            send_sem=self.send_sem.at[self.count],
            recv_sem=self.recv_sem.at[self.count],
            device_id=device,
            device_id_type=pl.DeviceIdType.MESH,
        )
        copy.start()
        self.count += 1
        self.started.append(copy)
        return copy

    def drain(self):
        for copy in self.started:
            copy.wait_send()


def sides(half, x, z):
    if half == 0:
        a, b = x, z
        near = (dp_device(x + 3, z), dp_device(x + 1, z)), (dp_device(x, z + 3), dp_device(x, z + 1))
    else:
        a, b = z, x
        near = (dp_device(x, z + 3), dp_device(x, z + 1)), (dp_device(x + 3, z), dp_device(x + 1, z))
    return a, b, near[0], near[1]


def place(half, a, b):
    return (a, b) if half == 0 else (b, a)


def around(k):
    return lax.rem(k + 3, 4), lax.rem(k + 1, 4), lax.rem(k + 2, 4)


ALL = pl.ds(0, 4)

class Background:
    def __init__(self):
        self.steps = []

    def add(self, *steps):
        self.steps.extend(steps)

    def run(self, count=1):
        for _ in range(min(count, len(self.steps))):
            self.steps.pop(0)()

    def until(self, step):
        while step in self.steps:
            self.steps.pop(0)()


def pipeline(stages, background, fillers=None):
    fillers = fillers or {}
    for step in range(NQ + len(stages) - 1):
        for k, stage in enumerate(stages):
            if 0 <= step - k < NQ:
                stage(step - k)
            if k == 0:
                for filler in fillers.get(step, ()):
                    filler()
                background.run()


class Gather:
    def __init__(self, ex, w):
        self.ex, self.w = ex, w
        d, t, self.x, self.z, self.c = torus()
        self.partner = {"tensor": t + 1 - 2 * self.c}
        self.state = [None, None]
        self.hand = []

    def at(self, h, a, b, quarters):
        return self.w.at[(self.c, *place(h, a, b), quarters)]

    def push(self, ref, device):
        return self.ex.go(ref, ref, device)

    def one(self):
        for h in range(2):
            a, b, near_a, near_b = sides(h, self.x, self.z)
            own = self.at(h, a, b, pl.ds(2 * h, 2))
            self.state[h] = [self.push(own, near_a[0]), self.push(own, near_a[1])]

    def two(self):
        for h in range(2):
            a, b, near_a, near_b = sides(h, self.x, self.z)
            lo, hi, far = around(a)
            from_hi, from_lo = self.state[h]
            from_lo.wait_recv()
            up = self.push(self.at(h, lo, b, 2 * h), near_a[1])
            from_hi.wait_recv()
            down = self.push(self.at(h, hi, b, 2 * h + 1), near_a[0])
            self.state[h] = [down, up]

    def three(self):
        for h in range(2):
            a, b, near_a, near_b = sides(h, self.x, self.z)
            for copy in self.state[h]:
                copy.wait_recv()
            row = self.at(h, ALL, b, pl.ds(2 * h, 2))
            self.state[h] = [self.push(row, near_b[0]), self.push(row, near_b[1])]
            self.hand.append(self.push(row, self.partner))

    def four(self):
        for h in range(2):
            a, b, near_a, near_b = sides(h, self.x, self.z)
            both = pl.ds(2 * h, 2)
            lo, hi, far = around(b)
            from_hi, from_lo = self.state[h]
            from_lo.wait_recv()
            up = self.push(self.at(h, ALL, lo, 2 * h), near_b[1])
            self.hand.append(self.push(self.at(h, ALL, lo, both), self.partner))
            from_hi.wait_recv()
            down = self.push(self.at(h, ALL, hi, 2 * h + 1), near_b[0])
            self.hand.append(self.push(self.at(h, ALL, hi, both), self.partner))
            self.state[h] = [down, up]

    def five(self):
        for h in range(2):
            a, b, near_a, near_b = sides(h, self.x, self.z)
            lo, hi, far = around(b)
            for copy in self.state[h]:
                copy.wait_recv()
            self.hand.append(self.push(self.at(h, ALL, far, pl.ds(2 * h, 2)), self.partner))

    def six(self):
        for copy in self.hand:
            copy.wait_recv()


class Scatter:
    def __init__(self, ex, r, out, got, r1, r2, r3, r4):
        self.ex, self.r, self.out, self.got = ex, r, out, got
        self.r1, self.r2, self.r3, self.r4 = r1, r2, r3, r4
        d, t, self.x, self.z, self.c = torus()
        self.partner = {"tensor": t + 1 - 2 * self.c}
        self.state = [None, None]
        self.sent = []

    def at(self, h, a, b, quarters):
        return self.r.at[(self.c, *place(h, a, b), quarters)]

    def push(self, src, dst, device):
        copy = self.ex.go(src, dst, device)
        self.sent.append(copy)
        return copy

    def landed(self, h):
        for copy in self.state[h]:
            copy.wait_recv()

    def zero(self):
        for h in range(2):
            both = pl.ds(2 * h, 2)
            self.state[h] = [
                self.push(self.r.at[1 - self.c, :, :, both], self.got.at[:, :, both], self.partner)
            ]

    def one(self):
        for h in range(2):
            a, b, near_a, near_b = sides(h, self.x, self.z)
            lo, hi, far = around(b)
            both = pl.ds(2 * h, 2)
            self.landed(h)

            def merge(i, _):
                ref = self.r.at[self.c, i, :, both]
                ref[...] = add(ref, self.got.at[i, :, both]).astype(BF)
                return 0

            lax.fori_loop(0, 4, merge, 0)
            self.state[h] = [
                self.push(self.at(h, ALL, far, 2 * h), self.r1.at[h, 0], near_b[0]),
                self.push(self.at(h, ALL, far, 2 * h + 1), self.r1.at[h, 1], near_b[1]),
            ]

    def two(self):
        for h in range(2):
            a, b, near_a, near_b = sides(h, self.x, self.z)
            lo, hi, far = around(b)
            both = pl.ds(2 * h, 2)
            self.landed(h)
            for i in range(4):
                for k, quarter, slot in ((lo, 2 * h, 0), (hi, 2 * h + 1, 1)):
                    ref = self.at(h, i, k, quarter)
                    ref[...] = add(ref, self.r1.at[h, slot, i]).astype(BF)
            self.state[h] = [
                self.push(self.at(h, ALL, lo, both), self.r2.at[h, 0], near_b[0]),
                self.push(self.at(h, ALL, hi, both), self.r2.at[h, 1], near_b[1]),
            ]

    def three(self):
        for h in range(2):
            a, b, near_a, near_b = sides(h, self.x, self.z)
            lo, hi, far = around(a)
            self.landed(h)
            for i in range(4):
                ref = self.at(h, i, b, pl.ds(2 * h, 2))
                ref[...] = add(ref, self.r2.at[h, 0, i], self.r2.at[h, 1, i]).astype(BF)
            self.state[h] = [
                self.push(self.at(h, far, b, 2 * h), self.r3.at[h, 0], near_a[0]),
                self.push(self.at(h, far, b, 2 * h + 1), self.r3.at[h, 1], near_a[1]),
            ]

    def four(self):
        for h in range(2):
            a, b, near_a, near_b = sides(h, self.x, self.z)
            lo, hi, far = around(a)
            both = pl.ds(2 * h, 2)
            self.landed(h)
            for k, quarter, slot in ((lo, 2 * h, 0), (hi, 2 * h + 1, 1)):
                ref = self.at(h, k, b, quarter)
                ref[...] = add(ref, self.r3.at[h, slot]).astype(BF)
            self.state[h] = [
                self.push(self.at(h, lo, b, both), self.r4.at[h, 0], near_a[0]),
                self.push(self.at(h, hi, b, both), self.r4.at[h, 1], near_a[1]),
            ]

    def five(self):
        for h in range(2):
            a, b, near_a, near_b = sides(h, self.x, self.z)
            self.landed(h)
            ref = self.at(h, a, b, pl.ds(2 * h, 2))
            self.out[2 * h : 2 * h + 2] = add(ref, self.r4.at[h, 0], self.r4.at[h, 1])
        for copy in self.sent:
            copy.wait_send()

    def steps(self):
        return self.zero, self.one, self.two, self.three, self.four, self.five


def add(*terms):
    total = terms[0][...].astype(F32)
    for term in terms[1:]:
        total = total + term[...].astype(F32)
    return total


def scatter_scratch(width):
    return [
        pltpu.VMEM((2, 4, 4, 4, 16, width), BF),
        pltpu.VMEM((4, 4, 4, 16, width), BF),
        pltpu.VMEM((2, 2, 4, 16, width), BF),
        pltpu.VMEM((2, 2, 4, 2, 16, width), BF),
        pltpu.VMEM((2, 2, 16, width), BF),
        pltpu.VMEM((2, 2, 2, 16, width), BF),
    ]


def mat(ref, c, lo, hi):
    return ref[c, :, :, :, :, lo:hi].reshape(D, hi - lo)


def put(ref, c, lo, hi, value):
    ref[c, :, :, :, :, lo:hi] = value.astype(BF).reshape(4, 4, 4, 16, hi - lo)


class Local:
    def __init__(self, sem):
        self.sem, self.count = sem, 0

    def go(self, src, dst):
        copy = pltpu.make_async_copy(src, dst, self.sem.at[self.count])
        copy.start()
        self.count += 1
        return copy


def column_sum(value):
    return jnp.sum(value.astype(F32), axis=0, keepdims=True)


def low_lanes(shape):
    return lax.broadcasted_iota(jnp.int32, shape, 1) < 64


def unpack_vectors(wa, vec):
    vec[0:8, :] = flip(mat(wa, 0, 512, ATT))[0:8]
    for c in range(2):
        heads = jnp.sum(mat(wa, c, 512, ATT).reshape(16, 64, 128)[:, 0:16].astype(F32), axis=0)
        rolled = pltpu.roll(heads, 64, 1)

        def both(k):
            return jnp.where(low_lanes((1, 128)), rolled[k : k + 1], heads[k + 1 : k + 2])

        vec[6:7, c * 128 : c * 128 + 128] = both(0)
        vec[6:7, 256 + c * 128 : 384 + c * 128] = both(2)
        for m in range(4):
            vec[7:8, c * 512 + 128 * m : c * 512 + 128 * m + 128] = both(4 + 2 * m)


def pack_vectors(vg, rv, lane):
    padded = jnp.concatenate([vg[...], jnp.zeros((120, D), F32)], axis=0)
    kind = lax.broadcasted_iota(jnp.int32, (128, D), 0)
    columns = flip(jnp.where(kind < 6, padded, 0.0)).reshape(16, 64, 128)
    row = lax.broadcasted_iota(jnp.int32, (64, 128), 0)
    for c in range(2):
        pieces = [vg[6:7, c * 128 : c * 128 + 128], vg[6:7, 256 + c * 128 : 384 + c * 128]]
        pieces += [vg[7:8, c * 512 + 128 * m : c * 512 + 128 * m + 128] for m in range(4)]
        heads = jnp.zeros((64, 128), F32)
        for k, piece in enumerate(pieces):
            rolled = pltpu.roll(jnp.broadcast_to(piece, (8, 128)), 64, 1)[0:1]
            heads = jnp.where(row == 2 * k, rolled, heads)
            heads = jnp.where(row == 2 * k + 1, piece, heads)
        heads = jnp.where(low_lanes((64, 128)), 0.0, heads)
        put(rv, c, lane, lane + 128, (columns + heads[None]).reshape(D, 128))


def forward_kernel(
    img_ref, cot_ref, qw_ref, kw_ref, vw_ref, uw_ref, ow_ref, dw_ref, vp_ref,
    *refs,
):
    refs = list(refs)
    saved = [[refs.pop(0) for _ in range(9)] for _ in range(2)]
    wa_out = [refs.pop(0) for _ in range(2)]
    wm_out = [refs.pop(0) for _ in range(2)]
    vec_ref, xc_ref, act_ref = [refs.pop(0) for _ in range(3)]
    kept = [[refs.pop(0) for _ in range(9)] for _ in range(2)]
    wa = [refs.pop(0) for _ in range(2)]
    wm = [refs.pop(0) for _ in range(2)]
    xg_ref, vt_ref, give_ref, local_sem, send_sem, recv_sem = [refs.pop(0) for _ in range(6)]
    one, two = Ring(*refs[:6]), Ring(*refs[6:12])
    d, t, x, z, c_here = torus()
    y = t // 2
    partner = {"tensor": t + 1 - 2 * c_here}
    others = [{"tensor": lax.rem(t + j, 8)} for j in range(1, 8)]
    entered = greet(
        [dp_device(x + 3, z), dp_device(x + 1, z), dp_device(x, z + 3), dp_device(x, z + 1)] + others
    )
    local, ex, background = Local(local_sem), Exchange(send_sem, recv_sem), Background()
    own = []
    for layer in range(2):
        mine = wa[layer].at[c_here, x, z]
        own.append(
            [local.go(src.at[layer], mine.at[:, :, pl.ds(128 * k, 128)]) for k, src in enumerate((qw_ref, kw_ref, vw_ref))]
        )
        own.append([local.go(uw_ref.at[layer], wm[layer].at[c_here, x, z, :, :, pl.ds(0, 512)])])
        wa[layer][c_here, x, z, :, :, 384:512] = flip(ow_ref[layer]).astype(BF).reshape(4, 16, 128)
        wa[layer][c_here, x, z, :, :, 512:ATT] = vp_ref[layer]
        wm[layer][c_here, x, z, :, :, 512:MLP] = flip(dw_ref[layer]).astype(BF).reshape(4, 16, 512)
    mine = local.go(img_ref.at[c_here], xg_ref.at[t])
    theirs = local.go(cot_ref.at[c_here], xc_ref.at[t])
    groups = [Gather(ex, ref) for ref in (wa[0], wm[0], wa[1], wm[1])]
    entered()

    def start(k):
        def run():
            for copy in own[k]:
                copy.wait()
            groups[k].one()

        return run

    def exchange(src, dst):
        copies = []
        for j in range(1, 8):
            target = lax.rem(t + j, 8)
            copies.append(ex.go(src.at[lax.rem(target, 2)], dst.at[t], others[j - 1]))
        return copies

    start(0)()
    images = exchange(img_ref, xg_ref)
    first = groups[0]
    first.two()
    first.three()
    start(1)()
    first.four()
    groups[1].two()
    mine.wait()
    for copy in images:
        copy.wait_recv()
    for r0, nr in CHUNKS:
        rows = pl.ds(r0, nr)
        for j in range(8):
            kept[0][0][rows, 128 * j : 128 * j + 128] = xg_ref[j, rows, :].astype(F32)
    first.five()
    first.six()
    groups[1].three()
    cotangents = exchange(cot_ref, xc_ref)
    masks = half_masks()
    valid = key_rows()
    m0, a1, m1 = groups[1], groups[2], groups[3]
    background.add(m0.four, m0.five, m0.six)
    for group, k in ((a1, 2), (m1, 3)):
        background.add(start(k), group.two, group.three, group.four, group.five, group.six)

    def layer_forward(layer):
        x_ref, n1_ref, qkv_ref, lse_ref, o_ref, mid_ref, n2_ref, slope_ref, a_ref = kept[layer]
        x_out, n1_out, qkv_out, lse_out, o_out, mid_out, n2_out, slope_out, a_out = saved[layer]
        vec = vec_ref.at[layer]
        unpack_vectors(wa[layer], vec)
        gain, shift = vec[0:1, :], vec[1:2, :]
        qkv_ref[:, ROWS:KEYS, :] = jnp.zeros((2, KEYS - ROWS, 384), BF)
        for r0, nr in CHUNKS:
            rows = pl.ds(r0, nr)
            xhat, _ = standardize(x_ref[rows, :])
            n1_ref[rows, :] = (xhat * gain + shift).astype(BF)
        waits = [local.go(x_ref, x_out), local.go(n1_ref, n1_out), local.go(wa[layer], wa_out[layer])]
        background.run()
        for c in range(2):
            out = dot(n1_ref[...], mat(wa[layer], c, 0, 384))
            qkv_ref[c, 0:ROWS, 0:128] = (out[:, 0:128] + vec[6:7, c * 128 : c * 128 + 128]).astype(BF)
            qkv_ref[c, 0:ROWS, 128:256] = out[:, 128:256].astype(BF)
            qkv_ref[c, 0:ROWS, 256:384] = (out[:, 256:384] + vec[6:7, 256 + c * 128 : 384 + c * 128]).astype(BF)
            vt_ref[c] = flip(qkv_ref[c, :, 256:384]).astype(BF)
        waits.append(local.go(qkv_ref, qkv_out))

        def attend(q):
            r0, nr = CHUNKS[q]
            total = None
            for c in range(2):
                queries, keys = qkv_ref[c, r0 : r0 + 128, 0:128], qkv_ref[c, :, 128:256]
                halves = []
                for h in range(2):
                    s = dot(keys, queries * masks[h], TN) * SCALE
                    s = jnp.where(valid, s, -1e30)
                    top = jnp.max(s, axis=0, keepdims=True)
                    e = jnp.exp(s - top)
                    norm = jnp.sum(e, axis=0, keepdims=True)
                    lse_ref[2 * c + h : 2 * c + h + 1, r0 : r0 + 128] = top + jnp.log(norm)
                    p = (e * (1.0 / norm)).astype(BF)
                    halves.append(dot(vt_ref[c], p))
                mixed = flip(pair(*halves))[0:nr].astype(BF)
                o_ref[c, r0 : r0 + nr, :] = mixed
                part = dot(mixed, mat(wa[layer], c, 384, 512), TN)
                total = part if total is None else total + part
            one.send[r0 : r0 + nr, :] = total.astype(BF)
            one.stage0(q)
            if q == NQ - 1:
                waits.extend([local.go(lse_ref, lse_out), local.go(o_ref, o_out)])

        def feed(q):
            r0, nr = CHUNKS[q]
            rows = pl.ds(r0, nr)
            if q == 0:
                background.until(groups[2 * layer + 1].six)
                waits.append(local.go(wm[layer], wm_out[layer]))
            one.stage4(q)
            mid = x_ref[rows, :] + one.full[rows, :].astype(F32) + vec[2:3, :]
            mid_ref[rows, :] = mid
            xhat, _ = standardize(mid)
            n2 = (xhat * vec[3:4, :] + vec[4:5, :]).astype(BF)
            n2_ref[rows, :] = n2
            total = None
            for c in range(2):
                u = dot(n2, mat(wm[layer], c, 0, 512)) + vec[7:8, c * 512 : c * 512 + 512]
                phi = 0.5 * (1.0 + lax.erf(u * (1.0 / math.sqrt(2.0))))
                slope = phi + u * (jnp.exp(-0.5 * u * u) * (1.0 / math.sqrt(2.0 * math.pi)))
                slope_ref[c, rows, :] = slope.astype(BF)
                a = (u * phi).astype(BF)
                a_ref[c, rows, :] = a
                part = dot(a, mat(wm[layer], c, 512, MLP), TN)
                total = part if total is None else total + part
            two.send[rows, :] = total.astype(BF)
            two.stage0(q)
            if q == NQ - 1:
                waits.extend(
                    local.go(src, dst)
                    for src, dst in ((mid_ref, mid_out), (n2_ref, n2_out), (slope_ref, slope_out), (a_ref, a_out))
                )

        def finish(q):
            r0, nr = CHUNKS[q]
            rows = pl.ds(r0, nr)
            two.stage4(q)
            kept[1][0][rows, :] = mid_ref[rows, :] + two.full[rows, :].astype(F32) + vec[5:6, :]

        swaps = []

        def last(q):
            r0, nr = CHUNKS[q]
            rows = pl.ds(r0, nr)
            two.arrive(1, q)
            c = block(y)
            total = two.send[rows, c].astype(F32) + two.far[0, rows, :].astype(F32) + two.far[1, rows, :].astype(F32)
            total = total + mid_ref[rows, c] + vec[5:6, c]
            left, right = total[:, 0:128].astype(BF), total[:, 128:256].astype(BF)
            act_ref[c_here, rows, :] = jnp.where(c_here == 0, left, right)
            give_ref[rows, :] = jnp.where(c_here == 0, right, left)
            swaps.append(ex.go(give_ref.at[rows], act_ref.at[c_here, rows], partner))

        stages = (attend, one.stage1, one.stage2, one.stage3, feed, two.stage1)
        stages += (two.stage2, two.stage3, finish) if layer == 0 else (last,)
        pipeline(stages, background)
        one.drain()
        two.drain()
        return waits, swaps

    waits0, _ = layer_forward(0)
    background.until(groups[2].six)
    waits1, swaps = layer_forward(1)
    theirs.wait()
    for copy in cotangents + swaps:
        copy.wait_recv()
    for copy in waits0 + waits1:
        copy.wait()
    ex.drain()


def backward_kernel(
    cot_ref, vec_ref, *refs,
):
    refs = list(refs)
    saved = [[refs.pop(0) for _ in range(9)] for _ in range(2)]
    wa_in = [refs.pop(0) for _ in range(2)]
    wm_in = [refs.pop(0) for _ in range(2)]
    gin_ref, mlp0_ref, mlp1_ref, att0_ref, att1_ref, small_ref = [refs.pop(0) for _ in range(6)]
    x_ref, n1_ref, qkv_ref, lse_ref, o_ref, mid_ref, n2_ref, slope_ref, a_ref = [refs.pop(0) for _ in range(9)]
    wa, wm = refs.pop(0), refs.pop(0)
    xg_ref, g_ref, gm_ref, go_ref, hid_ref, dout_ref, kt_ref, dqkv_ref, dk_ref, dv_ref, gmid_ref, vg_ref, give_ref = [
        refs.pop(0) for _ in range(13)
    ]
    local_sem, send_sem, recv_sem = [refs.pop(0) for _ in range(3)]
    mlp, att, small = [[refs.pop(0) for _ in range(6)] for _ in range(3)]
    one, two = Ring(*refs[:6]), Ring(*refs[6:12])
    d, t, x, z, c_here = torus()
    y = t // 2
    partner = {"tensor": t + 1 - 2 * c_here}
    entered = greet(
        [dp_device(x + 3, z), dp_device(x + 1, z), dp_device(x, z + 3), dp_device(x, z + 1), one.left, one.right, partner]
    )
    local, ex, background = Local(local_sem), Exchange(send_sem, recv_sem), Background()

    def load_mlp(layer):
        _, _, _, _, _, mid, n2, slope, a = saved[layer]
        pairs = ((wm_in[layer], wm), (slope, slope_ref), (a, a_ref), (mid, mid_ref), (n2, n2_ref))
        return [local.go(src, dst) for src, dst in pairs]

    def load_att(layer):
        stream, n1, qkv, lse, o = saved[layer][:5]
        pairs = ((wa_in[layer], wa), (qkv, qkv_ref), (lse, lse_ref), (o, o_ref), (stream, x_ref), (n1, n1_ref))
        return [local.go(src, dst) for src, dst in pairs]

    cot = local.go(cot_ref, xg_ref)
    mlp_loads, att_loads = load_mlp(1), load_att(1)
    masks = half_masks()
    valid = key_rows()
    dout_ref[:, ROWS:KEYS, :] = jnp.zeros((2, KEYS - ROWS, 128), BF)
    cot.wait()
    for r0, nr in CHUNKS:
        rows = pl.ds(r0, nr)
        for j in range(8):
            g_ref[rows, 128 * j : 128 * j + 128] = xg_ref[j, rows, :].astype(F32)
    entered()
    swaps = []

    def layer_backward(layer, mlp_loads, att_loads):
        vec = vec_ref.at[layer]
        vg_ref[...] = jnp.zeros((8, D), F32)
        dk_ref[...] = jnp.zeros(dk_ref.shape, F32)
        dv_ref[...] = jnp.zeros(dv_ref.shape, F32)
        for r0, nr in CHUNKS:
            gm_ref[r0 : r0 + nr, :] = g_ref[r0 : r0 + nr, :].astype(BF)
        for copy in mlp_loads:
            copy.wait()
        mlp_scatter = Scatter(ex, mlp[0], (mlp0_ref, mlp1_ref)[layer], *mlp[1:])
        att_scatter = Scatter(ex, att[0], (att0_ref, att1_ref)[layer], *att[1:])

        def add_vector(row, value, lane=0):
            width = value.shape[1]
            vg_ref[row : row + 1, lane : lane + width] = vg_ref[row : row + 1, lane : lane + width] + value

        def hidden(q):
            r0, nr = CHUNKS[q]
            rows = pl.ds(r0, nr)
            gm = gm_ref[rows, :]
            add_vector(5, column_sum(gm))
            total = None
            for c in range(2):
                da = dot(gm, mat(wm, c, 512, MLP))
                du = (da * slope_ref[c, rows, :].astype(F32)).astype(BF)
                hid_ref[c, rows, :] = du
                add_vector(7, column_sum(du), c * 512)
                part = dot(du, mat(wm, c, 0, 512), TN)
                total = part if total is None else total + part
            one.send[rows, :] = total.astype(BF)
            one.stage0(q)

        def norm_back(ring, q, stream, grad, gain_row, shift_row):
            r0, nr = CHUNKS[q]
            rows = pl.ds(r0, nr)
            ring.stage4(q)
            dn = ring.full[rows, :].astype(F32)
            xhat, rstd = standardize(stream[rows, :])
            add_vector(gain_row, column_sum(dn * xhat))
            add_vector(shift_row, column_sum(dn))
            e = dn * vec[gain_row : gain_row + 1, :]
            first = jnp.mean(e, axis=1, keepdims=True)
            second = jnp.mean(e * xhat, axis=1, keepdims=True)
            return grad[rows, :] + rstd * (e - first - xhat * second)

        def attend(q):
            r0, nr = CHUNKS[q]
            rows = pl.ds(r0, nr)
            if q == 0:
                for copy in att_loads:
                    copy.wait()
                for c in range(2):
                    kt_ref[c] = flip(qkv_ref[c, :, 128:256]).astype(BF)
            mid_grad = norm_back(one, q, mid_ref, g_ref, 3, 4)
            gmid_ref[rows, :] = mid_grad
            go = mid_grad.astype(BF)
            go_ref[rows, :] = go
            add_vector(2, column_sum(go))
            for c in range(2):
                dout_ref[c, rows, :] = dot(go, mat(wa, c, 384, 512)).astype(BF)
                queries = qkv_ref[c, r0 : r0 + 128, 0:128]
                keys, values = qkv_ref[c, :, 128:256], qkv_ref[c, :, 256:384]
                dout = dout_ref[c, r0 : r0 + 128, :]
                halves = []
                for h in range(2):
                    qh, doh = queries * masks[h], dout * masks[h]
                    s = dot(keys, qh, TN) * SCALE
                    p = jnp.where(valid, jnp.exp(s - lse_ref[2 * c + h : 2 * c + h + 1, r0 : r0 + 128]), 0.0)
                    dp = dot(values, doh, TN)
                    delta = jnp.sum(dp * p, axis=0, keepdims=True)
                    ds = (p * (dp - delta)).astype(BF)
                    dv_ref[c] = dv_ref[c] + dot(p.astype(BF), doh)
                    dk_ref[c] = dk_ref[c] + dot(ds, qh)
                    halves.append(dot(kt_ref[c], ds))
                dq = (flip(pair(*halves)) * SCALE)[0:nr].astype(BF)
                dqkv_ref[c, rows, 0:128] = dq

        def down_grad(c):
            def run():
                put(mlp[0], c, 512, MLP, dot(gm_ref[...], a_ref[c], NT))

            return run

        def up_grad(c):
            def run():
                put(mlp[0], c, 0, 512, dot(n2_ref[...], hid_ref[c], NT))

            return run

        def out_grad():
            for c in range(2):
                put(att[0], c, 384, 512, dot(go_ref[...], o_ref[c], NT))

        def qkv_grad(c):
            def run():
                put(att[0], c, 0, 384, dot(n1_ref[...], dqkv_ref[c], NT))

            return run

        pipeline(
            (hidden, one.stage1, one.stage2, one.stage3, attend),
            background,
            {
                1: (down_grad(0),),
                2: (down_grad(1),),
                5: (up_grad(0),),
                6: (up_grad(1), lambda: background.add(*mlp_scatter.steps())),
            },
        )
        more = (load_mlp(0) if layer else None,)
        for c in range(2):
            dqkv_ref[c, :, 128:256] = (dk_ref[c, 0:ROWS] * SCALE).astype(BF)
            dqkv_ref[c, :, 256:384] = dv_ref[c, 0:ROWS].astype(BF)

        def project(q):
            r0, nr = CHUNKS[q]
            rows = pl.ds(r0, nr)
            total = None
            for c in range(2):
                grads = dqkv_ref[c, rows, :]
                add_vector(6, column_sum(grads[:, 0:128]), c * 128)
                add_vector(6, column_sum(grads[:, 256:384]), 256 + c * 128)
                part = dot(grads, mat(wa, c, 0, 384), TN)
                total = part if total is None else total + part
            two.send[rows, :] = total.astype(BF)
            two.stage0(q)

        def finish(q):
            r0, nr = CHUNKS[q]
            rows = pl.ds(r0, nr)
            g_ref[rows, :] = norm_back(two, q, x_ref, gmid_ref, 0, 1)
            if layer == 0:
                left, right = g_ref[rows, block(2 * y, 128)], g_ref[rows, block(2 * y + 1, 128)]
                gin_ref[c_here, rows, :] = jnp.where(c_here == 0, left, right)
                give_ref[rows, :] = jnp.where(c_here == 0, right, left)
                swaps.append(ex.go(give_ref.at[rows], gin_ref.at[c_here, rows], partner))

        pipeline(
            (project, two.stage1, two.stage2, two.stage3, finish),
            background,
            {
                1: (out_grad,),
                2: (qkv_grad(0),),
                3: (qkv_grad(1), lambda: background.add(*att_scatter.steps())),
            },
        )
        pack_vectors(vg_ref, small[0], 128 * layer)
        one.drain()
        two.drain()
        return more[0]

    mlp_loads = layer_backward(1, mlp_loads, att_loads)
    layer_backward(0, mlp_loads, load_att(0))
    last = Scatter(ex, small[0], small_ref, *small[1:])
    last.zero()
    background.run(100)
    for step in last.steps()[1:]:
        step()
    for copy in swaps:
        copy.wait_recv()
        copy.wait_send()


VM = pl.BlockSpec(memory_space=pltpu.VMEM)
HBM = pl.BlockSpec(memory_space=pl.ANY)


def params(collective_id, megabytes):
    return pltpu.CompilerParams(
        collective_id=collective_id, has_side_effects=True, vmem_limit_bytes=megabytes * 1024 * 1024
    )


def shape(dims, dtype):
    return jax.ShapeDtypeStruct(dims, dtype)


LAYER = (
    ((ROWS, D), F32),
    ((ROWS, D), BF),
    ((2, KEYS, 384), BF),
    ((8, KEYS), F32),
    ((2, ROWS, 128), BF),
    ((ROWS, D), F32),
    ((ROWS, D), BF),
    ((2, ROWS, 512), BF),
    ((2, ROWS, 512), BF),
)
WA = ((2, 4, 4, 4, 16, ATT), BF)
WM = ((2, 4, 4, 4, 16, MLP), BF)
DMA = pltpu.SemaphoreType.DMA


def vmem(*kinds):
    return [pltpu.VMEM(*kind) for kind in kinds]


def forward(*operands):
    outs = [shape(*kind) for kind in LAYER * 2 + (WA, WA, WM, WM)]
    outs += [shape((2, 8, D), F32), shape((8, ROWS, 128), BF), shape((2, ROWS, 128), BF)]
    return pl.pallas_call(
        forward_kernel,
        out_shape=tuple(outs),
        in_specs=[HBM] * 6 + [VM] * 3,
        out_specs=tuple([HBM] * 22 + [VM, HBM, VM]),
        scratch_shapes=vmem(*LAYER, *LAYER, WA, WA, WM, WM, ((8, ROWS, 128), BF), ((2, 128, KEYS), BF), ((ROWS, 128), BF))
        + [DMA((40,)), DMA((128,)), DMA((128,))]
        + ring_scratch()
        + ring_scratch(),
        compiler_params=params(0, 58),
        name="forward",
    )(*operands)


def backward(*operands):
    return pl.pallas_call(
        backward_kernel,
        out_shape=(
            shape((2, ROWS, 128), F32),
            shape((4, 16, MLP), F32),
            shape((4, 16, MLP), F32),
            shape((4, 16, 512), F32),
            shape((4, 16, 512), F32),
            shape((4, 16, 256), F32),
        ),
        in_specs=[HBM, VM] + [HBM] * 22,
        out_specs=(VM,) * 6,
        scratch_shapes=vmem(
            *LAYER,
            WA,
            WM,
            ((8, ROWS, 128), BF),
            ((ROWS, D), F32),
            ((ROWS, D), BF),
            ((ROWS, D), BF),
            ((2, ROWS, 512), BF),
            ((2, KEYS, 128), BF),
            ((2, 128, KEYS), BF),
            ((2, ROWS, 384), BF),
            ((2, KEYS, 128), F32),
            ((2, KEYS, 128), F32),
            ((ROWS, D), F32),
            ((8, D), F32),
            ((ROWS, 128), F32),
        )
        + [DMA((32,)), DMA((100,)), DMA((100,))]
        + scatter_scratch(MLP)
        + scatter_scratch(512)
        + scatter_scratch(256)
        + ring_scratch()
        + ring_scratch(),
        compiler_params=params(1, 60),
        name="backward",
    )(*operands)


def pack_inputs(weights, d):
    ag, ash, qw, qb, kw, vw, vb, ow, ob, fg, fs, uw, ub, dw, db = weights
    columns = jnp.pad(jnp.stack([ag, ash, ob, fg, fs, db], axis=2), ((0, 0), (0, 0), (0, 58)))
    heads = jnp.concatenate([qb, vb, ub], axis=1)
    here = (jnp.arange(16) == d)[None, None, :, None]
    heads = jnp.where(here, heads[:, :, None, :], jnp.zeros((), BF)).reshape(2, 12, 64)
    heads = jnp.pad(heads, ((0, 0), (0, 52), (0, 0)))
    vectors = jnp.concatenate([columns, heads], axis=2).reshape(2, 4, 16, 128)
    split = (2, 4, 16)
    return (
        qw.reshape(*split, 128), kw.reshape(*split, 128), vw.reshape(*split, 128), uw.reshape(*split, 512), ow, dw, vectors,
    )


def unpack_grads(mlp, att, small, d):
    mlp = jnp.stack(mlp).reshape(2, 64, MLP)
    att = jnp.stack(att).reshape(2, 64, 512)
    small = jnp.transpose(small.reshape(64, 2, 128), (1, 0, 2))
    columns = [small[:, :, k] for k in range(6)]
    mine = lax.dynamic_slice_in_dim(small[:, 0:12, 64:128], d * 4, 4, axis=2)

    def turn(rows):
        return jnp.transpose(rows, (0, 2, 1))

    return (
        columns[0], columns[1], att[:, :, 0:128], mine[:, 0:2], att[:, :, 128:256], att[:, :, 256:384], mine[:, 2:4],
        turn(att[:, :, 384:512]), columns[2], columns[3], columns[4], mlp[:, :, 0:512], mine[:, 4:12],
        turn(mlp[:, :, 512:1024]), columns[5],
    )


def local(images, cotangent, counts, *weights):
    d = lax.axis_index("dp")
    alive = (jnp.arange(2) < counts[0])[:, None, None]
    pad = ((0, 0), (0, ROWS - SEQ), (0, 0))
    images = jnp.pad(images, pad)
    cotangent = jnp.pad(jnp.where(alive, cotangent, jnp.zeros((), BF)), pad)
    *saved, vec, cot, act = forward(images, cotangent, *pack_inputs(weights, d))
    gin, mlp0, mlp1, att0, att1, small = backward(cot, vec, *saved)
    return (
        jnp.where(alive, act[:, :SEQ], jnp.zeros((), BF)),
        gin[:, :SEQ],
        *unpack_grads((mlp0, mlp1), (att0, att1), small, d),
    )


def solution(mesh):
    row = P(None, "dp")
    columns = P(None, "dp", "tensor")
    heads = P(None, "tensor", "dp")
    weights = (
        row, row, columns, heads, columns, columns, heads, heads, row, row, row, columns, heads, heads, row,
    )
    stream = P("dp", None, "tensor")
    return jax.shard_map(
        local,
        mesh=mesh,
        in_specs=(stream, stream, P("dp"), *weights),
        out_specs=(stream, stream, *weights),
        check_vma=False,
    )
```

```python
import functools
import math

import jax
import jax.numpy as jnp
from jax import lax
from jax.experimental import pallas as pl
from jax.experimental.pallas import tpu as pltpu
from jax.sharding import PartitionSpec as P

HD = 64
EPSILON = 1e-06
SCALE = 1.0 / math.sqrt(HD)
BF = jnp.bfloat16
F32 = jnp.float32

SEQ = 577
D = 1024
ROWS = 592
KEYS = 640
ATT = 640
MLP = 1024
CHUNKS = ((0, 128), (128, 128), (256, 128), (384, 128), (512, 80))
NQ = len(CHUNKS)

TN = (((1,), (1,)), ((), ()))
NT = (((0,), (0,)), ((), ()))


def dot(a, b, dims=(((1,), (0,)), ((), ()))):
    return lax.dot_general(a, b, dims, preferred_element_type=F32)


def block(k, width=256):
    return pl.ds(pl.multiple_of(k * width, width), width)


def greet(devices):
    barrier = pltpu.get_barrier_semaphore()
    for device in devices:
        pl.semaphore_signal(barrier, inc=1, device_id=device, device_id_type=pl.DeviceIdType.MESH)
    return lambda: pl.semaphore_wait(barrier, len(devices))


class Ring:
    def __init__(self, send, near, far, full, send_sem, recv_sem):
        t = lax.axis_index("tensor")
        y = t // 2
        self.y = y
        self.yl, self.yr, self.yo = lax.rem(y + 3, 4), lax.rem(y + 1, 4), lax.rem(y + 2, 4)
        self.left = {"tensor": lax.rem(t + 6, 8)}
        self.right = {"tensor": lax.rem(t + 2, 8)}
        self.send, self.near, self.far, self.full = send, near, far, full
        self.send_sem, self.recv_sem = send_sem, recv_sem
        self.flying = {}

    def go(self, stage, q, to_left, to_right):
        copies = []
        for side, (src, dst) in enumerate((to_left, to_right)):
            copy = pltpu.make_async_remote_copy(
                src_ref=src,
                dst_ref=dst,
                send_sem=self.send_sem.at[stage, q, side],
                recv_sem=self.recv_sem.at[stage, q, side],
                device_id=self.left if side == 0 else self.right,
                device_id_type=pl.DeviceIdType.MESH,
            )
            copy.start()
            copies.append(copy)
        self.flying[stage, q] = copies

    def arrive(self, stage, q):
        for copy in self.flying[stage, q]:
            copy.wait_recv()

    def parts(self, q):
        r0, nr = CHUNKS[q]
        top = 64 if nr == 128 else 48
        return pl.ds(r0, nr), pl.ds(r0, top), pl.ds(r0 + top, nr - top)

    def stage0(self, q):
        rows, a, b = self.parts(q)
        c = block(self.yo)
        self.go(0, q, (self.send.at[a, c], self.near.at[0, a, :]), (self.send.at[b, c], self.near.at[1, b, :]))

    def stage1(self, q):
        rows, a, b = self.parts(q)
        self.arrive(0, q)
        cl, cr = block(self.yl), block(self.yr)
        self.send[a, cl] = (self.send[a, cl].astype(F32) + self.near[0, a, :].astype(F32)).astype(BF)
        self.send[b, cr] = (self.send[b, cr].astype(F32) + self.near[1, b, :].astype(F32)).astype(BF)
        self.go(
            1, q, (self.send.at[rows, cl], self.far.at[0, rows, :]), (self.send.at[rows, cr], self.far.at[1, rows, :])
        )

    def stage2(self, q):
        rows, a, b = self.parts(q)
        self.arrive(1, q)
        c = block(self.y)
        total = self.send[rows, c].astype(F32) + self.far[0, rows, :].astype(F32) + self.far[1, rows, :].astype(F32)
        self.full[rows, c] = total.astype(BF)
        self.go(2, q, (self.full.at[rows, c], self.full.at[rows, c]), (self.full.at[rows, c], self.full.at[rows, c]))

    def stage3(self, q):
        rows, a, b = self.parts(q)
        self.arrive(2, q)
        cl, cr = block(self.yl), block(self.yr)
        self.go(3, q, (self.full.at[a, cr], self.full.at[a, cr]), (self.full.at[b, cl], self.full.at[b, cl]))

    def stage4(self, q):
        self.arrive(3, q)

    def drain(self):
        for copies in self.flying.values():
            for copy in copies:
                copy.wait_send()
        self.flying = {}


def ring_scratch():
    return [
        pltpu.VMEM((ROWS, D), BF),
        pltpu.VMEM((2, ROWS, 256), BF),
        pltpu.VMEM((2, ROWS, 256), BF),
        pltpu.VMEM((ROWS, D), BF),
        pltpu.SemaphoreType.DMA((4, NQ, 2)),
        pltpu.SemaphoreType.DMA((4, NQ, 2)),
    ]


def standardize(x):
    average = jnp.mean(x, axis=1, keepdims=True)
    centered = x - average
    variance = jnp.mean(centered * centered, axis=1, keepdims=True)
    rstd = lax.rsqrt(variance + EPSILON)
    return centered * rstd, rstd


def half_masks():
    lane = lax.broadcasted_iota(jnp.int32, (1, 128), 1)
    first = (lane < 64).astype(F32)
    return first.astype(BF), (1.0 - first).astype(BF)


def key_rows():
    return lax.broadcasted_iota(jnp.int32, (KEYS, 128), 0) < SEQ


def flip(rows):
    return jnp.transpose(rows.astype(F32), (1, 0))


def pair(first, second):
    top = lax.broadcasted_iota(jnp.int32, first.shape, 0) < 64
    return jnp.where(top, first, second)


def torus():
    d, t = lax.axis_index("dp"), lax.axis_index("tensor")
    x, z = d // 4, lax.rem(d, 4)
    return d, t, x, z, lax.rem(t, 2)


def dp_device(x, z):
    return {"dp": lax.rem(x + 4, 4) * 4 + lax.rem(z + 4, 4)}


class Exchange:
    def __init__(self, send_sem, recv_sem):
        self.send_sem, self.recv_sem, self.count, self.started = send_sem, recv_sem, 0, []

    def go(self, src, dst, device):
        copy = pltpu.make_async_remote_copy(
            src_ref=src,
            dst_ref=dst,
            send_sem=self.send_sem.at[self.count],
            recv_sem=self.recv_sem.at[self.count],
            device_id=device,
            device_id_type=pl.DeviceIdType.MESH,
        )
        copy.start()
        self.count += 1
        self.started.append(copy)
        return copy

    def drain(self):
        for copy in self.started:
            copy.wait_send()


def sides(half, x, z):
    along_x = [dp_device(x + j, z) for j in (1, 2, 3)]
    along_z = [dp_device(x, z + j) for j in (1, 2, 3)]
    return (x, z, along_x, along_z) if half == 0 else (z, x, along_z, along_x)


def place(half, a, b):
    return (a, b) if half == 0 else (b, a)


def wrap(k):
    return lax.rem(k + 4, 4)


ALL = pl.ds(0, 4)

class Background:
    def __init__(self):
        self.steps = []

    def add(self, *steps):
        self.steps.extend(steps)

    def run(self, count=1):
        for _ in range(min(count, len(self.steps))):
            self.steps.pop(0)()

    def until(self, step):
        while step in self.steps:
            self.steps.pop(0)()


def pipeline(stages, background, fillers=None):
    fillers = fillers or {}
    for step in range(NQ + len(stages) - 1):
        for k, stage in enumerate(stages):
            if 0 <= step - k < NQ:
                stage(step - k)
            if k == 0:
                for filler in fillers.get(step, ()):
                    filler()
                background.run()


class Gather:
    def __init__(self, ex, w):
        self.ex, self.w = ex, w
        d, t, self.x, self.z, self.c = torus()
        self.partner = {"tensor": t + 1 - 2 * self.c}
        self.state = [None, None]
        self.hand = []

    def at(self, h, a, b, quarters):
        return self.w.at[(self.c, *place(h, a, b), quarters)]

    def push(self, ref, device):
        return self.ex.go(ref, ref, device)

    def one(self):
        for h in range(2):
            a, b, along_a, along_b = sides(h, self.x, self.z)
            own = self.at(h, a, b, pl.ds(2 * h, 2))
            self.state[h] = [self.push(own, device) for device in along_a]

    def two(self):
        for h in range(2):
            a, b, along_a, along_b = sides(h, self.x, self.z)
            for copy in self.state[h]:
                copy.wait_recv()
            row = self.at(h, ALL, b, pl.ds(2 * h, 2))
            self.state[h] = [self.push(row, device) for device in along_b]
            self.hand.append(self.push(row, self.partner))

    def three(self):
        for j in (0, 2, 1):
            for h in range(2):
                a, b, along_a, along_b = sides(h, self.x, self.z)
                self.state[h][j].wait_recv()
                self.hand.append(self.push(self.at(h, ALL, wrap(b - 1 - j), pl.ds(2 * h, 2)), self.partner))

    def four(self):
        for copy in self.hand:
            copy.wait_recv()


class Scatter:
    def __init__(self, ex, r, out, got, second, first):
        self.ex, self.r, self.out, self.got = ex, r, out, got
        self.second, self.first = second, first
        d, t, self.x, self.z, self.c = torus()
        self.partner = {"tensor": t + 1 - 2 * self.c}
        self.state = [None, None]
        self.sent = []

    def at(self, h, a, b, quarters):
        return self.r.at[(self.c, *place(h, a, b), quarters)]

    def push(self, src, dst, device):
        copy = self.ex.go(src, dst, device)
        self.sent.append(copy)
        return copy

    def landed(self, h):
        for copy in self.state[h]:
            copy.wait_recv()

    def zero(self):
        for h in range(2):
            both = pl.ds(2 * h, 2)
            self.state[h] = [
                self.push(self.r.at[1 - self.c, :, :, both], self.got.at[:, :, both], self.partner)
            ]

    def one(self):
        for h in range(2):
            a, b, along_a, along_b = sides(h, self.x, self.z)
            both = pl.ds(2 * h, 2)
            self.landed(h)

            def merge(i, _):
                ref = self.r.at[self.c, i, :, both]
                ref[...] = add(ref, self.got.at[i, :, both]).astype(BF)
                return 0

            lax.fori_loop(0, 4, merge, 0)
            self.state[h] = [
                self.push(self.at(h, ALL, wrap(b + 1 + j), both), self.second.at[h, j], along_b[j]) for j in range(3)
            ]

    def two(self):
        for h in range(2):
            a, b, along_a, along_b = sides(h, self.x, self.z)
            both = pl.ds(2 * h, 2)
            self.landed(h)
            for i in range(4):
                ref = self.at(h, i, b, both)
                ref[...] = add(ref, *(self.second.at[h, j, i] for j in range(3))).astype(BF)
            self.state[h] = [
                self.push(self.at(h, wrap(a + 1 + j), b, both), self.first.at[h, j], along_a[j]) for j in range(3)
            ]

    def three(self):
        for h in range(2):
            a, b, along_a, along_b = sides(h, self.x, self.z)
            both = pl.ds(2 * h, 2)
            self.landed(h)
            self.out[both] = add(self.at(h, a, b, both), *(self.first.at[h, j] for j in range(3)))
        for copy in self.sent:
            copy.wait_send()


def add(*terms):
    total = terms[0][...].astype(F32)
    for term in terms[1:]:
        total = total + term[...].astype(F32)
    return total


def scatter_scratch(width):
    return [
        pltpu.VMEM((2, 4, 4, 4, 16, width), BF),
        pltpu.VMEM((4, 4, 4, 16, width), BF),
        pltpu.VMEM((2, 3, 4, 2, 16, width), BF),
        pltpu.VMEM((2, 3, 2, 16, width), BF),
    ]


def mat(ref, c, lo, hi):
    return ref[c, :, :, :, :, lo:hi].reshape(D, hi - lo)


def put(ref, c, lo, hi, value):
    ref[c, :, :, :, :, lo:hi] = value.astype(BF).reshape(4, 4, 4, 16, hi - lo)


class Local:
    def __init__(self, sem):
        self.sem, self.count = sem, 0

    def go(self, src, dst):
        copy = pltpu.make_async_copy(src, dst, self.sem.at[self.count])
        copy.start()
        self.count += 1
        return copy


def column_sum(value):
    return jnp.sum(value.astype(F32), axis=0, keepdims=True)


def low_lanes(shape):
    return lax.broadcasted_iota(jnp.int32, shape, 1) < 64


def unpack_vectors(wa, vec):
    vec[0:8, :] = flip(mat(wa, 0, 512, ATT))[0:8]
    for c in range(2):
        heads = jnp.sum(mat(wa, c, 512, ATT).reshape(16, 64, 128)[:, 0:16].astype(F32), axis=0)
        rolled = pltpu.roll(heads, 64, 1)

        def both(k):
            return jnp.where(low_lanes((1, 128)), rolled[k : k + 1], heads[k + 1 : k + 2])

        vec[6:7, c * 128 : c * 128 + 128] = both(0)
        vec[6:7, 256 + c * 128 : 384 + c * 128] = both(2)
        for m in range(4):
            vec[7:8, c * 512 + 128 * m : c * 512 + 128 * m + 128] = both(4 + 2 * m)


def pack_vectors(vg, rv, lane):
    padded = jnp.concatenate([vg[...], jnp.zeros((120, D), F32)], axis=0)
    kind = lax.broadcasted_iota(jnp.int32, (128, D), 0)
    columns = flip(jnp.where(kind < 6, padded, 0.0)).reshape(16, 64, 128)
    row = lax.broadcasted_iota(jnp.int32, (64, 128), 0)
    for c in range(2):
        pieces = [vg[6:7, c * 128 : c * 128 + 128], vg[6:7, 256 + c * 128 : 384 + c * 128]]
        pieces += [vg[7:8, c * 512 + 128 * m : c * 512 + 128 * m + 128] for m in range(4)]
        heads = jnp.zeros((64, 128), F32)
        for k, piece in enumerate(pieces):
            rolled = pltpu.roll(jnp.broadcast_to(piece, (8, 128)), 64, 1)[0:1]
            heads = jnp.where(row == 2 * k, rolled, heads)
            heads = jnp.where(row == 2 * k + 1, piece, heads)
        heads = jnp.where(low_lanes((64, 128)), 0.0, heads)
        put(rv, c, lane, lane + 128, (columns + heads[None]).reshape(D, 128))


def forward_kernel(
    img_ref, cot_ref, qw_ref, kw_ref, vw_ref, uw_ref, ow_ref, dw_ref, vp_ref,
    *refs,
):
    refs = list(refs)
    saved = [[refs.pop(0) for _ in range(9)] for _ in range(2)]
    wa_out = [refs.pop(0) for _ in range(2)]
    wm_out = [refs.pop(0) for _ in range(2)]
    vec_ref, xc_ref, act_ref = [refs.pop(0) for _ in range(3)]
    kept = [[refs.pop(0) for _ in range(9)] for _ in range(2)]
    wa = [refs.pop(0) for _ in range(2)]
    wm = [refs.pop(0) for _ in range(2)]
    xg_ref, vt_ref, give_ref, local_sem, send_sem, recv_sem = [refs.pop(0) for _ in range(6)]
    one, two = Ring(*refs[:6]), Ring(*refs[6:12])
    d, t, x, z, c_here = torus()
    y = t // 2
    partner = {"tensor": t + 1 - 2 * c_here}
    others = [{"tensor": lax.rem(t + j, 8)} for j in range(1, 8)]
    _, _, along_x, along_z = sides(0, x, z)
    entered = greet(along_x + along_z + others)
    local, ex, background = Local(local_sem), Exchange(send_sem, recv_sem), Background()
    groups = [Gather(ex, ref) for ref in (wa[0], wm[0], wa[1], wm[1])]
    m0, a1, m1 = groups[1:]
    own = []
    for layer in range(2):
        slot = wa[layer].at[c_here, x, z]
        own.append(
            [local.go(src.at[layer], slot.at[:, :, pl.ds(128 * k, 128)]) for k, src in enumerate((qw_ref, kw_ref, vw_ref))]
        )
        own.append([local.go(uw_ref.at[layer], wm[layer].at[c_here, x, z, :, :, pl.ds(0, 512)])])
    mine = local.go(img_ref.at[c_here], xg_ref.at[t])
    theirs = local.go(cot_ref.at[c_here], xc_ref.at[t])

    def build_att(layer):
        wa[layer][c_here, x, z, :, :, 384:512] = flip(ow_ref[layer]).astype(BF).reshape(4, 16, 128)
        wa[layer][c_here, x, z, :, :, 512:ATT] = vp_ref[layer]

    def build_mlp(layer):
        wm[layer][c_here, x, z, :, :, 512:MLP] = flip(dw_ref[layer]).astype(BF).reshape(4, 16, 512)

    def start(k):
        def run():
            for copy in own[k]:
                copy.wait()
            groups[k].one()

        return run

    def exchange(src, dst):
        copies = []
        for j in range(1, 8):
            target = lax.rem(t + j, 8)
            copies.append(ex.go(src.at[lax.rem(target, 2)], dst.at[t], others[j - 1]))
        return copies

    build_att(0)
    entered()
    start(0)()
    images = exchange(img_ref, xg_ref)
    build_mlp(0)
    build_att(1)
    build_mlp(1)
    groups[0].two()
    start(1)()
    mine.wait()
    for copy in images:
        copy.wait_recv()
    cotangents = exchange(cot_ref, xc_ref)
    for r0, nr in CHUNKS:
        rows = pl.ds(r0, nr)
        for j in range(8):
            kept[0][0][rows, 128 * j : 128 * j + 128] = xg_ref[j, rows, :].astype(F32)
    groups[0].three()
    m0.two()
    groups[0].four()
    masks = half_masks()
    valid = key_rows()

    def rest():
        pass

    background.add(m0.three, m0.four, start(2), a1.two, start(3), a1.three, a1.four, m1.two, rest, m1.three, rest, m1.four)
    for layer in range(2):
        kept[layer][2][:, ROWS:KEYS, :] = jnp.zeros((2, KEYS - ROWS, 384), BF)

    def project(layer, q):
        r0, nr = CHUNKS[q]
        rows = pl.ds(r0, nr)
        x_ref, n1_ref, qkv_ref = kept[layer][:3]
        vec = vec_ref.at[layer]
        xhat, _ = standardize(x_ref[rows, :])
        n1 = (xhat * vec[0:1, :] + vec[1:2, :]).astype(BF)
        n1_ref[rows, :] = n1
        for c in range(2):
            out = dot(n1, mat(wa[layer], c, 0, 384))
            qkv_ref[c, rows, 0:128] = (out[:, 0:128] + vec[6:7, c * 128 : c * 128 + 128]).astype(BF)
            qkv_ref[c, rows, 128:256] = out[:, 128:256].astype(BF)
            qkv_ref[c, rows, 256:384] = (out[:, 256:384] + vec[6:7, 256 + c * 128 : 384 + c * 128]).astype(BF)

    unpack_vectors(wa[0], vec_ref.at[0])
    for q in range(NQ):
        project(0, q)

    def layer_forward(layer):
        x_ref, n1_ref, qkv_ref, lse_ref, o_ref, mid_ref, n2_ref, slope_ref, a_ref = kept[layer]
        x_out, n1_out, qkv_out, lse_out, o_out, mid_out, n2_out, slope_out, a_out = saved[layer]
        vec = vec_ref.at[layer]
        waits = [
            local.go(src, dst)
            for src, dst in ((x_ref, x_out), (n1_ref, n1_out), (wa[layer], wa_out[layer]), (qkv_ref, qkv_out))
        ]
        for c in range(2):
            vt_ref[c] = flip(qkv_ref[c, :, 256:384]).astype(BF)

        def attend(q):
            r0, nr = CHUNKS[q]
            total = None
            for c in range(2):
                queries, keys = qkv_ref[c, r0 : r0 + 128, 0:128], qkv_ref[c, :, 128:256]
                halves = []
                for h in range(2):
                    s = dot(keys, queries * masks[h], TN) * SCALE
                    s = jnp.where(valid, s, -1e30)
                    top = jnp.max(s, axis=0, keepdims=True)
                    e = jnp.exp(s - top)
                    norm = jnp.sum(e, axis=0, keepdims=True)
                    lse_ref[2 * c + h : 2 * c + h + 1, r0 : r0 + 128] = top + jnp.log(norm)
                    p = (e * (1.0 / norm)).astype(BF)
                    halves.append(dot(vt_ref[c], p))
                mixed = flip(pair(*halves))[0:nr].astype(BF)
                o_ref[c, r0 : r0 + nr, :] = mixed
                part = dot(mixed, mat(wa[layer], c, 384, 512), TN)
                total = part if total is None else total + part
            one.send[r0 : r0 + nr, :] = total.astype(BF)
            one.stage0(q)
            if q == NQ - 1:
                waits.extend([local.go(lse_ref, lse_out), local.go(o_ref, o_out)])

        def feed(q):
            r0, nr = CHUNKS[q]
            rows = pl.ds(r0, nr)
            if q == 0:
                background.until(groups[2 * layer + 1].four)
                waits.append(local.go(wm[layer], wm_out[layer]))
            one.stage4(q)
            mid = x_ref[rows, :] + one.full[rows, :].astype(F32) + vec[2:3, :]
            mid_ref[rows, :] = mid
            xhat, _ = standardize(mid)
            n2 = (xhat * vec[3:4, :] + vec[4:5, :]).astype(BF)
            n2_ref[rows, :] = n2
            total = None
            for c in range(2):
                u = dot(n2, mat(wm[layer], c, 0, 512)) + vec[7:8, c * 512 : c * 512 + 512]
                phi = 0.5 * (1.0 + lax.erf(u * (1.0 / math.sqrt(2.0))))
                slope = phi + u * (jnp.exp(-0.5 * u * u) * (1.0 / math.sqrt(2.0 * math.pi)))
                slope_ref[c, rows, :] = slope.astype(BF)
                a = (u * phi).astype(BF)
                a_ref[c, rows, :] = a
                part = dot(a, mat(wm[layer], c, 512, MLP), TN)
                total = part if total is None else total + part
            two.send[rows, :] = total.astype(BF)
            two.stage0(q)
            if q == NQ - 1:
                waits.extend(
                    local.go(src, dst)
                    for src, dst in ((mid_ref, mid_out), (n2_ref, n2_out), (slope_ref, slope_out), (a_ref, a_out))
                )

        def finish(q):
            r0, nr = CHUNKS[q]
            rows = pl.ds(r0, nr)
            two.stage4(q)
            kept[1][0][rows, :] = mid_ref[rows, :] + two.full[rows, :].astype(F32) + vec[5:6, :]
            if q == 0:
                background.until(a1.four)
                unpack_vectors(wa[1], vec_ref.at[1])
            project(1, q)

        swaps = []

        def last(q):
            r0, nr = CHUNKS[q]
            rows = pl.ds(r0, nr)
            two.arrive(1, q)
            c = block(y)
            total = two.send[rows, c].astype(F32) + two.far[0, rows, :].astype(F32) + two.far[1, rows, :].astype(F32)
            total = total + mid_ref[rows, c] + vec[5:6, c]
            left, right = total[:, 0:128].astype(BF), total[:, 128:256].astype(BF)
            act_ref[c_here, rows, :] = jnp.where(c_here == 0, left, right)
            give_ref[rows, :] = jnp.where(c_here == 0, right, left)
            swaps.append(ex.go(give_ref.at[rows], act_ref.at[c_here, rows], partner))

        stages = (attend, one.stage1, one.stage2, one.stage3, feed, two.stage1)
        stages += (two.stage2, two.stage3, finish) if layer == 0 else (last,)
        pipeline(stages, background)
        one.drain()
        two.drain()
        return waits, swaps

    waits0, _ = layer_forward(0)
    waits1, swaps = layer_forward(1)
    theirs.wait()
    for copy in cotangents + swaps:
        copy.wait_recv()
    for copy in waits0 + waits1:
        copy.wait()
    ex.drain()


def backward_kernel(
    cot_ref, vec_ref, *refs,
):
    refs = list(refs)
    saved = [[refs.pop(0) for _ in range(9)] for _ in range(2)]
    wa_in = [refs.pop(0) for _ in range(2)]
    wm_in = [refs.pop(0) for _ in range(2)]
    gin_ref, mlp0_ref, mlp1_ref, att0_ref, att1_ref, small_ref = [refs.pop(0) for _ in range(6)]
    x_ref, n1_ref, qkv_ref, lse_ref, o_ref, mid_ref, n2_ref, slope_ref, a_ref = [refs.pop(0) for _ in range(9)]
    wa, wm = refs.pop(0), refs.pop(0)
    xg_ref, g_ref, gm_ref, go_ref, hid_ref, dout_ref, kt_ref, dqkv_ref, dk_ref, dv_ref, gmid_ref, vg_ref, give_ref = [
        refs.pop(0) for _ in range(13)
    ]
    local_sem, send_sem, recv_sem = [refs.pop(0) for _ in range(3)]
    mlp, att, small = [[refs.pop(0) for _ in range(4)] for _ in range(3)]
    one, two = Ring(*refs[:6]), Ring(*refs[6:12])
    d, t, x, z, c_here = torus()
    y = t // 2
    partner = {"tensor": t + 1 - 2 * c_here}
    _, _, along_x, along_z = sides(0, x, z)
    entered = greet(along_x + along_z + [one.left, one.right, partner])
    local, ex, background = Local(local_sem), Exchange(send_sem, recv_sem), Background()

    def load_mlp(layer):
        _, _, _, _, _, mid, n2, slope, a = saved[layer]
        pairs = ((wm_in[layer], wm), (slope, slope_ref), (a, a_ref), (mid, mid_ref), (n2, n2_ref))
        return [local.go(src, dst) for src, dst in pairs]

    def load_att(layer):
        stream, n1, qkv, lse, o = saved[layer][:5]
        pairs = ((wa_in[layer], wa), (qkv, qkv_ref), (lse, lse_ref), (o, o_ref), (n1, n1_ref))
        return [local.go(src, dst) for src, dst in pairs]

    cot = local.go(cot_ref, xg_ref)
    loads = {1: load_mlp(1)}
    att_loads = {1: load_att(1)}
    x_loads = {1: local.go(saved[1][0], x_ref)}
    masks = half_masks()
    valid = key_rows()
    dout_ref[:, ROWS:KEYS, :] = jnp.zeros((2, KEYS - ROWS, 128), BF)
    cot.wait()
    for r0, nr in CHUNKS:
        rows = pl.ds(r0, nr)
        for j in range(8):
            g_ref[rows, 128 * j : 128 * j + 128] = xg_ref[j, rows, :].astype(F32)
    entered()
    swaps = []

    vg_ref[...] = jnp.zeros((2, 8, D), F32)

    def layer_steps(layer):
        vec, vg = vec_ref.at[layer], vg_ref.at[layer]
        mlp_scatter = Scatter(ex, mlp[0], (mlp0_ref, mlp1_ref)[layer], *mlp[1:])
        att_scatter = Scatter(ex, att[0], (att0_ref, att1_ref)[layer], *att[1:])

        def add_vector(row, value, lane=0):
            width = value.shape[1]
            vg[row : row + 1, lane : lane + width] = vg[row : row + 1, lane : lane + width] + value

        def hidden(q):
            r0, nr = CHUNKS[q]
            rows = pl.ds(r0, nr)
            if q == 0:
                for copy in loads[layer]:
                    copy.wait()
            gm = g_ref[rows, :].astype(BF)
            gm_ref[rows, :] = gm
            add_vector(5, column_sum(gm))
            total = None
            for c in range(2):
                da = dot(gm, mat(wm, c, 512, MLP))
                du = (da * slope_ref[c, rows, :].astype(F32)).astype(BF)
                hid_ref[c, rows, :] = du
                add_vector(7, column_sum(du), c * 512)
                part = dot(du, mat(wm, c, 0, 512), TN)
                total = part if total is None else total + part
            one.send[rows, :] = total.astype(BF)
            one.stage0(q)

        def norm_back(ring, q, stream, grad, gain_row, shift_row):
            r0, nr = CHUNKS[q]
            rows = pl.ds(r0, nr)
            ring.stage4(q)
            dn = ring.full[rows, :].astype(F32)
            xhat, rstd = standardize(stream[rows, :])
            add_vector(gain_row, column_sum(dn * xhat))
            add_vector(shift_row, column_sum(dn))
            e = dn * vec[gain_row : gain_row + 1, :]
            first = jnp.mean(e, axis=1, keepdims=True)
            second = jnp.mean(e * xhat, axis=1, keepdims=True)
            return grad[rows, :] + rstd * (e - first - xhat * second)

        def attend(q):
            r0, nr = CHUNKS[q]
            rows = pl.ds(r0, nr)
            if q == 0:
                for copy in att_loads[layer]:
                    copy.wait()
                for c in range(2):
                    kt_ref[c] = flip(qkv_ref[c, :, 128:256]).astype(BF)
                dk_ref[...] = jnp.zeros(dk_ref.shape, F32)
                dv_ref[...] = jnp.zeros(dv_ref.shape, F32)
            mid_grad = norm_back(one, q, mid_ref, g_ref, 3, 4)
            gmid_ref[rows, :] = mid_grad
            go = mid_grad.astype(BF)
            go_ref[rows, :] = go
            add_vector(2, column_sum(go))
            for c in range(2):
                dout_ref[c, rows, :] = dot(go, mat(wa, c, 384, 512)).astype(BF)
                queries = qkv_ref[c, r0 : r0 + 128, 0:128]
                keys, values = qkv_ref[c, :, 128:256], qkv_ref[c, :, 256:384]
                dout = dout_ref[c, r0 : r0 + 128, :]
                halves = []
                for h in range(2):
                    qh, doh = queries * masks[h], dout * masks[h]
                    s = dot(keys, qh, TN) * SCALE
                    p = jnp.where(valid, jnp.exp(s - lse_ref[2 * c + h : 2 * c + h + 1, r0 : r0 + 128]), 0.0)
                    dp = dot(values, doh, TN)
                    delta = jnp.sum(dp * p, axis=0, keepdims=True)
                    ds = (p * (dp - delta)).astype(BF)
                    dv_ref[c] = dv_ref[c] + dot(p.astype(BF), doh)
                    dk_ref[c] = dk_ref[c] + dot(ds, qh)
                    halves.append(dot(kt_ref[c], ds))
                dq = (flip(pair(*halves)) * SCALE)[0:nr].astype(BF)
                dqkv_ref[c, rows, 0:128] = dq

        def down_grad(c):
            def run():
                put(mlp[0], c, 512, MLP, dot(gm_ref[...], a_ref[c], NT))

            return run

        def up_grad(c):
            def run():
                put(mlp[0], c, 0, 512, dot(n2_ref[...], hid_ref[c], NT))

            return run

        def out_grad():
            for c in range(2):
                put(att[0], c, 384, 512, dot(go_ref[...], o_ref[c], NT))

        def qkv_grad(c):
            def run():
                put(att[0], c, 0, 384, dot(n1_ref[...], dqkv_ref[c], NT))

            return run

        def settle():
            for c in range(2):
                dqkv_ref[c, :, 128:256] = (dk_ref[c, 0:ROWS] * SCALE).astype(BF)
                dqkv_ref[c, :, 256:384] = dv_ref[c, 0:ROWS].astype(BF)

        def project(q):
            r0, nr = CHUNKS[q]
            rows = pl.ds(r0, nr)
            total = None
            for c in range(2):
                grads = dqkv_ref[c, rows, :]
                add_vector(6, column_sum(grads[:, 0:128]), c * 128)
                add_vector(6, column_sum(grads[:, 256:384]), 256 + c * 128)
                part = dot(grads, mat(wa, c, 0, 384), TN)
                total = part if total is None else total + part
            two.send[rows, :] = total.astype(BF)
            two.stage0(q)

        def finish(q):
            r0, nr = CHUNKS[q]
            rows = pl.ds(r0, nr)
            if q == 0:
                x_loads[layer].wait()
            g_ref[rows, :] = norm_back(two, q, x_ref, gmid_ref, 0, 1)
            if layer == 0:
                left, right = g_ref[rows, block(2 * y, 128)], g_ref[rows, block(2 * y + 1, 128)]
                gin_ref[c_here, rows, :] = jnp.where(c_here == 0, left, right)
                give_ref[rows, :] = jnp.where(c_here == 0, right, left)
                swaps.append(ex.go(give_ref.at[rows], gin_ref.at[c_here, rows], partner))

        def pack():
            pack_vectors(vg, small[0], 128 * layer)

        return (
            hidden, attend, project, finish, settle, pack, mlp_scatter, att_scatter,
            (down_grad(0), down_grad(1)), (up_grad(0), up_grad(1)), (out_grad, qkv_grad(0), qkv_grad(1)),
        )

    def rest():
        pass

    hidden1, attend1, project1, finish1, settle1, pack1, m1, a1, down1, up1, grads1 = layer_steps(1)
    hidden0, attend0, project0, finish0, settle0, pack0, m0, a0, down0, up0, grads0 = layer_steps(0)
    pipeline(
        (hidden1, one.stage1, one.stage2, one.stage3, attend1),
        background,
        {5: (up1[0], down1[0]), 6: (up1[1], down1[1], m1.zero)},
    )
    one.drain()
    loads[0] = load_mlp(0)
    settle1()

    def turn(q):
        finish1(q)
        hidden0(q)

    def reload():
        att_loads[0] = load_att(0)

    def reload_x():
        x_loads[0] = local.go(saved[0][0], x_ref)

    def begin(steps):
        return lambda: background.add(*steps)

    background.add(m1.one, rest, m1.two, rest, a1.zero, m1.three, a1.one, rest, a1.two, rest, a1.three)
    pipeline(
        (project1, two.stage1, two.stage2, two.stage3, turn, one.stage1, one.stage2, one.stage3, attend0),
        background,
        {
            1: grads1[:1],
            2: grads1[1:2],
            3: grads1[2:],
            5: (reload,),
            9: (reload_x, lambda: background.until(m1.three), up0[0], up0[1]),
            10: (down0[0], down0[1], lambda: background.until(a1.three), m0.zero),
        },
    )
    one.drain()
    two.drain()
    pack1()
    settle0()
    background.add(m0.one, rest, m0.two, a0.zero, m0.three, a0.one, a0.two)
    pipeline(
        (project0, two.stage1, two.stage2, two.stage3, finish0),
        background,
        {1: grads0[:1], 2: grads0[1:2], 3: grads0[2:]},
    )
    pack0()
    last = Scatter(ex, small[0], small_ref, *small[1:])
    last.zero()
    background.run(100)
    last.one()
    a0.three()
    last.two()
    last.three()
    two.drain()
    for copy in swaps:
        copy.wait_recv()
        copy.wait_send()


VM = pl.BlockSpec(memory_space=pltpu.VMEM)
HBM = pl.BlockSpec(memory_space=pl.ANY)


def params(collective_id, megabytes):
    return pltpu.CompilerParams(
        collective_id=collective_id, has_side_effects=True, vmem_limit_bytes=megabytes * 1024 * 1024
    )


def shape(dims, dtype):
    return jax.ShapeDtypeStruct(dims, dtype)


LAYER = (
    ((ROWS, D), F32),
    ((ROWS, D), BF),
    ((2, KEYS, 384), BF),
    ((8, KEYS), F32),
    ((2, ROWS, 128), BF),
    ((ROWS, D), F32),
    ((ROWS, D), BF),
    ((2, ROWS, 512), BF),
    ((2, ROWS, 512), BF),
)
WA = ((2, 4, 4, 4, 16, ATT), BF)
WM = ((2, 4, 4, 4, 16, MLP), BF)
DMA = pltpu.SemaphoreType.DMA


def vmem(*kinds):
    return [pltpu.VMEM(*kind) for kind in kinds]


def forward(*operands):
    outs = [shape(*kind) for kind in LAYER * 2 + (WA, WA, WM, WM)]
    outs += [shape((2, 8, D), F32), shape((8, ROWS, 128), BF), shape((2, ROWS, 128), BF)]
    return pl.pallas_call(
        forward_kernel,
        out_shape=tuple(outs),
        in_specs=[HBM] * 6 + [VM] * 3,
        out_specs=tuple([HBM] * 22 + [VM, HBM, VM]),
        scratch_shapes=vmem(*LAYER, *LAYER, WA, WA, WM, WM, ((8, ROWS, 128), BF), ((2, 128, KEYS), BF), ((ROWS, 128), BF))
        + [DMA((40,)), DMA((128,)), DMA((128,))]
        + ring_scratch()
        + ring_scratch(),
        compiler_params=params(0, 58),
        name="forward",
    )(*operands)


def backward(*operands):
    return pl.pallas_call(
        backward_kernel,
        out_shape=(
            shape((2, ROWS, 128), F32),
            shape((4, 16, MLP), F32),
            shape((4, 16, MLP), F32),
            shape((4, 16, 512), F32),
            shape((4, 16, 512), F32),
            shape((4, 16, 256), F32),
        ),
        in_specs=[HBM, VM] + [HBM] * 22,
        out_specs=(VM,) * 6,
        scratch_shapes=vmem(
            *LAYER,
            WA,
            WM,
            ((8, ROWS, 128), BF),
            ((ROWS, D), F32),
            ((ROWS, D), BF),
            ((ROWS, D), BF),
            ((2, ROWS, 512), BF),
            ((2, KEYS, 128), BF),
            ((2, 128, KEYS), BF),
            ((2, ROWS, 384), BF),
            ((2, KEYS, 128), F32),
            ((2, KEYS, 128), F32),
            ((ROWS, D), F32),
            ((2, 8, D), F32),
            ((ROWS, 128), F32),
        )
        + [DMA((32,)), DMA((100,)), DMA((100,))]
        + scatter_scratch(MLP)
        + scatter_scratch(512)
        + scatter_scratch(256)
        + ring_scratch()
        + ring_scratch(),
        compiler_params=params(1, 60),
        name="backward",
    )(*operands)


def pack_inputs(weights, d):
    ag, ash, qw, qb, kw, vw, vb, ow, ob, fg, fs, uw, ub, dw, db = weights
    columns = jnp.pad(jnp.stack([ag, ash, ob, fg, fs, db], axis=2), ((0, 0), (0, 0), (0, 58)))
    heads = jnp.concatenate([qb, vb, ub], axis=1)
    here = (jnp.arange(16) == d)[None, None, :, None]
    heads = jnp.where(here, heads[:, :, None, :], jnp.zeros((), BF)).reshape(2, 12, 64)
    heads = jnp.pad(heads, ((0, 0), (0, 52), (0, 0)))
    vectors = jnp.concatenate([columns, heads], axis=2).reshape(2, 4, 16, 128)
    split = (2, 4, 16)
    return (
        qw.reshape(*split, 128), kw.reshape(*split, 128), vw.reshape(*split, 128), uw.reshape(*split, 512), ow, dw, vectors,
    )


def unpack_grads(mlp, att, small, d):
    mlp = jnp.stack(mlp).reshape(2, 64, MLP)
    att = jnp.stack(att).reshape(2, 64, 512)
    small = jnp.transpose(small.reshape(64, 2, 128), (1, 0, 2))
    columns = [small[:, :, k] for k in range(6)]
    mine = lax.dynamic_slice_in_dim(small[:, 0:12, 64:128], d * 4, 4, axis=2)

    def turn(rows):
        return jnp.transpose(rows, (0, 2, 1))

    return (
        columns[0], columns[1], att[:, :, 0:128], mine[:, 0:2], att[:, :, 128:256], att[:, :, 256:384], mine[:, 2:4],
        turn(att[:, :, 384:512]), columns[2], columns[3], columns[4], mlp[:, :, 0:512], mine[:, 4:12],
        turn(mlp[:, :, 512:1024]), columns[5],
    )


def local(images, cotangent, counts, *weights):
    d = lax.axis_index("dp")
    alive = (jnp.arange(2) < counts[0])[:, None, None]
    pad = ((0, 0), (0, ROWS - SEQ), (0, 0))
    images = jnp.pad(images, pad)
    cotangent = jnp.pad(jnp.where(alive, cotangent, jnp.zeros((), BF)), pad)
    *saved, vec, cot, act = forward(images, cotangent, *pack_inputs(weights, d))
    gin, mlp0, mlp1, att0, att1, small = backward(cot, vec, *saved)
    return (
        jnp.where(alive, act[:, :SEQ], jnp.zeros((), BF)),
        gin[:, :SEQ],
        *unpack_grads((mlp0, mlp1), (att0, att1), small, d),
    )


def solution(mesh):
    row = P(None, "dp")
    columns = P(None, "dp", "tensor")
    heads = P(None, "tensor", "dp")
    weights = (
        row, row, columns, heads, columns, columns, heads, heads, row, row, row, columns, heads, heads, row,
    )
    stream = P("dp", None, "tensor")
    return jax.shard_map(
        local,
        mesh=mesh,
        in_specs=(stream, stream, P("dp"), *weights),
        out_specs=(stream, stream, *weights),
        check_vma=False,
    )
```

```python
import functools
import math

import jax
import jax.numpy as jnp
from jax import lax
from jax.experimental import pallas as pl
from jax.experimental.pallas import tpu as pltpu
from jax.sharding import PartitionSpec as P

HD = 64
EPSILON = 1e-06
SCALE = 1.0 / math.sqrt(HD)
BF = jnp.bfloat16
F32 = jnp.float32

SEQ = 577
D = 1024
ROWS = 592
KEYS = 640
ATT = 512
OUT = 512
MLP = 1024
CHUNKS = ((0, 128), (128, 128), (256, 128), (384, 128), (512, 80))
NQ = len(CHUNKS)

TN = (((1,), (1,)), ((), ()))
NT = (((0,), (0,)), ((), ()))


def dot(a, b, dims=(((1,), (0,)), ((), ()))):
    return lax.dot_general(a, b, dims, preferred_element_type=F32)


def block(k, width=256):
    return pl.ds(pl.multiple_of(k * width, width), width)


def greet(devices):
    barrier = pltpu.get_barrier_semaphore()
    for device in devices:
        pl.semaphore_signal(barrier, inc=1, device_id=device, device_id_type=pl.DeviceIdType.MESH)
    return lambda: pl.semaphore_wait(barrier, len(devices))


class Ring:
    def __init__(self, send, near, far, full, send_sem, recv_sem):
        t = lax.axis_index("tensor")
        y = t // 2
        self.y = y
        self.yl, self.yr, self.yo = lax.rem(y + 3, 4), lax.rem(y + 1, 4), lax.rem(y + 2, 4)
        self.left = {"tensor": lax.rem(t + 6, 8)}
        self.right = {"tensor": lax.rem(t + 2, 8)}
        self.send, self.near, self.far, self.full = send, near, far, full
        self.send_sem, self.recv_sem = send_sem, recv_sem
        self.flying = {}

    def go(self, stage, q, to_left, to_right):
        copies = []
        for side, (src, dst) in enumerate((to_left, to_right)):
            copy = pltpu.make_async_remote_copy(
                src_ref=src,
                dst_ref=dst,
                send_sem=self.send_sem.at[stage, q, side],
                recv_sem=self.recv_sem.at[stage, q, side],
                device_id=self.left if side == 0 else self.right,
                device_id_type=pl.DeviceIdType.MESH,
            )
            copy.start()
            copies.append(copy)
        self.flying[stage, q] = copies

    def arrive(self, stage, q):
        for copy in self.flying[stage, q]:
            copy.wait_recv()

    def parts(self, q):
        r0, nr = CHUNKS[q]
        top = 64 if nr == 128 else 48
        return pl.ds(r0, nr), pl.ds(r0, top), pl.ds(r0 + top, nr - top)

    def stage0(self, q):
        rows, a, b = self.parts(q)
        c = block(self.yo)
        self.go(0, q, (self.send.at[a, c], self.near.at[0, a, :]), (self.send.at[b, c], self.near.at[1, b, :]))

    def stage1(self, q):
        rows, a, b = self.parts(q)
        self.arrive(0, q)
        cl, cr = block(self.yl), block(self.yr)
        self.send[a, cl] = (self.send[a, cl].astype(F32) + self.near[0, a, :].astype(F32)).astype(BF)
        self.send[b, cr] = (self.send[b, cr].astype(F32) + self.near[1, b, :].astype(F32)).astype(BF)
        self.go(
            1, q, (self.send.at[rows, cl], self.far.at[0, rows, :]), (self.send.at[rows, cr], self.far.at[1, rows, :])
        )

    def stage2(self, q):
        rows, a, b = self.parts(q)
        self.arrive(1, q)
        c = block(self.y)
        total = self.send[rows, c].astype(F32) + self.far[0, rows, :].astype(F32) + self.far[1, rows, :].astype(F32)
        self.full[rows, c] = total.astype(BF)
        self.go(2, q, (self.full.at[rows, c], self.full.at[rows, c]), (self.full.at[rows, c], self.full.at[rows, c]))

    def stage3(self, q):
        rows, a, b = self.parts(q)
        self.arrive(2, q)
        cl, cr = block(self.yl), block(self.yr)
        self.go(3, q, (self.full.at[a, cr], self.full.at[a, cr]), (self.full.at[b, cl], self.full.at[b, cl]))

    def stage4(self, q):
        self.arrive(3, q)

    def drain(self):
        for copies in self.flying.values():
            for copy in copies:
                copy.wait_send()
        self.flying = {}


class Spread(Ring):
    def __init__(self, full, send_sem, recv_sem):
        super().__init__(None, None, None, full, send_sem, recv_sem)

    def stage0(self, q):
        rows, a, b = self.parts(q)
        own = self.full.at[:, rows, block(self.y, 128)]
        self.go(0, q, (own, own), (own, own))

    def stage1(self, q):
        rows, a, b = self.parts(q)
        self.arrive(0, q)
        from_right, from_left = self.full.at[:, a, block(self.yr, 128)], self.full.at[:, b, block(self.yl, 128)]
        self.go(1, q, (from_right, from_right), (from_left, from_left))

    def stage2(self, q):
        self.arrive(1, q)


def ring_scratch():
    return [
        pltpu.VMEM((ROWS, D), BF),
        pltpu.VMEM((2, ROWS, 256), BF),
        pltpu.VMEM((2, ROWS, 256), BF),
        pltpu.VMEM((ROWS, D), BF),
        pltpu.SemaphoreType.DMA((4, NQ, 2)),
        pltpu.SemaphoreType.DMA((4, NQ, 2)),
    ]


def standardize(x):
    average = jnp.mean(x, axis=1, keepdims=True)
    centered = x - average
    variance = jnp.mean(centered * centered, axis=1, keepdims=True)
    rstd = lax.rsqrt(variance + EPSILON)
    return centered * rstd, rstd


def half_masks():
    lane = lax.broadcasted_iota(jnp.int32, (1, 128), 1)
    first = (lane < 64).astype(F32)
    return first.astype(BF), (1.0 - first).astype(BF)


def key_rows():
    return lax.broadcasted_iota(jnp.int32, (KEYS, 128), 0) < SEQ


def flip(rows):
    return jnp.transpose(rows.astype(F32), (1, 0))


def pair(first, second):
    top = lax.broadcasted_iota(jnp.int32, first.shape, 0) < 64
    return jnp.where(top, first, second)


def torus():
    d, t = lax.axis_index("dp"), lax.axis_index("tensor")
    x, z = d // 4, lax.rem(d, 4)
    return d, t, x, z, lax.rem(t, 2)


def dp_device(x, z):
    return {"dp": lax.rem(x + 4, 4) * 4 + lax.rem(z + 4, 4)}


class Exchange:
    def __init__(self, send_sem, recv_sem):
        self.send_sem, self.recv_sem, self.count, self.started = send_sem, recv_sem, 0, []

    def go(self, src, dst, device):
        copy = pltpu.make_async_remote_copy(
            src_ref=src,
            dst_ref=dst,
            send_sem=self.send_sem.at[self.count],
            recv_sem=self.recv_sem.at[self.count],
            device_id=device,
            device_id_type=pl.DeviceIdType.MESH,
        )
        copy.start()
        self.count += 1
        self.started.append(copy)
        return copy

    def drain(self):
        for copy in self.started:
            copy.wait_send()


def sides(half, x, z):
    along_x = [dp_device(x + j, z) for j in (1, 2, 3)]
    along_z = [dp_device(x, z + j) for j in (1, 2, 3)]
    return (x, z, along_x, along_z) if half == 0 else (z, x, along_z, along_x)


def place(half, a, b):
    return (a, b) if half == 0 else (b, a)


def wrap(k):
    return lax.rem(k + 4, 4)


ALL = pl.ds(0, 4)

class Background:
    def __init__(self):
        self.steps = []

    def add(self, *steps):
        self.steps.extend(steps)

    def run(self, count=1):
        for _ in range(min(count, len(self.steps))):
            self.steps.pop(0)()

    def until(self, step):
        while step in self.steps:
            self.steps.pop(0)()


def pipeline(stages, background, fillers=None):
    fillers = fillers or {}
    for step in range(NQ + len(stages) - 1):
        for k, stage in enumerate(stages):
            if 0 <= step - k < NQ:
                stage(step - k)
            if k == 0:
                for filler in fillers.get(step, ()):
                    filler()
                background.run()


class Gather:
    def __init__(self, ex, w):
        self.ex, self.w = ex, w
        d, t, self.x, self.z, self.c = torus()
        self.partner = {"tensor": t + 1 - 2 * self.c}
        self.state = [None, None]
        self.hand = []

    def at(self, h, a, b, quarters):
        return self.w.at[(self.c, *place(h, a, b), quarters)]

    def push(self, ref, device):
        return self.ex.go(ref, ref, device)

    def one(self):
        for h in range(2):
            a, b, along_a, along_b = sides(h, self.x, self.z)
            own = self.at(h, a, b, pl.ds(2 * h, 2))
            self.state[h] = [self.push(own, device) for device in along_a]

    def two(self):
        for h in range(2):
            a, b, along_a, along_b = sides(h, self.x, self.z)
            for copy in self.state[h]:
                copy.wait_recv()
            row = self.at(h, ALL, b, pl.ds(2 * h, 2))
            self.state[h] = [self.push(row, device) for device in along_b]
            self.hand.append(self.push(row, self.partner))

    def three(self):
        for j in (0, 2, 1):
            for h in range(2):
                a, b, along_a, along_b = sides(h, self.x, self.z)
                self.state[h][j].wait_recv()
                self.hand.append(self.push(self.at(h, ALL, wrap(b - 1 - j), pl.ds(2 * h, 2)), self.partner))

    def four(self):
        for copy in self.hand:
            copy.wait_recv()


class Scatter:
    def __init__(self, ex, r, store, got, second, first):
        self.ex, self.r, self.store, self.got = ex, r, store, got
        self.second, self.first = second, first
        d, t, self.x, self.z, self.c = torus()
        self.partner = {"tensor": t + 1 - 2 * self.c}
        self.state = [None, None]
        self.sent = []

    def at(self, h, a, b, quarters):
        return self.r.at[(self.c, *place(h, a, b), quarters)]

    def push(self, src, dst, device):
        copy = self.ex.go(src, dst, device)
        self.sent.append(copy)
        return copy

    def landed(self, h):
        for copy in self.state[h]:
            copy.wait_recv()

    def zero(self):
        for h in range(2):
            both = pl.ds(2 * h, 2)
            self.state[h] = [
                self.push(self.r.at[1 - self.c, :, :, both], self.got.at[:, :, both], self.partner)
            ]

    def one(self):
        for h in range(2):
            a, b, along_a, along_b = sides(h, self.x, self.z)
            both = pl.ds(2 * h, 2)
            self.landed(h)

            def merge(i, _):
                ref = self.r.at[self.c, i, :, both]
                ref[...] = add(ref, self.got.at[i, :, both]).astype(BF)
                return 0

            lax.fori_loop(0, 4, merge, 0)
            self.state[h] = [
                self.push(self.at(h, ALL, wrap(b + 1 + j), both), self.second.at[h, j], along_b[j]) for j in range(3)
            ]

    def two(self):
        for h in range(2):
            a, b, along_a, along_b = sides(h, self.x, self.z)
            both = pl.ds(2 * h, 2)
            self.landed(h)
            for i in range(4):
                ref = self.at(h, i, b, both)
                ref[...] = add(ref, *(self.second.at[h, j, i] for j in range(3))).astype(BF)
            self.state[h] = [
                self.push(self.at(h, wrap(a + 1 + j), b, both), self.first.at[h, j], along_a[j]) for j in range(3)
            ]

    def three(self):
        for h in range(2):
            a, b, along_a, along_b = sides(h, self.x, self.z)
            both = pl.ds(2 * h, 2)
            self.landed(h)
            total = add(self.at(h, a, b, both), *(self.first.at[h, j] for j in range(3)))
            self.store(h, total.reshape(32, total.shape[2]))
        for copy in self.sent:
            copy.wait_send()


def add(*terms):
    total = terms[0][...].astype(F32)
    for term in terms[1:]:
        total = total + term[...].astype(F32)
    return total


def scatter_scratch(width):
    return [
        pltpu.VMEM((2, 4, 4, 4, 16, width), BF),
        pltpu.VMEM((4, 4, 4, 16, width), BF),
        pltpu.VMEM((2, 3, 4, 2, 16, width), BF),
        pltpu.VMEM((2, 3, 2, 16, width), BF),
    ]


def mat(ref, c, lo, hi):
    return ref[c, :, :, :, :, lo:hi].reshape(D, hi - lo)


def put(ref, c, lo, hi, value):
    ref[c, :, :, :, :, lo:hi] = value.astype(BF).reshape(4, 4, 4, 16, hi - lo)


class Local:
    def __init__(self, sem):
        self.sem, self.count = sem, 0

    def go(self, src, dst):
        copy = pltpu.make_async_copy(src, dst, self.sem.at[self.count])
        copy.start()
        self.count += 1
        return copy


def column_sum(value):
    return jnp.sum(value.astype(F32), axis=0, keepdims=True)


def low_lanes(shape):
    return lax.broadcasted_iota(jnp.int32, shape, 1) < 64


def unpack_vectors(wa, vec):
    vec[0:8, :] = flip(mat(wa, 0, 384, ATT))[0:8]
    for c in range(2):
        heads = jnp.sum(mat(wa, c, 384, ATT).reshape(16, 64, 128)[:, 0:16].astype(F32), axis=0)
        rolled = pltpu.roll(heads, 64, 1)

        def both(k):
            return jnp.where(low_lanes((1, 128)), rolled[k : k + 1], heads[k + 1 : k + 2])

        vec[6:7, c * 128 : c * 128 + 128] = both(0)
        vec[6:7, 256 + c * 128 : 384 + c * 128] = both(2)
        for m in range(4):
            vec[7:8, c * 512 + 128 * m : c * 512 + 128 * m + 128] = both(4 + 2 * m)


def pack_vectors(vg, rv, lane):
    padded = jnp.concatenate([vg[...], jnp.zeros((120, D), F32)], axis=0)
    kind = lax.broadcasted_iota(jnp.int32, (128, D), 0)
    columns = flip(jnp.where(kind < 6, padded, 0.0)).reshape(16, 64, 128)
    row = lax.broadcasted_iota(jnp.int32, (64, 128), 0)
    for c in range(2):
        pieces = [vg[6:7, c * 128 : c * 128 + 128], vg[6:7, 256 + c * 128 : 384 + c * 128]]
        pieces += [vg[7:8, c * 512 + 128 * m : c * 512 + 128 * m + 128] for m in range(4)]
        heads = jnp.zeros((64, 128), F32)
        for k, piece in enumerate(pieces):
            rolled = pltpu.roll(jnp.broadcast_to(piece, (8, 128)), 64, 1)[0:1]
            heads = jnp.where(row == 2 * k, rolled, heads)
            heads = jnp.where(row == 2 * k + 1, piece, heads)
        heads = jnp.where(low_lanes((64, 128)), 0.0, heads)
        put(rv, c, lane, lane + 128, (columns + heads[None]).reshape(D, 128))


def forward_kernel(
    img_ref, cot_ref, qw_ref, kw_ref, vw_ref, uw_ref, ow_ref, dw_ref,
    *refs,
):
    refs = list(refs)
    features = [refs.pop(0) for _ in range(6)]
    heads = [refs.pop(0) for _ in range(3)]
    saved = [[refs.pop(0) for _ in range(9)] for _ in range(2)]
    wa_out = [refs.pop(0) for _ in range(2)]
    wm_out = [refs.pop(0) for _ in range(2)]
    wo_out = [refs.pop(0) for _ in range(2)]
    vec_ref, xc_ref, act_ref = [refs.pop(0) for _ in range(3)]
    kept = [[refs.pop(0) for _ in range(8)] for _ in range(2)]
    wa = [refs.pop(0) for _ in range(2)]
    wm = [refs.pop(0) for _ in range(2)]
    wo = [refs.pop(0) for _ in range(2)]
    heads_full = [refs.pop(0) for _ in range(2)]
    xg_ref, vt_ref, give_ref, local_sem, send_sem, recv_sem = [refs.pop(0) for _ in range(6)]
    spread_sems = refs[6:8]
    square_ref, strip_ref = refs[8:10]
    two = Ring(*refs[:6])
    d, t, x, z, c_here = torus()
    y = t // 2
    partner = {"tensor": t + 1 - 2 * c_here}
    others = [{"tensor": lax.rem(t + j, 8)} for j in range(1, 8)]
    _, _, along_x, along_z = sides(0, x, z)
    entered = greet(along_x + along_z + others)
    local, ex, background = Local(local_sem), Exchange(send_sem, recv_sem), Background()
    groups = [Gather(ex, ref) for ref in (wa[0], wm[0], wa[1], wm[1])]
    m0, a1, m1 = groups[1:]
    o0, o1 = [Gather(ex, ref) for ref in wo]
    pieces = []
    own = []
    for layer in range(2):
        slot = wa[layer].at[c_here, x, z]
        own.append(
            [local.go(src.at[layer], slot.at[:, :, pl.ds(128 * k, 128)]) for k, src in enumerate((qw_ref, kw_ref, vw_ref))]
        )
        own.append([local.go(uw_ref.at[layer], wm[layer].at[c_here, x, z, :, :, pl.ds(0, 512)])])
    mine = local.go(img_ref.at[c_here], xg_ref.at[t])
    theirs = local.go(cot_ref.at[c_here], xc_ref.at[t])

    def build_att(layer):
        for k, ref in enumerate(features):
            square_ref[k : k + 1, 0:64] = ref[...].astype(F32)[layer : layer + 1]
        columns = flip(square_ref[...])[0:64]
        first = 0
        for ref in heads:
            rows = ref[layer].astype(F32)
            strip_ref[first : first + rows.shape[0], 0:4] = rows
            first += rows.shape[0]
        strip = pltpu.roll(strip_ref[...], 64 + 4 * d, 1)
        vectors = columns + jnp.concatenate([strip, jnp.zeros((48, 128), F32)], axis=0)
        wa[layer][c_here, x, z, :, :, 384:ATT] = vectors.astype(BF).reshape(4, 16, 128)

    def build_out(layer):
        wo[layer][c_here, x, z, :, :, block(y, 128)] = ow_ref[layer].reshape(4, 16, 128)
        piece = wo[layer].at[c_here, x, z, :, :, block(y, 128)]
        pieces.append([ex.go(piece, piece, others[j]) for j in (1, 3, 5)])

    def start_out(layer):
        def run():
            for copy in pieces[layer]:
                copy.wait_recv()
            (o0, o1)[layer].one()

        return run

    def build_mlp(layer):
        wm[layer][c_here, x, z, :, :, 512:MLP] = dw_ref[layer].reshape(4, 16, 512)

    def start(k):
        def run():
            for copy in own[k]:
                copy.wait()
            groups[k].one()

        return run

    def exchange(src, dst):
        copies = []
        for j in range(1, 8):
            target = lax.rem(t + j, 8)
            copies.append(ex.go(src.at[lax.rem(target, 2)], dst.at[t], others[j - 1]))
        return copies

    square_ref[...] = jnp.zeros((128, 128), F32)
    strip_ref[...] = jnp.zeros((16, 128), F32)
    build_att(0)
    entered()
    start(0)()
    build_out(0)
    images = exchange(img_ref, xg_ref)
    build_mlp(0)
    build_out(1)
    build_att(1)
    build_mlp(1)
    groups[0].two()
    start_out(0)()
    start(1)()
    mine.wait()
    for copy in images:
        copy.wait_recv()
    cotangents = exchange(cot_ref, xc_ref)
    for r0, nr in CHUNKS:
        rows = pl.ds(r0, nr)
        for j in range(8):
            kept[0][0][rows, 128 * j : 128 * j + 128] = xg_ref[j, rows, :].astype(F32)
    groups[0].three()
    o0.two()
    m0.two()
    groups[0].four()
    masks = half_masks()
    valid = key_rows()

    def rest():
        pass

    background.add(o0.three, start(2), m0.three, o0.four, m0.four, a1.two, start_out(1), a1.three, a1.four, start(3))
    background.add(o1.two, rest, o1.three, m1.two, o1.four, m1.three, m1.four)
    for layer in range(2):
        kept[layer][2][:, ROWS:KEYS, :] = jnp.zeros((2, KEYS - ROWS, 384), BF)

    def project(layer, q):
        r0, nr = CHUNKS[q]
        rows = pl.ds(r0, nr)
        x_ref, n1_ref, qkv_ref = kept[layer][:3]
        vec = vec_ref.at[layer]
        xhat, _ = standardize(x_ref[rows, :])
        n1 = (xhat * vec[0:1, :] + vec[1:2, :]).astype(BF)
        n1_ref[rows, :] = n1
        for c in range(2):
            out = dot(n1, mat(wa[layer], c, 0, 384))
            qkv_ref[c, rows, 0:128] = (out[:, 0:128] + vec[6:7, c * 128 : c * 128 + 128]).astype(BF)
            qkv_ref[c, rows, 128:256] = out[:, 128:256].astype(BF)
            qkv_ref[c, rows, 256:384] = (out[:, 256:384] + vec[6:7, 256 + c * 128 : 384 + c * 128]).astype(BF)

    unpack_vectors(wa[0], vec_ref.at[0])
    for q in range(NQ):
        project(0, q)

    def layer_forward(layer):
        x_ref, n1_ref, qkv_ref, lse_ref, mid_ref, n2_ref, slope_ref, a_ref = kept[layer]
        one = Spread(heads_full[layer], *spread_sems)
        x_out, n1_out, qkv_out, lse_out, o_out, mid_out, n2_out, slope_out, a_out = saved[layer]
        vec = vec_ref.at[layer]
        waits = [
            local.go(src, dst)
            for src, dst in ((x_ref, x_out), (n1_ref, n1_out), (wa[layer], wa_out[layer]), (qkv_ref, qkv_out))
        ]
        for c in range(2):
            vt_ref[c] = flip(qkv_ref[c, :, 256:384]).astype(BF)

        def attend(q):
            r0, nr = CHUNKS[q]
            for c in range(2):
                queries, keys = qkv_ref[c, r0 : r0 + 128, 0:128], qkv_ref[c, :, 128:256]
                halves = []
                for h in range(2):
                    s = dot(keys, queries * masks[h], TN) * SCALE
                    s = jnp.where(valid, s, -1e30)
                    top = jnp.max(s, axis=0, keepdims=True)
                    e = jnp.exp(s - top)
                    norm = jnp.sum(e, axis=0, keepdims=True)
                    lse_ref[2 * c + h : 2 * c + h + 1, r0 : r0 + 128] = top + jnp.log(norm)
                    p = (e * (1.0 / norm)).astype(BF)
                    halves.append(dot(vt_ref[c], p))
                one.full[c, r0 : r0 + nr, block(y, 128)] = flip(pair(*halves))[0:nr].astype(BF)
            one.stage0(q)
            if q == NQ - 1:
                waits.extend([local.go(lse_ref, lse_out), local.go(one.full.at[:, :, block(y, 128)], o_out)])

        def feed(q):
            r0, nr = CHUNKS[q]
            rows = pl.ds(r0, nr)
            if q == 0:
                background.until(groups[2 * layer + 1].four)
                waits.append(local.go(wm[layer], wm_out[layer]))
                waits.append(local.go(wo[layer].at[:, :, :, :, :, block(y, 128)], wo_out[layer]))
            one.stage2(q)
            mid = x_ref[rows, :] + vec[2:3, :]
            for c in range(2):
                mid = mid + dot(one.full[c, rows, :], mat(wo[layer], c, 0, OUT), TN)
            mid_ref[rows, :] = mid
            xhat, _ = standardize(mid)
            n2 = (xhat * vec[3:4, :] + vec[4:5, :]).astype(BF)
            n2_ref[rows, :] = n2
            total = None
            for c in range(2):
                u = dot(n2, mat(wm[layer], c, 0, 512)) + vec[7:8, c * 512 : c * 512 + 512]
                phi = 0.5 * (1.0 + lax.erf(u * (1.0 / math.sqrt(2.0))))
                slope = phi + u * (jnp.exp(-0.5 * u * u) * (1.0 / math.sqrt(2.0 * math.pi)))
                slope_ref[c, rows, :] = slope.astype(BF)
                a = (u * phi).astype(BF)
                a_ref[c, rows, :] = a
                part = dot(a, mat(wm[layer], c, 512, MLP), TN)
                total = part if total is None else total + part
            two.send[rows, :] = total.astype(BF)
            two.stage0(q)
            if q == NQ - 1:
                waits.extend(
                    local.go(src, dst)
                    for src, dst in ((mid_ref, mid_out), (n2_ref, n2_out), (slope_ref, slope_out), (a_ref, a_out))
                )

        def finish(q):
            r0, nr = CHUNKS[q]
            rows = pl.ds(r0, nr)
            two.stage4(q)
            kept[1][0][rows, :] = mid_ref[rows, :] + two.full[rows, :].astype(F32) + vec[5:6, :]
            if q == 0:
                background.until(a1.four)
                unpack_vectors(wa[1], vec_ref.at[1])
            project(1, q)

        swaps = []

        def last(q):
            r0, nr = CHUNKS[q]
            rows = pl.ds(r0, nr)
            two.arrive(1, q)
            c = block(y)
            total = two.send[rows, c].astype(F32) + two.far[0, rows, :].astype(F32) + two.far[1, rows, :].astype(F32)
            total = total + mid_ref[rows, c] + vec[5:6, c]
            left, right = total[:, 0:128].astype(BF), total[:, 128:256].astype(BF)
            act_ref[c_here, rows, :] = jnp.where(c_here == 0, left, right)
            give_ref[rows, :] = jnp.where(c_here == 0, right, left)
            swaps.append(ex.go(give_ref.at[rows], act_ref.at[c_here, rows], partner))

        stages = (attend, one.stage1, feed, two.stage1)
        stages += (two.stage2, two.stage3, finish) if layer == 0 else (last,)
        pipeline(stages, background)
        one.drain()
        two.drain()
        return waits, swaps

    waits0, _ = layer_forward(0)
    waits1, swaps = layer_forward(1)
    theirs.wait()
    for copy in cotangents + swaps:
        copy.wait_recv()
    for copy in waits0 + waits1:
        copy.wait()
    ex.drain()


def backward_kernel(
    cot_ref, vec_ref, *refs,
):
    refs = list(refs)
    saved = [[refs.pop(0) for _ in range(9)] for _ in range(2)]
    wa_in = [refs.pop(0) for _ in range(2)]
    wm_in = [refs.pop(0) for _ in range(2)]
    wo_in = [refs.pop(0) for _ in range(2)]
    gin_ref, qg_ref, kg_ref, vgrad_ref, og_ref, ug_ref, dg_ref, small_ref = [refs.pop(0) for _ in range(8)]
    x_ref, n1_ref, qkv_ref, lse_ref, o_ref, mid_ref, n2_ref, slope_ref, a_ref = [refs.pop(0) for _ in range(9)]
    wa, wm = refs.pop(0), refs.pop(0)
    xg_ref, g_ref, gm_ref, go_ref, hid_ref, dout_ref, kt_ref, dqkv_ref, dk_ref, dv_ref, gmid_ref, vg_ref, give_ref = [
        refs.pop(0) for _ in range(13)
    ]
    local_sem, send_sem, recv_sem = [refs.pop(0) for _ in range(3)]
    mlp, att, small = [[refs.pop(0) for _ in range(4)] for _ in range(3)]
    one, two = Ring(*refs[:6]), Ring(*refs[6:12])
    d, t, x, z, c_here = torus()
    y = t // 2
    partner = {"tensor": t + 1 - 2 * c_here}
    _, _, along_x, along_z = sides(0, x, z)
    entered = greet(along_x + along_z + [one.left, one.right, partner])
    local, ex, background = Local(local_sem), Exchange(send_sem, recv_sem), Background()

    def load_mlp(layer):
        _, _, _, _, _, mid, n2, slope, a = saved[layer]
        pairs = ((wm_in[layer], wm), (slope, slope_ref), (a, a_ref), (mid, mid_ref), (n2, n2_ref))
        return [local.go(src, dst) for src, dst in pairs]

    def load_att(layer):
        stream, n1, qkv, lse, o = saved[layer][:5]
        low, high = pl.ds(0, 384), pl.ds(384, 128)
        pairs = (
            (wa_in[layer].at[:, :, :, :, :, low], wa.at[:, :, :, :, :, low]),
            (wo_in[layer], wa.at[:, :, :, :, :, high]),
        )
        pairs += ((qkv, qkv_ref), (lse, lse_ref), (o, o_ref), (n1, n1_ref))
        return [local.go(src, dst) for src, dst in pairs]

    cot = local.go(cot_ref, xg_ref)
    loads = {1: load_mlp(1)}
    att_loads = {1: load_att(1)}
    x_loads = {1: local.go(saved[1][0], x_ref)}
    masks = half_masks()
    valid = key_rows()
    dout_ref[:, ROWS:KEYS, :] = jnp.zeros((2, KEYS - ROWS, 128), BF)
    cot.wait()
    for r0, nr in CHUNKS:
        rows = pl.ds(r0, nr)
        for j in range(8):
            g_ref[rows, 128 * j : 128 * j + 128] = xg_ref[j, rows, :].astype(F32)
    entered()
    swaps = []

    vg_ref[...] = jnp.zeros((2, 8, D), F32)

    def layer_steps(layer):
        vec, vg = vec_ref.at[layer], vg_ref.at[layer]

        def store_mlp(h, value):
            rows = slice(32 * h, 32 * h + 32)
            ug_ref[layer, rows, :] = value[:, 0:512]
            dg_ref[layer, rows, :] = value[:, 512:1024]

        def store_att(h, value):
            rows = slice(32 * h, 32 * h + 32)
            for k, ref in enumerate((qg_ref, kg_ref, vgrad_ref, og_ref)):
                ref[layer, rows, :] = value[:, 128 * k : 128 * k + 128]

        mlp_scatter = Scatter(ex, mlp[0], store_mlp, *mlp[1:])
        att_scatter = Scatter(ex, att[0], store_att, *att[1:])

        def add_vector(row, value, lane=0):
            width = value.shape[1]
            vg[row : row + 1, lane : lane + width] = vg[row : row + 1, lane : lane + width] + value

        def hidden(q):
            r0, nr = CHUNKS[q]
            rows = pl.ds(r0, nr)
            if q == 0:
                for copy in loads[layer]:
                    copy.wait()
            gm = g_ref[rows, :].astype(BF)
            gm_ref[rows, :] = gm
            add_vector(5, column_sum(gm))
            total = None
            for c in range(2):
                da = dot(gm, mat(wm, c, 512, MLP))
                du = (da * slope_ref[c, rows, :].astype(F32)).astype(BF)
                hid_ref[c, rows, :] = du
                add_vector(7, column_sum(du), c * 512)
                part = dot(du, mat(wm, c, 0, 512), TN)
                total = part if total is None else total + part
            one.send[rows, :] = total.astype(BF)
            one.stage0(q)

        def norm_back(ring, q, stream, grad, gain_row, shift_row):
            r0, nr = CHUNKS[q]
            rows = pl.ds(r0, nr)
            ring.stage4(q)
            dn = ring.full[rows, :].astype(F32)
            xhat, rstd = standardize(stream[rows, :])
            add_vector(gain_row, column_sum(dn * xhat))
            add_vector(shift_row, column_sum(dn))
            e = dn * vec[gain_row : gain_row + 1, :]
            first = jnp.mean(e, axis=1, keepdims=True)
            second = jnp.mean(e * xhat, axis=1, keepdims=True)
            return grad[rows, :] + rstd * (e - first - xhat * second)

        def attend(q):
            r0, nr = CHUNKS[q]
            rows = pl.ds(r0, nr)
            if q == 0:
                for copy in att_loads[layer]:
                    copy.wait()
                for c in range(2):
                    kt_ref[c] = flip(qkv_ref[c, :, 128:256]).astype(BF)
                dk_ref[...] = jnp.zeros(dk_ref.shape, F32)
                dv_ref[...] = jnp.zeros(dv_ref.shape, F32)
            mid_grad = norm_back(one, q, mid_ref, g_ref, 3, 4)
            gmid_ref[rows, :] = mid_grad
            go = mid_grad.astype(BF)
            go_ref[rows, :] = go
            add_vector(2, column_sum(go))
            for c in range(2):
                dout_ref[c, rows, :] = dot(go, mat(wa, c, 384, 512)).astype(BF)
                queries = qkv_ref[c, r0 : r0 + 128, 0:128]
                keys, values = qkv_ref[c, :, 128:256], qkv_ref[c, :, 256:384]
                dout = dout_ref[c, r0 : r0 + 128, :]
                halves = []
                for h in range(2):
                    qh, doh = queries * masks[h], dout * masks[h]
                    s = dot(keys, qh, TN) * SCALE
                    p = jnp.where(valid, jnp.exp(s - lse_ref[2 * c + h : 2 * c + h + 1, r0 : r0 + 128]), 0.0)
                    dp = dot(values, doh, TN)
                    delta = jnp.sum(dp * p, axis=0, keepdims=True)
                    ds = (p * (dp - delta)).astype(BF)
                    dv_ref[c] = dv_ref[c] + dot(p.astype(BF), doh)
                    dk_ref[c] = dk_ref[c] + dot(ds, qh)
                    halves.append(dot(kt_ref[c], ds))
                dq = (flip(pair(*halves)) * SCALE)[0:nr].astype(BF)
                dqkv_ref[c, rows, 0:128] = dq

        def down_grad(c):
            def run():
                put(mlp[0], c, 512, MLP, dot(gm_ref[...], a_ref[c], NT))

            return run

        def up_grad(c):
            def run():
                put(mlp[0], c, 0, 512, dot(n2_ref[...], hid_ref[c], NT))

            return run

        def out_grad():
            for c in range(2):
                put(att[0], c, 384, 512, dot(go_ref[...], o_ref[c], NT))

        def qkv_grad(c):
            def run():
                put(att[0], c, 0, 384, dot(n1_ref[...], dqkv_ref[c], NT))

            return run

        def settle():
            for c in range(2):
                dqkv_ref[c, :, 128:256] = (dk_ref[c, 0:ROWS] * SCALE).astype(BF)
                dqkv_ref[c, :, 256:384] = dv_ref[c, 0:ROWS].astype(BF)

        def project(q):
            r0, nr = CHUNKS[q]
            rows = pl.ds(r0, nr)
            total = None
            for c in range(2):
                grads = dqkv_ref[c, rows, :]
                add_vector(6, column_sum(grads[:, 0:128]), c * 128)
                add_vector(6, column_sum(grads[:, 256:384]), 256 + c * 128)
                part = dot(grads, mat(wa, c, 0, 384), TN)
                total = part if total is None else total + part
            two.send[rows, :] = total.astype(BF)
            two.stage0(q)

        def finish(q):
            r0, nr = CHUNKS[q]
            rows = pl.ds(r0, nr)
            if q == 0:
                x_loads[layer].wait()
            g_ref[rows, :] = norm_back(two, q, x_ref, gmid_ref, 0, 1)
            if layer == 0:
                left, right = g_ref[rows, block(2 * y, 128)], g_ref[rows, block(2 * y + 1, 128)]
                gin_ref[c_here, rows, :] = jnp.where(c_here == 0, left, right)
                give_ref[rows, :] = jnp.where(c_here == 0, right, left)
                swaps.append(ex.go(give_ref.at[rows], gin_ref.at[c_here, rows], partner))

        def pack():
            pack_vectors(vg, small[0], 128 * layer)

        return (
            hidden, attend, project, finish, settle, pack, mlp_scatter, att_scatter,
            (down_grad(0), down_grad(1)), (up_grad(0), up_grad(1)), (out_grad, qkv_grad(0), qkv_grad(1)),
        )

    def rest():
        pass

    hidden1, attend1, project1, finish1, settle1, pack1, m1, a1, down1, up1, grads1 = layer_steps(1)
    hidden0, attend0, project0, finish0, settle0, pack0, m0, a0, down0, up0, grads0 = layer_steps(0)
    pipeline(
        (hidden1, one.stage1, one.stage2, one.stage3, attend1),
        background,
        {5: (up1[0], down1[0]), 6: (up1[1], down1[1], m1.zero)},
    )
    one.drain()
    loads[0] = load_mlp(0)
    settle1()

    def turn(q):
        finish1(q)
        hidden0(q)

    def reload():
        att_loads[0] = load_att(0)

    def reload_x():
        x_loads[0] = local.go(saved[0][0], x_ref)

    def begin(steps):
        return lambda: background.add(*steps)

    background.add(m1.one, rest, m1.two, rest, a1.zero, m1.three, a1.one, rest, a1.two, a1.three)
    pipeline(
        (project1, two.stage1, two.stage2, two.stage3, turn, one.stage1, one.stage2, one.stage3, attend0),
        background,
        {
            1: grads1[:1],
            2: grads1[1:2],
            3: grads1[2:],
            5: (reload,),
            9: (reload_x, lambda: background.until(a1.three), *up0, *down0, m0.zero, begin((rest, m0.one, rest, rest))),
        },
    )
    one.drain()
    two.drain()
    pack1()
    settle0()
    background.add(m0.two, a0.zero, m0.three, a0.one, rest, a0.two, rest, a0.three)
    pipeline(
        (project0, two.stage1, two.stage2, two.stage3, finish0),
        background,
        {0: grads0[:2], 1: grads0[2:]},
    )
    pack0()

    def store_small(h, value):
        small_ref[32 * h : 32 * h + 32, :] = value

    last = Scatter(ex, small[0], store_small, *small[1:])
    last.zero()
    background.run(100)
    last.one()
    last.two()
    last.three()
    two.drain()
    for copy in swaps:
        copy.wait_recv()
        copy.wait_send()


VM = pl.BlockSpec(memory_space=pltpu.VMEM)
HBM = pl.BlockSpec(memory_space=pl.ANY)


def params(collective_id, megabytes):
    return pltpu.CompilerParams(
        collective_id=collective_id, has_side_effects=True, vmem_limit_bytes=megabytes * 1024 * 1024
    )


def shape(dims, dtype):
    return jax.ShapeDtypeStruct(dims, dtype)


LAYER = (
    ((ROWS, D), F32),
    ((ROWS, D), BF),
    ((2, KEYS, 384), BF),
    ((8, KEYS), F32),
    ((2, ROWS, 128), BF),
    ((ROWS, D), F32),
    ((ROWS, D), BF),
    ((2, ROWS, 512), BF),
    ((2, ROWS, 512), BF),
)
WA = ((2, 4, 4, 4, 16, ATT), BF)
WM = ((2, 4, 4, 4, 16, MLP), BF)
WO = ((2, 4, 4, 4, 16, OUT), BF)
WO_OWN = ((2, 4, 4, 4, 16, 128), BF)
HEADS = ((2, ROWS, OUT), BF)
KEPT = LAYER[:4] + LAYER[5:]
DMA = pltpu.SemaphoreType.DMA


def vmem(*kinds):
    return [pltpu.VMEM(*kind) for kind in kinds]


def forward(*operands):
    outs = [shape(*kind) for kind in LAYER * 2 + (WA, WA, WM, WM, WO_OWN, WO_OWN)]
    outs += [shape((2, 8, D), F32), shape((8, ROWS, 128), BF), shape((2, ROWS, 128), BF)]
    return pl.pallas_call(
        forward_kernel,
        out_shape=tuple(outs),
        in_specs=[HBM] * 6 + [VM] * 11,
        out_specs=tuple([HBM] * 24 + [VM, HBM, VM]),
        scratch_shapes=vmem(
            *KEPT, *KEPT, WA, WA, WM, WM, WO, WO, HEADS, HEADS,
            ((8, ROWS, 128), BF), ((2, 128, KEYS), BF), ((ROWS, 128), BF),
        )
        + [DMA((40,)), DMA((160,)), DMA((160,))]
        + ring_scratch()
        + [DMA((2, NQ, 2)), DMA((2, NQ, 2))]
        + vmem(((128, 128), F32), ((16, 128), F32)),
        compiler_params=params(0, 58),
        name="forward",
    )(*operands)


def backward(*operands):
    return pl.pallas_call(
        backward_kernel,
        out_shape=(
            shape((2, ROWS, 128), F32),
            shape((2, 64, 128), F32),
            shape((2, 64, 128), F32),
            shape((2, 64, 128), F32),
            shape((2, 64, 128), F32),
            shape((2, 64, 512), F32),
            shape((2, 64, 512), F32),
            shape((64, 256), F32),
        ),
        in_specs=[HBM, VM] + [HBM] * 24,
        out_specs=(VM,) * 8,
        scratch_shapes=vmem(
            *LAYER,
            WA,
            WM,
            ((8, ROWS, 128), BF),
            ((ROWS, D), F32),
            ((ROWS, D), BF),
            ((ROWS, D), BF),
            ((2, ROWS, 512), BF),
            ((2, KEYS, 128), BF),
            ((2, 128, KEYS), BF),
            ((2, ROWS, 384), BF),
            ((2, KEYS, 128), F32),
            ((2, KEYS, 128), F32),
            ((ROWS, D), F32),
            ((2, 8, D), F32),
            ((ROWS, 128), F32),
        )
        + [DMA((32,)), DMA((100,)), DMA((100,))]
        + scatter_scratch(MLP)
        + scatter_scratch(512)
        + scatter_scratch(256)
        + ring_scratch()
        + ring_scratch(),
        compiler_params=params(1, 60),
        name="backward",
    )(*operands)


def split_inputs(weights):
    ag, ash, qw, qb, kw, vw, vb, ow, ob, fg, fs, uw, ub, dw, db = weights
    split = (2, 4, 16)
    return (
        qw.reshape(*split, 128), kw.reshape(*split, 128), vw.reshape(*split, 128), uw.reshape(*split, 512),
        jnp.swapaxes(ow, 1, 2), jnp.swapaxes(dw, 1, 2), ag, ash, ob, fg, fs, db, qb, vb, ub,
    )


def unpack_grads(qg, kg, vg, og, ug, dg, small, d):
    small = jnp.transpose(small.reshape(64, 2, 128), (1, 0, 2))
    columns = [small[:, :, k] for k in range(6)]
    mine = lax.dynamic_slice_in_dim(small[:, 0:12, 64:128], d * 4, 4, axis=2)
    return (
        columns[0], columns[1], qg, mine[:, 0:2], kg, vg, mine[:, 2:4], jnp.swapaxes(og, 1, 2), columns[2], columns[3],
        columns[4], ug, mine[:, 4:12], jnp.swapaxes(dg, 1, 2), columns[5],
    )


def local(images, cotangent, counts, *weights):
    d = lax.axis_index("dp")
    alive = (jnp.arange(2) < counts[0])[:, None, None]
    pad = ((0, 0), (0, ROWS - SEQ), (0, 0))
    images = jnp.pad(images, pad)
    cotangent = jnp.pad(jnp.where(alive, cotangent, jnp.zeros((), BF)), pad)
    *saved, vec, cot, act = forward(images, cotangent, *split_inputs(weights))
    gin, *grads = backward(cot, vec, *saved)
    return (
        jnp.where(alive, act[:, :SEQ], jnp.zeros((), BF)),
        gin[:, :SEQ],
        *unpack_grads(*grads, d),
    )


def solution(mesh):
    row = P(None, "dp")
    columns = P(None, "dp", "tensor")
    heads = P(None, "tensor", "dp")
    weights = (
        row, row, columns, heads, columns, columns, heads, heads, row, row, row, columns, heads, heads, row,
    )
    stream = P("dp", None, "tensor")
    return jax.shard_map(
        local,
        mesh=mesh,
        in_specs=(stream, stream, P("dp"), *weights),
        out_specs=(stream, stream, *weights),
        check_vma=False,
    )
```

```python
import functools
import math

import jax
import jax.numpy as jnp
from jax import lax
from jax.experimental import pallas as pl
from jax.experimental.pallas import tpu as pltpu
from jax.sharding import PartitionSpec as P

HD = 64
EPSILON = 1e-06
SCALE = 1.0 / math.sqrt(HD)
BF = jnp.bfloat16
F32 = jnp.float32

SEQ = 577
D = 1024
ROWS = 592
KEYS = 640
ATT = 512
OUT = 512
MLP = 1024
CHUNKS = ((0, 128), (128, 128), (256, 128), (384, 128), (512, 80))
NQ = len(CHUNKS)

TN = (((1,), (1,)), ((), ()))
NT = (((0,), (0,)), ((), ()))


def dot(a, b, dims=(((1,), (0,)), ((), ()))):
    return lax.dot_general(a, b, dims, preferred_element_type=F32)


def block(k, width=256):
    return pl.ds(pl.multiple_of(k * width, width), width)


def greet(devices):
    barrier = pltpu.get_barrier_semaphore()
    for device in devices:
        pl.semaphore_signal(barrier, inc=1, device_id=device, device_id_type=pl.DeviceIdType.MESH)
    return lambda: pl.semaphore_wait(barrier, len(devices))


class Ring:
    def __init__(self, send, near, far, full, send_sem, recv_sem):
        t = lax.axis_index("tensor")
        y = t // 2
        self.y = y
        self.yl, self.yr, self.yo = lax.rem(y + 3, 4), lax.rem(y + 1, 4), lax.rem(y + 2, 4)
        self.left = {"tensor": lax.rem(t + 6, 8)}
        self.right = {"tensor": lax.rem(t + 2, 8)}
        self.send, self.near, self.far, self.full = send, near, far, full
        self.send_sem, self.recv_sem = send_sem, recv_sem
        self.flying = {}

    def go(self, stage, q, to_left, to_right):
        copies = []
        for side, (src, dst) in enumerate((to_left, to_right)):
            copy = pltpu.make_async_remote_copy(
                src_ref=src,
                dst_ref=dst,
                send_sem=self.send_sem.at[stage, q, side],
                recv_sem=self.recv_sem.at[stage, q, side],
                device_id=self.left if side == 0 else self.right,
                device_id_type=pl.DeviceIdType.MESH,
            )
            copy.start()
            copies.append(copy)
        self.flying[stage, q] = copies

    def arrive(self, stage, q):
        for copy in self.flying[stage, q]:
            copy.wait_recv()

    def parts(self, q):
        r0, nr = CHUNKS[q]
        top = 64 if nr == 128 else 48
        return pl.ds(r0, nr), pl.ds(r0, top), pl.ds(r0 + top, nr - top)

    def stage0(self, q):
        rows, a, b = self.parts(q)
        c = block(self.yo)
        self.go(0, q, (self.send.at[a, c], self.near.at[0, a, :]), (self.send.at[b, c], self.near.at[1, b, :]))

    def stage1(self, q):
        rows, a, b = self.parts(q)
        self.arrive(0, q)
        cl, cr = block(self.yl), block(self.yr)
        self.send[a, cl] = (self.send[a, cl].astype(F32) + self.near[0, a, :].astype(F32)).astype(BF)
        self.send[b, cr] = (self.send[b, cr].astype(F32) + self.near[1, b, :].astype(F32)).astype(BF)
        self.go(
            1, q, (self.send.at[rows, cl], self.far.at[0, rows, :]), (self.send.at[rows, cr], self.far.at[1, rows, :])
        )

    def stage2(self, q):
        rows, a, b = self.parts(q)
        self.arrive(1, q)
        c = block(self.y)
        total = self.send[rows, c].astype(F32) + self.far[0, rows, :].astype(F32) + self.far[1, rows, :].astype(F32)
        self.full[rows, c] = total.astype(BF)
        self.go(2, q, (self.full.at[rows, c], self.full.at[rows, c]), (self.full.at[rows, c], self.full.at[rows, c]))

    def stage3(self, q):
        rows, a, b = self.parts(q)
        self.arrive(2, q)
        cl, cr = block(self.yl), block(self.yr)
        self.go(3, q, (self.full.at[a, cr], self.full.at[a, cr]), (self.full.at[b, cl], self.full.at[b, cl]))

    def stage4(self, q):
        self.arrive(3, q)

    def drain(self):
        for copies in self.flying.values():
            for copy in copies:
                copy.wait_send()
        self.flying = {}


class Spread(Ring):
    def __init__(self, full, send_sem, recv_sem):
        super().__init__(None, None, None, full, send_sem, recv_sem)

    def stage0(self, q):
        rows, a, b = self.parts(q)
        own = self.full.at[:, rows, block(self.y, 128)]
        self.go(0, q, (own, own), (own, own))

    def stage1(self, q):
        rows, a, b = self.parts(q)
        self.arrive(0, q)
        from_right, from_left = self.full.at[:, a, block(self.yr, 128)], self.full.at[:, b, block(self.yl, 128)]
        self.go(1, q, (from_right, from_right), (from_left, from_left))

    def stage2(self, q):
        self.arrive(1, q)


def ring_scratch():
    return [
        pltpu.VMEM((ROWS, D), BF),
        pltpu.VMEM((2, ROWS, 256), BF),
        pltpu.VMEM((2, ROWS, 256), BF),
        pltpu.VMEM((ROWS, D), BF),
        pltpu.SemaphoreType.DMA((4, NQ, 2)),
        pltpu.SemaphoreType.DMA((4, NQ, 2)),
    ]


def standardize(x):
    average = jnp.mean(x, axis=1, keepdims=True)
    centered = x - average
    variance = jnp.mean(centered * centered, axis=1, keepdims=True)
    rstd = lax.rsqrt(variance + EPSILON)
    return centered * rstd, rstd


def half_masks():
    lane = lax.broadcasted_iota(jnp.int32, (1, 128), 1)
    first = (lane < 64).astype(F32)
    return first.astype(BF), (1.0 - first).astype(BF)


def key_rows():
    return lax.broadcasted_iota(jnp.int32, (KEYS, 128), 0) < SEQ


def flip(rows):
    return jnp.transpose(rows.astype(F32), (1, 0))


def pair(first, second):
    top = lax.broadcasted_iota(jnp.int32, first.shape, 0) < 64
    return jnp.where(top, first, second)


def torus():
    d, t = lax.axis_index("dp"), lax.axis_index("tensor")
    x, z = d // 4, lax.rem(d, 4)
    return d, t, x, z, lax.rem(t, 2)


def dp_device(x, z):
    return {"dp": lax.rem(x + 4, 4) * 4 + lax.rem(z + 4, 4)}


class Exchange:
    def __init__(self, send_sem, recv_sem):
        self.send_sem, self.recv_sem, self.count, self.started = send_sem, recv_sem, 0, []

    def go(self, src, dst, device):
        copy = pltpu.make_async_remote_copy(
            src_ref=src,
            dst_ref=dst,
            send_sem=self.send_sem.at[self.count],
            recv_sem=self.recv_sem.at[self.count],
            device_id=device,
            device_id_type=pl.DeviceIdType.MESH,
        )
        copy.start()
        self.count += 1
        self.started.append(copy)
        return copy

    def drain(self):
        for copy in self.started:
            copy.wait_send()


def sides(half, x, z):
    along_x = [dp_device(x + j, z) for j in (1, 2, 3)]
    along_z = [dp_device(x, z + j) for j in (1, 2, 3)]
    return (x, z, along_x, along_z) if half == 0 else (z, x, along_z, along_x)


def place(half, a, b):
    return (a, b) if half == 0 else (b, a)


def wrap(k):
    return lax.rem(k + 4, 4)


ALL = pl.ds(0, 4)

class Background:
    def __init__(self):
        self.steps = []

    def add(self, *steps):
        self.steps.extend(steps)

    def run(self, count=1):
        for _ in range(min(count, len(self.steps))):
            self.steps.pop(0)()

    def until(self, step):
        while step in self.steps:
            self.steps.pop(0)()


def pipeline(stages, background, fillers=None):
    fillers = fillers or {}
    for step in range(NQ + len(stages) - 1):
        for k, stage in enumerate(stages):
            if 0 <= step - k < NQ:
                stage(step - k)
            if k == 0:
                for filler in fillers.get(step, ()):
                    filler()
                background.run()


class Gather:
    def __init__(self, ex, w):
        self.ex, self.w = ex, w
        d, t, self.x, self.z, self.c = torus()
        self.partner = {"tensor": t + 1 - 2 * self.c}
        self.state = [None, None]
        self.hand = []

    def at(self, h, a, b, quarters):
        return self.w.at[(self.c, *place(h, a, b), quarters)]

    def push(self, ref, device):
        return self.ex.go(ref, ref, device)

    def one(self):
        for h in range(2):
            a, b, along_a, along_b = sides(h, self.x, self.z)
            own = self.at(h, a, b, pl.ds(2 * h, 2))
            self.state[h] = [self.push(own, device) for device in along_a]

    def two(self):
        for h in range(2):
            a, b, along_a, along_b = sides(h, self.x, self.z)
            for copy in self.state[h]:
                copy.wait_recv()
            row = self.at(h, ALL, b, pl.ds(2 * h, 2))
            self.state[h] = [self.push(row, device) for device in along_b]
            self.hand.append(self.push(row, self.partner))

    def three(self):
        for j in (0, 2, 1):
            for h in range(2):
                a, b, along_a, along_b = sides(h, self.x, self.z)
                self.state[h][j].wait_recv()
                self.hand.append(self.push(self.at(h, ALL, wrap(b - 1 - j), pl.ds(2 * h, 2)), self.partner))

    def four(self):
        for copy in self.hand:
            copy.wait_recv()


class Scatter:
    def __init__(self, ex, r, store, got, second, first):
        self.ex, self.r, self.store, self.got = ex, r, store, got
        self.second, self.first = second, first
        d, t, self.x, self.z, self.c = torus()
        self.partner = {"tensor": t + 1 - 2 * self.c}
        self.state = [None, None]
        self.sent = []

    def at(self, h, a, b, quarters):
        return self.r.at[(self.c, *place(h, a, b), quarters)]

    def push(self, src, dst, device):
        copy = self.ex.go(src, dst, device)
        self.sent.append(copy)
        return copy

    def landed(self, h):
        for copy in self.state[h]:
            copy.wait_recv()

    def zero(self):
        for h in range(2):
            both = pl.ds(2 * h, 2)
            self.state[h] = [
                self.push(self.r.at[1 - self.c, :, :, both], self.got.at[:, :, both], self.partner)
            ]

    def one(self):
        for h in range(2):
            a, b, along_a, along_b = sides(h, self.x, self.z)
            both = pl.ds(2 * h, 2)
            self.landed(h)

            def merge(i, _):
                ref = self.r.at[self.c, i, :, both]
                ref[...] = add(ref, self.got.at[i, :, both]).astype(BF)
                return 0

            lax.fori_loop(0, 4, merge, 0)
            self.state[h] = [
                self.push(self.at(h, ALL, wrap(b + 1 + j), both), self.second.at[h, j], along_b[j]) for j in range(3)
            ]

    def two(self):
        for h in range(2):
            a, b, along_a, along_b = sides(h, self.x, self.z)
            both = pl.ds(2 * h, 2)
            self.landed(h)
            for i in range(4):
                ref = self.at(h, i, b, both)
                ref[...] = add(ref, *(self.second.at[h, j, i] for j in range(3))).astype(BF)
            self.state[h] = [
                self.push(self.at(h, wrap(a + 1 + j), b, both), self.first.at[h, j], along_a[j]) for j in range(3)
            ]

    def three(self):
        for h in range(2):
            a, b, along_a, along_b = sides(h, self.x, self.z)
            both = pl.ds(2 * h, 2)
            self.landed(h)
            total = add(self.at(h, a, b, both), *(self.first.at[h, j] for j in range(3)))
            self.store(h, total.reshape(32, total.shape[2]))
        for copy in self.sent:
            copy.wait_send()


def add(*terms):
    total = terms[0][...].astype(F32)
    for term in terms[1:]:
        total = total + term[...].astype(F32)
    return total


def scatter_scratch(width):
    return [
        pltpu.VMEM((2, 4, 4, 4, 16, width), BF),
        pltpu.VMEM((4, 4, 4, 16, width), BF),
        pltpu.VMEM((2, 3, 4, 2, 16, width), BF),
        pltpu.VMEM((2, 3, 2, 16, width), BF),
    ]


def mat(ref, c, lo, hi):
    return ref[c, :, :, :, :, lo:hi].reshape(D, hi - lo)


def put(ref, c, lo, hi, value):
    ref[c, :, :, :, :, lo:hi] = value.astype(BF).reshape(4, 4, 4, 16, hi - lo)


class Local:
    def __init__(self, sem):
        self.sem, self.count = sem, 0

    def go(self, src, dst):
        copy = pltpu.make_async_copy(src, dst, self.sem.at[self.count])
        copy.start()
        self.count += 1
        return copy


def column_sum(value):
    return jnp.sum(value.astype(F32), axis=0, keepdims=True)


def low_lanes(shape):
    return lax.broadcasted_iota(jnp.int32, shape, 1) < 64


def unpack_vectors(wa, vec):
    vec[0:8, :] = flip(mat(wa, 0, 384, ATT))[0:8]
    for c in range(2):
        heads = jnp.sum(mat(wa, c, 384, ATT).reshape(16, 64, 128)[:, 0:16].astype(F32), axis=0)
        rolled = pltpu.roll(heads, 64, 1)

        def both(k):
            return jnp.where(low_lanes((1, 128)), rolled[k : k + 1], heads[k + 1 : k + 2])

        vec[6:7, c * 128 : c * 128 + 128] = both(0)
        vec[6:7, 256 + c * 128 : 384 + c * 128] = both(2)
        for m in range(4):
            vec[7:8, c * 512 + 128 * m : c * 512 + 128 * m + 128] = both(4 + 2 * m)


def pack_vectors(vg, rv, lane):
    padded = jnp.concatenate([vg[...], jnp.zeros((120, D), F32)], axis=0)
    kind = lax.broadcasted_iota(jnp.int32, (128, D), 0)
    columns = flip(jnp.where(kind < 6, padded, 0.0)).reshape(16, 64, 128)
    row = lax.broadcasted_iota(jnp.int32, (64, 128), 0)
    for c in range(2):
        pieces = [vg[6:7, c * 128 : c * 128 + 128], vg[6:7, 256 + c * 128 : 384 + c * 128]]
        pieces += [vg[7:8, c * 512 + 128 * m : c * 512 + 128 * m + 128] for m in range(4)]
        heads = jnp.zeros((64, 128), F32)
        for k, piece in enumerate(pieces):
            rolled = pltpu.roll(jnp.broadcast_to(piece, (8, 128)), 64, 1)[0:1]
            heads = jnp.where(row == 2 * k, rolled, heads)
            heads = jnp.where(row == 2 * k + 1, piece, heads)
        heads = jnp.where(low_lanes((64, 128)), 0.0, heads)
        put(rv, c, lane, lane + 128, (columns + heads[None]).reshape(D, 128))


def forward_kernel(
    img_ref, cot_ref, qw_ref, kw_ref, vw_ref, uw_ref, ow_ref, dw_ref,
    *refs,
):
    refs = list(refs)
    features = [refs.pop(0) for _ in range(6)]
    heads = [refs.pop(0) for _ in range(3)]
    saved = [[refs.pop(0) for _ in range(9)] for _ in range(2)]
    wa_out = [refs.pop(0) for _ in range(2)]
    wm_out = [refs.pop(0) for _ in range(2)]
    wo_out = [refs.pop(0) for _ in range(2)]
    vec_ref, xc_ref, act_ref = [refs.pop(0) for _ in range(3)]
    kept = [[refs.pop(0) for _ in range(8)] for _ in range(2)]
    wa = [refs.pop(0) for _ in range(2)]
    wm = [refs.pop(0) for _ in range(2)]
    wo = [refs.pop(0) for _ in range(2)]
    heads_full = [refs.pop(0) for _ in range(2)]
    xg_ref, vt_ref, give_ref, local_sem, send_sem, recv_sem = [refs.pop(0) for _ in range(6)]
    spread_sems = refs[6:8]
    square_ref, strip_ref = refs[8:10]
    two = Ring(*refs[:6])
    d, t, x, z, c_here = torus()
    y = t // 2
    partner = {"tensor": t + 1 - 2 * c_here}
    others = [{"tensor": lax.rem(t + j, 8)} for j in range(1, 8)]
    _, _, along_x, along_z = sides(0, x, z)
    entered = greet(along_x + along_z + others)
    local, ex, background = Local(local_sem), Exchange(send_sem, recv_sem), Background()
    groups = [Gather(ex, ref) for ref in (wa[0], wm[0], wa[1], wm[1])]
    m0, a1, m1 = groups[1:]
    o0, o1 = [Gather(ex, ref) for ref in wo]
    pieces = []
    own = []
    for layer in range(2):
        slot = wa[layer].at[c_here, x, z]
        own.append(
            [local.go(src.at[layer], slot.at[:, :, pl.ds(128 * k, 128)]) for k, src in enumerate((qw_ref, kw_ref, vw_ref))]
        )
        own.append([local.go(uw_ref.at[layer], wm[layer].at[c_here, x, z, :, :, pl.ds(0, 512)])])
    mine = local.go(img_ref.at[c_here], xg_ref.at[t])
    theirs = local.go(cot_ref.at[c_here], xc_ref.at[t])

    def build_att(layer):
        for k, ref in enumerate(features):
            square_ref[k : k + 1, 0:64] = ref[...].astype(F32)[layer : layer + 1]
        columns = flip(square_ref[...])[0:64]
        first = 0
        for ref in heads:
            rows = ref[layer].astype(F32)
            strip_ref[first : first + rows.shape[0], 0:4] = rows
            first += rows.shape[0]
        strip = pltpu.roll(strip_ref[...], 64 + 4 * d, 1)
        vectors = columns + jnp.concatenate([strip, jnp.zeros((48, 128), F32)], axis=0)
        wa[layer][c_here, x, z, :, :, 384:ATT] = vectors.astype(BF).reshape(4, 16, 128)

    def build_out(layer):
        wo[layer][c_here, x, z, :, :, block(y, 128)] = ow_ref[layer].reshape(4, 16, 128)
        piece = wo[layer].at[c_here, x, z, :, :, block(y, 128)]
        pieces.append([ex.go(piece, piece, others[j]) for j in (1, 3, 5)])

    def start_out(layer):
        def run():
            for copy in pieces[layer]:
                copy.wait_recv()
            (o0, o1)[layer].one()

        return run

    def build_mlp(layer):
        wm[layer][c_here, x, z, :, :, 512:MLP] = dw_ref[layer].reshape(4, 16, 512)

    def start(k):
        def run():
            for copy in own[k]:
                copy.wait()
            groups[k].one()

        return run

    def exchange(src, dst):
        copies = []
        for j in range(1, 8):
            target = lax.rem(t + j, 8)
            copies.append(ex.go(src.at[lax.rem(target, 2)], dst.at[t], others[j - 1]))
        return copies

    square_ref[...] = jnp.zeros((128, 128), F32)
    strip_ref[...] = jnp.zeros((16, 128), F32)
    build_att(0)
    entered()
    start(0)()
    build_out(0)
    images = exchange(img_ref, xg_ref)
    build_mlp(0)
    build_out(1)
    build_att(1)
    build_mlp(1)
    groups[0].two()
    start_out(0)()
    start(1)()
    mine.wait()
    for copy in images:
        copy.wait_recv()
    cotangents = exchange(cot_ref, xc_ref)
    for r0, nr in CHUNKS:
        rows = pl.ds(r0, nr)
        for j in range(8):
            kept[0][0][rows, 128 * j : 128 * j + 128] = xg_ref[j, rows, :].astype(F32)
    groups[0].three()
    o0.two()
    m0.two()
    groups[0].four()
    masks = half_masks()
    valid = key_rows()

    def rest():
        pass

    background.add(o0.three, start(2), m0.three, o0.four, m0.four, a1.two, start_out(1), a1.three, a1.four, start(3))
    background.add(o1.two, rest, o1.three, m1.two, o1.four, m1.three, m1.four)
    for layer in range(2):
        kept[layer][2][:, ROWS:KEYS, :] = jnp.zeros((2, KEYS - ROWS, 384), BF)

    def project(layer, q):
        r0, nr = CHUNKS[q]
        rows = pl.ds(r0, nr)
        x_ref, n1_ref, qkv_ref = kept[layer][:3]
        vec = vec_ref.at[layer]
        xhat, _ = standardize(x_ref[rows, :])
        n1 = (xhat * vec[0:1, :] + vec[1:2, :]).astype(BF)
        n1_ref[rows, :] = n1
        for c in range(2):
            out = dot(n1, mat(wa[layer], c, 0, 384))
            qkv_ref[c, rows, 0:128] = (out[:, 0:128] + vec[6:7, c * 128 : c * 128 + 128]).astype(BF)
            qkv_ref[c, rows, 128:256] = out[:, 128:256].astype(BF)
            qkv_ref[c, rows, 256:384] = (out[:, 256:384] + vec[6:7, 256 + c * 128 : 384 + c * 128]).astype(BF)

    unpack_vectors(wa[0], vec_ref.at[0])
    for q in range(NQ):
        project(0, q)

    def layer_forward(layer):
        x_ref, n1_ref, qkv_ref, lse_ref, mid_ref, n2_ref, slope_ref, a_ref = kept[layer]
        one = Spread(heads_full[layer], *spread_sems)
        x_out, n1_out, qkv_out, lse_out, o_out, mid_out, n2_out, slope_out, a_out = saved[layer]
        vec = vec_ref.at[layer]
        waits = [
            local.go(src, dst)
            for src, dst in ((x_ref, x_out), (n1_ref, n1_out), (wa[layer], wa_out[layer]), (qkv_ref, qkv_out))
        ]
        for c in range(2):
            vt_ref[c] = flip(qkv_ref[c, :, 256:384]).astype(BF)

        def attend(q):
            r0, nr = CHUNKS[q]
            for c in range(2):
                queries, keys = qkv_ref[c, r0 : r0 + 128, 0:128], qkv_ref[c, :, 128:256]
                halves = []
                for h in range(2):
                    s = dot(keys, queries * masks[h], TN) * SCALE
                    s = jnp.where(valid, s, -1e30)
                    top = jnp.max(s, axis=0, keepdims=True)
                    e = jnp.exp(s - top)
                    norm = jnp.sum(e, axis=0, keepdims=True)
                    lse_ref[2 * c + h : 2 * c + h + 1, r0 : r0 + 128] = top + jnp.log(norm)
                    p = (e * (1.0 / norm)).astype(BF)
                    halves.append(dot(vt_ref[c], p))
                one.full[c, r0 : r0 + nr, block(y, 128)] = flip(pair(*halves))[0:nr].astype(BF)
            one.stage0(q)
            if q == NQ - 1:
                waits.extend([local.go(lse_ref, lse_out), local.go(one.full.at[:, :, block(y, 128)], o_out)])

        def feed(q):
            r0, nr = CHUNKS[q]
            rows = pl.ds(r0, nr)
            if q == 0:
                background.until(groups[2 * layer + 1].four)
                waits.append(local.go(wm[layer], wm_out[layer]))
                waits.append(local.go(wo[layer].at[:, :, :, :, :, block(y, 128)], wo_out[layer]))
            one.stage2(q)
            mid = x_ref[rows, :] + vec[2:3, :]
            for c in range(2):
                mid = mid + dot(one.full[c, rows, :], mat(wo[layer], c, 0, OUT), TN)
            mid_ref[rows, :] = mid
            xhat, _ = standardize(mid)
            n2 = (xhat * vec[3:4, :] + vec[4:5, :]).astype(BF)
            n2_ref[rows, :] = n2
            total = None
            for c in range(2):
                u = dot(n2, mat(wm[layer], c, 0, 512)) + vec[7:8, c * 512 : c * 512 + 512]
                phi = 0.5 * (1.0 + lax.erf(u * (1.0 / math.sqrt(2.0))))
                slope = phi + u * (jnp.exp(-0.5 * u * u) * (1.0 / math.sqrt(2.0 * math.pi)))
                slope_ref[c, rows, :] = slope.astype(BF)
                a = (u * phi).astype(BF)
                a_ref[c, rows, :] = a
                part = dot(a, mat(wm[layer], c, 512, MLP), TN)
                total = part if total is None else total + part
            two.send[rows, :] = total.astype(BF)
            two.stage0(q)
            if q == NQ - 1:
                waits.extend(
                    local.go(src, dst)
                    for src, dst in ((mid_ref, mid_out), (n2_ref, n2_out), (slope_ref, slope_out), (a_ref, a_out))
                )

        def finish(q):
            r0, nr = CHUNKS[q]
            rows = pl.ds(r0, nr)
            two.stage4(q)
            kept[1][0][rows, :] = mid_ref[rows, :] + two.full[rows, :].astype(F32) + vec[5:6, :]
            if q == 0:
                background.until(a1.four)
                unpack_vectors(wa[1], vec_ref.at[1])
            project(1, q)

        swaps = []

        def last(q):
            r0, nr = CHUNKS[q]
            rows = pl.ds(r0, nr)
            two.arrive(1, q)
            c = block(y)
            total = two.send[rows, c].astype(F32) + two.far[0, rows, :].astype(F32) + two.far[1, rows, :].astype(F32)
            total = total + mid_ref[rows, c] + vec[5:6, c]
            left, right = total[:, 0:128].astype(BF), total[:, 128:256].astype(BF)
            act_ref[c_here, rows, :] = jnp.where(c_here == 0, left, right)
            give_ref[rows, :] = jnp.where(c_here == 0, right, left)
            swaps.append(ex.go(give_ref.at[rows], act_ref.at[c_here, rows], partner))

        stages = (attend, one.stage1, feed, two.stage1)
        stages += (two.stage2, two.stage3, finish) if layer == 0 else (last,)
        pipeline(stages, background)
        one.drain()
        two.drain()
        return waits, swaps

    waits0, _ = layer_forward(0)
    waits1, swaps = layer_forward(1)
    theirs.wait()
    for copy in cotangents + swaps:
        copy.wait_recv()
    for copy in waits0 + waits1:
        copy.wait()
    ex.drain()


def backward_kernel(
    cot_ref, vec_ref, *refs,
):
    refs = list(refs)
    saved = [[refs.pop(0) for _ in range(9)] for _ in range(2)]
    wa_in = [refs.pop(0) for _ in range(2)]
    wm_in = [refs.pop(0) for _ in range(2)]
    wo_in = [refs.pop(0) for _ in range(2)]
    gin_ref, grads_ref, small_ref = [refs.pop(0) for _ in range(3)]
    x_ref, n1_ref, qkv_ref, lse_ref, o_ref, mid_ref, n2_ref, slope_ref, a_ref = [refs.pop(0) for _ in range(9)]
    wa, wm = refs.pop(0), refs.pop(0)
    xg_ref, g_ref, gm_ref, go_ref, hid_ref, dout_ref, kt_ref, dqkv_ref, dk_ref, dv_ref, gmid_ref, vg_ref, give_ref = [
        refs.pop(0) for _ in range(13)
    ]
    local_sem, send_sem, recv_sem = [refs.pop(0) for _ in range(3)]
    mlp, att, small = [[refs.pop(0) for _ in range(4)] for _ in range(3)]
    one, two = Ring(*refs[:6]), Ring(*refs[6:12])
    d, t, x, z, c_here = torus()
    y = t // 2
    partner = {"tensor": t + 1 - 2 * c_here}
    _, _, along_x, along_z = sides(0, x, z)
    entered = greet(along_x + along_z + [one.left, one.right, partner])
    local, ex, background = Local(local_sem), Exchange(send_sem, recv_sem), Background()

    def load_mlp(layer):
        _, _, _, _, _, mid, n2, slope, a = saved[layer]
        pairs = ((wm_in[layer], wm), (slope, slope_ref), (a, a_ref), (mid, mid_ref), (n2, n2_ref))
        return [local.go(src, dst) for src, dst in pairs]

    def load_att(layer):
        stream, n1, qkv, lse, o = saved[layer][:5]
        low, high = pl.ds(0, 384), pl.ds(384, 128)
        pairs = (
            (wa_in[layer].at[:, :, :, :, :, low], wa.at[:, :, :, :, :, low]),
            (wo_in[layer], wa.at[:, :, :, :, :, high]),
        )
        pairs += ((qkv, qkv_ref), (lse, lse_ref), (o, o_ref), (n1, n1_ref))
        return [local.go(src, dst) for src, dst in pairs]

    cot = local.go(cot_ref, xg_ref)
    loads = {1: load_mlp(1)}
    att_loads = {1: load_att(1)}
    x_loads = {1: local.go(saved[1][0], x_ref)}
    masks = half_masks()
    valid = key_rows()
    dout_ref[:, ROWS:KEYS, :] = jnp.zeros((2, KEYS - ROWS, 128), BF)
    cot.wait()
    for r0, nr in CHUNKS:
        rows = pl.ds(r0, nr)
        for j in range(8):
            g_ref[rows, 128 * j : 128 * j + 128] = xg_ref[j, rows, :].astype(F32)
    entered()
    swaps = []

    vg_ref[...] = jnp.zeros((2, 8, D), F32)

    def layer_steps(layer):
        vec, vg = vec_ref.at[layer], vg_ref.at[layer]

        def store_mlp(h, value):
            rows = slice(32 * h, 32 * h + 32)
            grads_ref[layer, rows, 512:1536] = value

        def store_att(h, value):
            rows = slice(32 * h, 32 * h + 32)
            grads_ref[layer, rows, 0:512] = value

        mlp_scatter = Scatter(ex, mlp[0], store_mlp, *mlp[1:])
        att_scatter = Scatter(ex, att[0], store_att, *att[1:])

        def add_vector(row, value, lane=0):
            width = value.shape[1]
            vg[row : row + 1, lane : lane + width] = vg[row : row + 1, lane : lane + width] + value

        def hidden(q):
            r0, nr = CHUNKS[q]
            rows = pl.ds(r0, nr)
            if q == 0:
                for copy in loads[layer]:
                    copy.wait()
            gm = g_ref[rows, :].astype(BF)
            gm_ref[rows, :] = gm
            add_vector(5, column_sum(gm))
            total = None
            for c in range(2):
                da = dot(gm, mat(wm, c, 512, MLP))
                du = (da * slope_ref[c, rows, :].astype(F32)).astype(BF)
                hid_ref[c, rows, :] = du
                add_vector(7, column_sum(du), c * 512)
                part = dot(du, mat(wm, c, 0, 512), TN)
                total = part if total is None else total + part
            one.send[rows, :] = total.astype(BF)
            one.stage0(q)

        def norm_back(ring, q, stream, grad, gain_row, shift_row):
            r0, nr = CHUNKS[q]
            rows = pl.ds(r0, nr)
            ring.stage4(q)
            dn = ring.full[rows, :].astype(F32)
            xhat, rstd = standardize(stream[rows, :])
            add_vector(gain_row, column_sum(dn * xhat))
            add_vector(shift_row, column_sum(dn))
            e = dn * vec[gain_row : gain_row + 1, :]
            first = jnp.mean(e, axis=1, keepdims=True)
            second = jnp.mean(e * xhat, axis=1, keepdims=True)
            return grad[rows, :] + rstd * (e - first - xhat * second)

        def attend(q):
            r0, nr = CHUNKS[q]
            rows = pl.ds(r0, nr)
            if q == 0:
                for copy in att_loads[layer]:
                    copy.wait()
                for c in range(2):
                    kt_ref[c] = flip(qkv_ref[c, :, 128:256]).astype(BF)
                dk_ref[...] = jnp.zeros(dk_ref.shape, F32)
                dv_ref[...] = jnp.zeros(dv_ref.shape, F32)
            mid_grad = norm_back(one, q, mid_ref, g_ref, 3, 4)
            gmid_ref[rows, :] = mid_grad
            go = mid_grad.astype(BF)
            go_ref[rows, :] = go
            add_vector(2, column_sum(go))
            for c in range(2):
                dout_ref[c, rows, :] = dot(go, mat(wa, c, 384, 512)).astype(BF)
                queries = qkv_ref[c, r0 : r0 + 128, 0:128]
                keys, values = qkv_ref[c, :, 128:256], qkv_ref[c, :, 256:384]
                dout = dout_ref[c, r0 : r0 + 128, :]
                halves = []
                for h in range(2):
                    qh, doh = queries * masks[h], dout * masks[h]
                    s = dot(keys, qh, TN) * SCALE
                    p = jnp.where(valid, jnp.exp(s - lse_ref[2 * c + h : 2 * c + h + 1, r0 : r0 + 128]), 0.0)
                    dp = dot(values, doh, TN)
                    delta = jnp.sum(dp * p, axis=0, keepdims=True)
                    ds = (p * (dp - delta)).astype(BF)
                    dv_ref[c] = dv_ref[c] + dot(p.astype(BF), doh)
                    dk_ref[c] = dk_ref[c] + dot(ds, qh)
                    halves.append(dot(kt_ref[c], ds))
                dq = (flip(pair(*halves)) * SCALE)[0:nr].astype(BF)
                dqkv_ref[c, rows, 0:128] = dq

        def down_grad(c):
            def run():
                put(mlp[0], c, 512, MLP, dot(gm_ref[...], a_ref[c], NT))

            return run

        def up_grad(c):
            def run():
                put(mlp[0], c, 0, 512, dot(n2_ref[...], hid_ref[c], NT))

            return run

        def out_grad():
            for c in range(2):
                put(att[0], c, 384, 512, dot(go_ref[...], o_ref[c], NT))

        def qkv_grad(c):
            def run():
                put(att[0], c, 0, 384, dot(n1_ref[...], dqkv_ref[c], NT))

            return run

        def settle():
            for c in range(2):
                dqkv_ref[c, :, 128:256] = (dk_ref[c, 0:ROWS] * SCALE).astype(BF)
                dqkv_ref[c, :, 256:384] = dv_ref[c, 0:ROWS].astype(BF)

        def project(q):
            r0, nr = CHUNKS[q]
            rows = pl.ds(r0, nr)
            total = None
            for c in range(2):
                grads = dqkv_ref[c, rows, :]
                add_vector(6, column_sum(grads[:, 0:128]), c * 128)
                add_vector(6, column_sum(grads[:, 256:384]), 256 + c * 128)
                part = dot(grads, mat(wa, c, 0, 384), TN)
                total = part if total is None else total + part
            two.send[rows, :] = total.astype(BF)
            two.stage0(q)

        def finish(q):
            r0, nr = CHUNKS[q]
            rows = pl.ds(r0, nr)
            if q == 0:
                x_loads[layer].wait()
            g_ref[rows, :] = norm_back(two, q, x_ref, gmid_ref, 0, 1)
            if layer == 0:
                left, right = g_ref[rows, block(2 * y, 128)], g_ref[rows, block(2 * y + 1, 128)]
                gin_ref[c_here, rows, :] = jnp.where(c_here == 0, left, right)
                give_ref[rows, :] = jnp.where(c_here == 0, right, left)
                swaps.append(ex.go(give_ref.at[rows], gin_ref.at[c_here, rows], partner))

        def pack():
            pack_vectors(vg, small[0], 128 * layer)

        return (
            hidden, attend, project, finish, settle, pack, mlp_scatter, att_scatter,
            (down_grad(0), down_grad(1)), (up_grad(0), up_grad(1)), (out_grad, qkv_grad(0), qkv_grad(1)),
        )

    def rest():
        pass

    hidden1, attend1, project1, finish1, settle1, pack1, m1, a1, down1, up1, grads1 = layer_steps(1)
    hidden0, attend0, project0, finish0, settle0, pack0, m0, a0, down0, up0, grads0 = layer_steps(0)
    pipeline(
        (hidden1, one.stage1, one.stage2, one.stage3, attend1),
        background,
        {5: (up1[0], down1[0]), 6: (up1[1], down1[1], m1.zero)},
    )
    one.drain()
    loads[0] = load_mlp(0)
    settle1()

    def turn(q):
        finish1(q)
        hidden0(q)

    def reload():
        att_loads[0] = load_att(0)

    def reload_x():
        x_loads[0] = local.go(saved[0][0], x_ref)

    def begin(steps):
        return lambda: background.add(*steps)

    background.add(m1.one, rest, m1.two, rest, a1.zero, m1.three, a1.one, rest, a1.two, a1.three)
    pipeline(
        (project1, two.stage1, two.stage2, two.stage3, turn, one.stage1, one.stage2, one.stage3, attend0),
        background,
        {
            1: grads1[:1],
            2: grads1[1:2],
            3: grads1[2:],
            5: (reload,),
            9: (reload_x, lambda: background.until(a1.three), *up0, *down0, m0.zero, begin((rest, m0.one, rest, rest))),
        },
    )
    one.drain()
    two.drain()
    pack1()
    settle0()
    background.add(m0.two, a0.zero, m0.three, a0.one, rest, a0.two, rest, a0.three)
    pipeline(
        (project0, two.stage1, two.stage2, two.stage3, finish0),
        background,
        {0: grads0[:2], 1: grads0[2:]},
    )
    pack0()

    def store_small(h, value):
        small_ref[32 * h : 32 * h + 32, :] = value

    last = Scatter(ex, small[0], store_small, *small[1:])
    last.zero()
    background.run(100)
    last.one()
    last.two()
    last.three()
    two.drain()
    for copy in swaps:
        copy.wait_recv()
        copy.wait_send()


VM = pl.BlockSpec(memory_space=pltpu.VMEM)
HBM = pl.BlockSpec(memory_space=pl.ANY)


def params(collective_id, megabytes):
    return pltpu.CompilerParams(
        collective_id=collective_id, has_side_effects=True, vmem_limit_bytes=megabytes * 1024 * 1024
    )


def shape(dims, dtype):
    return jax.ShapeDtypeStruct(dims, dtype)


LAYER = (
    ((ROWS, D), F32),
    ((ROWS, D), BF),
    ((2, KEYS, 384), BF),
    ((8, KEYS), F32),
    ((2, ROWS, 128), BF),
    ((ROWS, D), F32),
    ((ROWS, D), BF),
    ((2, ROWS, 512), BF),
    ((2, ROWS, 512), BF),
)
WA = ((2, 4, 4, 4, 16, ATT), BF)
WM = ((2, 4, 4, 4, 16, MLP), BF)
WO = ((2, 4, 4, 4, 16, OUT), BF)
WO_OWN = ((2, 4, 4, 4, 16, 128), BF)
HEADS = ((2, ROWS, OUT), BF)
KEPT = LAYER[:4] + LAYER[5:]
DMA = pltpu.SemaphoreType.DMA


def vmem(*kinds):
    return [pltpu.VMEM(*kind) for kind in kinds]


def forward(*operands):
    outs = [shape(*kind) for kind in LAYER * 2 + (WA, WA, WM, WM, WO_OWN, WO_OWN)]
    outs += [shape((2, 8, D), F32), shape((8, ROWS, 128), BF), shape((2, ROWS, 128), BF)]
    return pl.pallas_call(
        forward_kernel,
        out_shape=tuple(outs),
        in_specs=[HBM] * 6 + [VM] * 11,
        out_specs=tuple([HBM] * 24 + [VM, HBM, VM]),
        scratch_shapes=vmem(
            *KEPT, *KEPT, WA, WA, WM, WM, WO, WO, HEADS, HEADS,
            ((8, ROWS, 128), BF), ((2, 128, KEYS), BF), ((ROWS, 128), BF),
        )
        + [DMA((40,)), DMA((160,)), DMA((160,))]
        + ring_scratch()
        + [DMA((2, NQ, 2)), DMA((2, NQ, 2))]
        + vmem(((128, 128), F32), ((16, 128), F32)),
        compiler_params=params(0, 58),
        name="forward",
    )(*operands)


def backward(*operands):
    return pl.pallas_call(
        backward_kernel,
        out_shape=(
            shape((2, ROWS, 128), F32),
            shape((2, 64, 1536), F32),
            shape((64, 256), F32),
        ),
        in_specs=[HBM, VM] + [HBM] * 24,
        out_specs=(VM,) * 3,
        scratch_shapes=vmem(
            *LAYER,
            WA,
            WM,
            ((8, ROWS, 128), BF),
            ((ROWS, D), F32),
            ((ROWS, D), BF),
            ((ROWS, D), BF),
            ((2, ROWS, 512), BF),
            ((2, KEYS, 128), BF),
            ((2, 128, KEYS), BF),
            ((2, ROWS, 384), BF),
            ((2, KEYS, 128), F32),
            ((2, KEYS, 128), F32),
            ((ROWS, D), F32),
            ((2, 8, D), F32),
            ((ROWS, 128), F32),
        )
        + [DMA((32,)), DMA((100,)), DMA((100,))]
        + scatter_scratch(MLP)
        + scatter_scratch(512)
        + scatter_scratch(256)
        + ring_scratch()
        + ring_scratch(),
        compiler_params=params(1, 60),
        name="backward",
    )(*operands)


def split_inputs(weights):
    ag, ash, qw, qb, kw, vw, vb, ow, ob, fg, fs, uw, ub, dw, db = weights
    split = (2, 4, 16)
    return (
        qw.reshape(*split, 128), kw.reshape(*split, 128), vw.reshape(*split, 128), uw.reshape(*split, 512),
        jnp.swapaxes(ow, 1, 2), jnp.swapaxes(dw, 1, 2), ag, ash, ob, fg, fs, db, qb, vb, ub,
    )


def unpack_grads(grads, small, d):
    qg, kg, vg, og = [grads[:, :, 128 * k : 128 * k + 128] for k in range(4)]
    ug, dg = grads[:, :, 512:1024], grads[:, :, 1024:1536]
    small = jnp.transpose(small.reshape(64, 2, 128), (1, 0, 2))
    columns = [small[:, :, k] for k in range(6)]
    mine = lax.dynamic_slice_in_dim(small[:, 0:12, 64:128], d * 4, 4, axis=2)
    return (
        columns[0], columns[1], qg, mine[:, 0:2], kg, vg, mine[:, 2:4], jnp.swapaxes(og, 1, 2), columns[2], columns[3],
        columns[4], ug, mine[:, 4:12], jnp.swapaxes(dg, 1, 2), columns[5],
    )


def local(images, cotangent, counts, *weights):
    d = lax.axis_index("dp")
    alive = (jnp.arange(2) < counts[0])[:, None, None]
    pad = ((0, 0), (0, ROWS - SEQ), (0, 0))
    images = jnp.pad(images, pad)
    cotangent = jnp.pad(jnp.where(alive, cotangent, jnp.zeros((), BF)), pad)
    *saved, vec, cot, act = forward(images, cotangent, *split_inputs(weights))
    gin, grads, small = backward(cot, vec, *saved)
    return (
        jnp.where(alive, act[:, :SEQ], jnp.zeros((), BF)),
        gin[:, :SEQ],
        *unpack_grads(grads, small, d),
    )


def solution(mesh):
    row = P(None, "dp")
    columns = P(None, "dp", "tensor")
    heads = P(None, "tensor", "dp")
    weights = (
        row, row, columns, heads, columns, columns, heads, heads, row, row, row, columns, heads, heads, row,
    )
    stream = P("dp", None, "tensor")
    return jax.shard_map(
        local,
        mesh=mesh,
        in_specs=(stream, stream, P("dp"), *weights),
        out_specs=(stream, stream, *weights),
        check_vma=False,
    )
```
